32 devices in a mesh: shot: 2 (over x), slab: 16 (over z, y, core).
Axes of the slice: x: 2, y: 2, z: 4, core: 2. Of those that a mesh axis runs over, the one named last changes fastest.
Arguments:
- wavefield: float32 [2, 2, 2048, 2048], P('shot', None, 'slab'), parts along dimension 0, may hold values from -5 to 5
- frequencies: float32 [2], P('shot'), parts along dimension 0, may hold values from 1 to 3
- velocity: float32 [1, 2048, 2048], P(None, 'slab'), may hold values from 1 to 2.25, as said below
- bracket: int32 [1, 2048, 2048], P(None, 'slab'), may hold values from 0 to 1
Outputs:
- propagated: float32 [2, 2, 2048, 2048], P('shot', None, 'slab'), parts along dimension 0
- image: float32 [2, 2048, 2048], P('shot', 'slab'), parts along dimension 0
The draws below stay inside these ranges and needn't reach their ends.
There are 2 independent parts, one for each index of `shot`. The reference program is written for one: setup_inputs(seed, part) draws one part's arguments, and reference() takes and returns one part's arrays. A program takes and returns all parts, laid end to end along the dimension named above; an argument that names none is the same for every part. Nothing has to cross between parts.
Inputs may be any that keep to these rules, and one draw needn't show every extreme that they name: velocity[d, y, x] lies between the reference speeds c_b and c_(b+1) with b = bracket[d, x, y].
All inputs are finite; a program needn't handle non-finite values.
Results may differ from the reference program's by a relative error of at most 0.0003.
Values sent between devices are 32-bit elements; how exact they have to be, the bound alone decides.
No kernel may reach another device: no remote copies, remote signals or barrier semaphores. Data moves between devices by JAX's collectives and lax.ppermute only.
A program may use at most 64 MiB of HBM per device.

```python
import math
import jax
import jax.numpy as jnp
from jax import lax

NX = 2048
NY = 2048
NF = 1
DEPTH = 1
NREF = 3


ref_speeds = (1.0, 1.5, 2.25)


def chosen_brackets(key):
    return jax.random.randint(jax.random.fold_in(key, 71), (DEPTH, NX, NY), 0, NREF - 1, dtype=jnp.int32)


def draw_bracket(key, part):
    return chosen_brackets(key)


def draw_velocity(key, part):
    chosen = chosen_brackets(key)
    speeds = jnp.array(ref_speeds, jnp.float32)
    fraction = jax.random.uniform(jax.random.fold_in(key, 72), (DEPTH, NX, NY), jnp.float32)
    lower_speed = speeds[chosen]
    upper_speed = speeds[chosen + 1]
    speed_grid = lower_speed + fraction * (upper_speed - lower_speed)
    return jnp.transpose(speed_grid, (0, 2, 1)).astype(jnp.float32)


def draw_wavefield(key, part):
    grid_shape = (NF, 2, NX, NY)
    values = jnp.clip(jax.random.normal(key, grid_shape, jnp.float32), -5.0, 5.0)
    return values.astype(jnp.float32)


def setup_inputs(seed: int = 0, part: int = 0) -> dict:
    arg_keys = jax.random.split(jax.random.key(seed), 5)
    own_keys = jax.random.split(jax.random.fold_in(arg_keys[4], part), 5)
    wavefield = draw_wavefield(jax.random.fold_in(jax.random.fold_in(arg_keys[4], part), 71), part)
    frequencies = jnp.clip(jnp.exp(jax.random.uniform(own_keys[1], (NF,), jnp.float32, math.log(1.0), math.log(3.0))), 1.0, 3.0)
    velocity = draw_velocity(jax.random.fold_in(arg_keys[4], 71), part)
    bracket = draw_bracket(jax.random.fold_in(arg_keys[4], 71), part)
    return dict(wavefield=wavefield, frequencies=frequencies, velocity=velocity, bracket=bracket)


ref_speeds = (1.0, 1.5, 2.25)
step_length = 1.0

def wavenumbers(extent):
    indices = jnp.arange(extent, dtype=jnp.int32)
    return jnp.minimum(indices, extent - indices).astype(jnp.float32) * (2.0 * math.pi / extent)

def weights(speed_grid, chosen):
    speeds = jnp.array(ref_speeds, jnp.float32)
    lower_speed = jnp.zeros_like(speed_grid)
    upper_speed = jnp.zeros_like(speed_grid)
    for ref_index in range(len(ref_speeds) - 1):
        lower_speed = lower_speed + jnp.where(chosen == ref_index, speeds[ref_index], 0.0)
        upper_speed = upper_speed + jnp.where(chosen == ref_index, speeds[ref_index + 1], 0.0)
    fraction = (speed_grid - lower_speed) / (upper_speed - lower_speed)
    residual_phase = 1.0 / speed_grid - ((1.0 - fraction) / lower_speed + fraction / upper_speed)
    coefficients = []
    for ref_index in range(len(ref_speeds)):
        coefficients.append(jnp.where(chosen == ref_index, 1.0 - fraction, 0.0) + jnp.where(chosen == ref_index - 1, fraction, 0.0))
    return (coefficients, residual_phase)

def reference(wavefield, frequencies, velocity, bracket):
    first_wave = wavenumbers(NX)
    second_wave = wavenumbers(NY)
    wave_square = first_wave[:, None] * first_wave[:, None] + second_wave[None, :] * second_wave[None, :]
    slowness = 1.0 / jnp.array(ref_speeds, jnp.float32)
    speed_rows = jnp.transpose(velocity, (0, 2, 1))
    fields = [lax.complex(wavefield[freq_index, 0], wavefield[freq_index, 1]) for freq_index in range(NF)]
    images = []
    for depth_index in range(DEPTH):
        coefficients, residual_phase = weights(speed_rows[depth_index], bracket[depth_index])
        updated = []
        for freq_index in range(NF):
            angular = frequencies[freq_index]
            spectrum = jnp.fft.fft2(fields[freq_index])
            blended = jnp.zeros_like(spectrum)
            for ref_index in range(NREF):
                wave_number = angular * slowness[ref_index]
                vertical = wave_number * wave_number - wave_square
                root_abs = jnp.sqrt(jnp.abs(vertical))
                real_part = jnp.where(vertical >= 0, jnp.cos(step_length * root_abs), jnp.exp(-step_length * root_abs))
                imag_part = jnp.where(vertical >= 0, jnp.sin(step_length * root_abs), 0.0)
                shifter = lax.complex(real_part, imag_part)
                blended = blended + coefficients[ref_index] * jnp.fft.ifft2(spectrum * shifter)
            angles = angular * step_length * residual_phase
            updated.append(blended * lax.complex(jnp.cos(angles), jnp.sin(angles)))
        fields = updated
        summed = jnp.real(fields[0])
        for freq_index in range(1, NF):
            summed = summed + jnp.real(fields[freq_index])
        images.append(summed)
    propagated = jnp.stack([jnp.stack([jnp.real(field_now), jnp.imag(field_now)]) for field_now in fields])
    return (propagated, jnp.stack(images))
```

```python
import math

import jax
import jax.numpy as jnp
import ml_dtypes
import numpy as np
from jax import lax
from jax.experimental import pallas as pl
from jax.experimental.pallas import tpu as pltpu
from jax.sharding import PartitionSpec as P

ref_speeds = (1.0, 1.5, 2.25)
step_length = 1.0
highest = lax.Precision.HIGHEST


def dft_table(height, breadth, modulus, direction):
    down_index = lax.iota(jnp.int32, height)[:, None]
    across_index = lax.iota(jnp.int32, breadth)[None, :]
    angles = (down_index * across_index % modulus).astype(jnp.float32) * (
        direction * 2.0 * math.pi / modulus
    )
    return (jnp.cos(angles), jnp.sin(angles))


def contract(pattern, left_pair, right_pair):

    def product(one_side, other_side):
        return jnp.einsum(pattern, one_side, other_side, precision=highest)

    return (
        product(left_pair[0], right_pair[0]) - product(left_pair[1], right_pair[1]),
        product(left_pair[0], right_pair[1]) + product(left_pair[1], right_pair[0]),
    )


def rotate(values, factor_pair):
    return (
        values[0] * factor_pair[0] - values[1] * factor_pair[1],
        values[0] * factor_pair[1] + values[1] * factor_pair[0],
    )


def forward_lines(fields):
    item_count, row_count, extent = fields[0].shape
    devices = lax.axis_size("slab")
    line_count = extent // devices
    reshaped = tuple(
        (part_now.reshape(item_count, row_count, line_count, devices) for part_now in fields)
    )
    section_one = contract(
        "nrab,ak->nrkb", reshaped, dft_table(line_count, line_count, line_count, -1.0)
    )
    twisted = rotate(
        section_one,
        tuple((turning[None, None] for turning in dft_table(line_count, devices, extent, -1.0))),
    )
    section_two = contract("nrkb,bq->nkqr", twisted, dft_table(devices, devices, devices, -1.0))
    return tuple(
        (part_now.reshape(item_count, line_count, devices * row_count) for part_now in section_two)
    )


def forward_rows(fields):
    item_count, line_count, extent = fields[0].shape
    devices = lax.axis_size("slab")
    row_count = extent // devices
    reshaped = tuple(
        (part_now.reshape(item_count, line_count, devices, row_count) for part_now in fields)
    )
    section_one = contract("ncab,ak->nckb", reshaped, dft_table(devices, devices, devices, -1.0))
    twisted = rotate(
        section_one,
        tuple((turning[None, None] for turning in dft_table(devices, row_count, extent, -1.0))),
    )
    section_two = contract(
        "nckb,bq->nckq", twisted, dft_table(row_count, row_count, row_count, -1.0)
    )
    return tuple((part_now.reshape(item_count, line_count, extent) for part_now in section_two))


def inverse_rows(fields):
    item_count, line_count, extent = fields[0].shape
    devices = lax.axis_size("slab")
    row_count = extent // devices
    reshaped = tuple(
        (part_now.reshape(item_count, line_count, devices, row_count) for part_now in fields)
    )
    section_one = contract(
        "nckq,bq->nckb", reshaped, dft_table(row_count, row_count, row_count, 1.0)
    )
    twisted = rotate(
        section_one,
        tuple((turning[None, None] for turning in dft_table(devices, row_count, extent, 1.0))),
    )
    section_two = contract("nckb,ak->ncab", twisted, dft_table(devices, devices, devices, 1.0))
    return tuple(
        (
            part_now.reshape(item_count, line_count, extent) * (1.0 / extent)
            for part_now in section_two
        )
    )


def inverse_lines(fields):
    item_count, line_count, extent = fields[0].shape
    devices = lax.axis_size("slab")
    row_count = extent // devices
    total_lines = line_count * devices
    reshaped = tuple(
        (part_now.reshape(item_count, line_count, devices, row_count) for part_now in fields)
    )
    section_one = contract("nkqr,bq->nkbr", reshaped, dft_table(devices, devices, devices, 1.0))
    twisted = rotate(
        section_one,
        tuple(
            (
                turning[None, :, :, None]
                for turning in dft_table(line_count, devices, total_lines, 1.0)
            )
        ),
    )
    section_two = contract(
        "nkbr,ak->nrab", twisted, dft_table(line_count, line_count, line_count, 1.0)
    )
    return tuple(
        (
            part_now.reshape(item_count, row_count, total_lines) * (1.0 / total_lines)
            for part_now in section_two
        )
    )


def phase_shift(values, wave_square, angular):
    slowness = 1.0 / jnp.array(ref_speeds, jnp.float32)
    wave_number = angular[:, None] * slowness[None, :]
    vertical = (wave_number * wave_number)[:, :, None, None] - wave_square[None, None]
    root_abs = jnp.sqrt(jnp.abs(vertical))
    real_part = jnp.where(
        vertical >= 0, jnp.cos(step_length * root_abs), jnp.exp(-step_length * root_abs)
    )
    imag_part = jnp.where(vertical >= 0, jnp.sin(step_length * root_abs), 0.0)
    shifted = rotate((values[0][:, None], values[1][:, None]), (real_part, imag_part))
    item_count = values[0].shape[0]
    return tuple(
        (
            part_now.reshape((item_count * len(ref_speeds),) + values[0].shape[1:])
            for part_now in shifted
        )
    )


def weights(speed_grid, chosen):
    speeds = jnp.array(ref_speeds, jnp.float32)
    lower_speed = jnp.zeros_like(speed_grid)
    upper_speed = jnp.zeros_like(speed_grid)
    for ref_index in range(len(ref_speeds) - 1):
        lower_speed = lower_speed + jnp.where(chosen == ref_index, speeds[ref_index], 0.0)
        upper_speed = upper_speed + jnp.where(chosen == ref_index, speeds[ref_index + 1], 0.0)
    fraction = (speed_grid - lower_speed) / (upper_speed - lower_speed)
    residual_phase = 1.0 / speed_grid - ((1.0 - fraction) / lower_speed + fraction / upper_speed)
    coefficients = []
    for ref_index in range(len(ref_speeds)):
        coefficients.append(
            jnp.where(chosen == ref_index, 1.0 - fraction, 0.0)
            + jnp.where(chosen == ref_index - 1, fraction, 0.0)
        )
    return (jnp.stack(coefficients), residual_phase)


def advance(fields, angular, coefficients, residual_phase, spec_square):
    item_count, row_count, extent = fields[0].shape
    prepared = forward_lines(fields)
    spectrum = forward_rows(
        (
            lax.all_to_all(prepared[0], "slab", split_axis=2, concat_axis=2, tiled=True),
            lax.all_to_all(prepared[1], "slab", split_axis=2, concat_axis=2, tiled=True),
        )
    )
    returned = inverse_rows(phase_shift(spectrum, spec_square, angular))
    waves = inverse_lines(
        (
            lax.all_to_all(returned[0], "slab", split_axis=2, concat_axis=2, tiled=True),
            lax.all_to_all(returned[1], "slab", split_axis=2, concat_axis=2, tiled=True),
        )
    )
    ref_count = len(ref_speeds)
    wave_real = waves[0].reshape(item_count, ref_count, row_count, extent)
    wave_imag = waves[1].reshape(item_count, ref_count, row_count, extent)
    blended_real = jnp.sum(coefficients[None] * wave_real, axis=1)
    blended_imag = jnp.sum(coefficients[None] * wave_imag, axis=1)
    angles = angular[:, None, None] * step_length * residual_phase[None]
    return rotate((blended_real, blended_imag), (jnp.cos(angles), jnp.sin(angles)))


def folded(indices, modulus):
    return jnp.minimum(indices, modulus - indices).astype(jnp.float32) * (2.0 * math.pi / modulus)


def per_device_general(wavefield, frequencies, velocity, bracket):
    devices = lax.axis_size("slab")
    device_index = lax.axis_index("slab")
    row_count = wavefield.shape[2]
    extent_y = wavefield.shape[3]
    extent_x = row_count * devices
    line_count = extent_y // devices
    speed_columns = lax.all_to_all(velocity, "slab", split_axis=2, concat_axis=1, tiled=True)
    speed_rows = jnp.transpose(speed_columns, (0, 2, 1))
    column = lax.iota(jnp.int32, extent_x)
    line_index = lax.iota(jnp.int32, line_count)
    spec_first = folded(column // row_count + devices * (column % row_count), extent_x)
    spec_second = folded(device_index * line_count + line_index, extent_y)
    spec_square = (
        spec_first[None, :] * spec_first[None, :] + spec_second[:, None] * spec_second[:, None]
    )
    current = (wavefield[:, 0], wavefield[:, 1])
    coefficients, residual_phase = weights(speed_rows[0], bracket[0])
    single = (current[0], current[1])
    pieces = [advance(single, frequencies, coefficients, residual_phase, spec_square)]
    current = (
        jnp.concatenate([piece[0] for piece in pieces], axis=0),
        jnp.concatenate([piece[1] for piece in pieces], axis=0),
    )
    image_rows = [jnp.sum(current[0], axis=0)]
    return (jnp.stack(current, axis=1), jnp.stack(image_rows))


radix = 16
lane = 128
full = radix * lane
row_block = 32
blocks = lane // row_block
piece = 2 * row_block + row_block // 2
vmem_bytes = 56 * 1024 * 1024


def split_table(table):
    upper = table.astype(ml_dtypes.bfloat16)
    lower = (table - upper.astype(np.float64)).astype(ml_dtypes.bfloat16)
    return upper, lower


def line_matrices(direction):
    angles = 2.0 * np.pi / lane * (np.outer(np.arange(lane), np.arange(lane)) % lane)
    cosine, sine = np.cos(angles), direction * np.sin(angles)
    return np.block([[cosine, sine], [-sine, cosine]])


def right_table(direction):
    upper, lower = split_table(line_matrices(direction))
    return np.concatenate([upper, upper, lower], axis=0)


def left_table(direction):
    upper, lower = split_table(line_matrices(direction).T)
    return np.concatenate([upper, upper, lower], axis=1)


def twiddle(direction, scale):
    angles = 2.0 * np.pi / full * np.outer(np.arange(radix), np.arange(lane))
    return np.stack([np.cos(angles), direction * np.sin(angles)], axis=1) * scale


def lane_twiddle(direction, scale):
    table = twiddle(direction, scale)[:, :, None, :]
    return np.ascontiguousarray(np.broadcast_to(table, (radix, 2, 8, lane))).astype(np.float32)


def sublane_twiddle(direction, scale):
    table = twiddle(direction, scale)[:, :, :, None]
    return np.ascontiguousarray(np.broadcast_to(table, (radix, 2, lane, lane))).astype(np.float32)


def root_series(offset, degree):
    nodes = np.polynomial.chebyshev.Chebyshev.interpolate(
        lambda q: np.sinc(np.sqrt(q) / np.pi) if offset else np.cos(np.sqrt(q)), degree, domain=[0.0, 9.0]
    )
    return [float(value) for value in nodes.convert(kind=np.polynomial.Polynomial).coef]


cos_series = root_series(0, 7)
sinc_series = root_series(1, 6)


def horner(series, argument):
    total = jnp.full_like(argument, series[-1])
    for value in series[-2::-1]:
        total = total * argument + value
    return total


def times(left, right):
    return left[0] * right[0] - left[1] * right[1], left[0] * right[1] + left[1] * right[0]


def quarter(values, direction):
    (a_re, a_im), (b_re, b_im), (c_re, c_im), (d_re, d_im) = values
    p_re, p_im, m_re, m_im = a_re + c_re, a_im + c_im, a_re - c_re, a_im - c_im
    q_re, q_im, n_re, n_im = b_re + d_re, b_im + d_im, b_re - d_re, b_im - d_im
    if direction < 0:
        turn_re, turn_im = n_im, -n_re
    else:
        turn_re, turn_im = -n_im, n_re
    return [
        (p_re + q_re, p_im + q_im),
        (m_re + turn_re, m_im + turn_im),
        (p_re - q_re, p_im - q_im),
        (m_re - turn_re, m_im - turn_im),
    ]


def turned(value, power, direction):
    re, im = value
    power %= 16
    if power == 0:
        return value
    if power == 4:
        return (-direction * im, direction * re) if direction < 0 else (-im, re)
    half = math.sqrt(0.5)
    if power == 2:
        return ((re - direction * im) * half, (im + direction * re) * half)
    if power == 6:
        return ((-re - direction * im) * half, (direction * re - im) * half)
    cosine, sine = math.cos(math.pi * power / 8), direction * math.sin(math.pi * power / 8)
    return re * cosine - im * sine, re * sine + im * cosine


def sixteen(values, direction):
    first = [quarter([values[4 * a + b] for a in range(4)], direction) for b in range(4)]
    result = [None] * 16
    for c in range(4):
        outs = quarter([turned(first[b][c], b * c, direction) for b in range(4)], direction)
        for d in range(4):
            result[c + 4 * d] = outs[d]
    return result


def halves(values):
    upper = values.astype(jnp.bfloat16)
    lower = (values - upper.astype(jnp.float32)).astype(jnp.bfloat16)
    return upper, lower


def right_product(values, table):
    upper, lower = halves(values)
    return jnp.dot(jnp.concatenate([upper, lower, upper], axis=1), table, preferred_element_type=jnp.float32)


def left_product(table, values):
    upper, lower = halves(values)
    return jnp.dot(table, jnp.concatenate([upper, lower, upper], axis=0), preferred_element_type=jnp.float32)


def tile(index):
    return slice(index * lane, (index + 1) * lane)


def lines_kernel(field_ref, speed_ref, turn_ref, table_ref, out_ref, work_ref):
    step = pl.program_id(0)

    def rows(index, carry):
        here = pl.ds(pl.multiple_of(index * 8, 8), 8)
        parts = sixteen(
            [(field_ref[0, 0, here, tile(j)], field_ref[0, 1, here, tile(j)]) for j in range(radix)], -1
        )
        for k in range(radix):
            re, im = times(parts[k], (turn_ref[k, 0], turn_ref[k, 1]))
            work_ref[k, here, 0:lane] = re
            work_ref[k, here, lane : 2 * lane] = im
        return carry

    lax.fori_loop(0, row_block // 8, rows, 0)
    lines = right_product(work_ref[...].reshape(radix * row_block, 2 * lane), table_ref[...])
    half = row_block // 2
    begin = lax.axis_index("shot") * (lane // 2) + step * half
    speed_rows = pl.ds(pl.multiple_of(begin, 8), half)
    for k in range(radix):
        block = lines[k * row_block : (k + 1) * row_block]
        out_ref[k, 0, 0:row_block] = block[:, 0:lane]
        out_ref[k, 0, row_block : 2 * row_block] = block[:, lane : 2 * lane]
        out_ref[k, 0, 2 * row_block : piece] = speed_ref[0, speed_rows, tile(k)]


def lines_call(wavefield, velocity):
    return pl.pallas_call(
        lines_kernel,
        grid=(blocks,),
        in_specs=[
            pl.BlockSpec((1, 2, row_block, full), lambda g: (0, 0, g, 0)),
            pl.BlockSpec((1, lane, full), lambda g: (0, 0, 0)),
            pl.BlockSpec((radix, 2, 8, lane), lambda g: (0, 0, 0, 0)),
            pl.BlockSpec((6 * lane, 2 * lane), lambda g: (0, 0)),
        ],
        out_specs=pl.BlockSpec((radix, 1, piece, lane), lambda g: (0, g, 0, 0)),
        out_shape=jax.ShapeDtypeStruct((radix, blocks, piece, lane), jnp.float32),
        scratch_shapes=[pltpu.VMEM((radix, row_block, 2 * lane), jnp.float32)],
        compiler_params=pltpu.CompilerParams(vmem_limit_bytes=vmem_bytes),
        name="forward_lines",
    )(wavefield, velocity, lane_twiddle(-1, 1.0), right_table(-1))


def phase_kernel(angular_ref, out_ref):
    device = lax.axis_index("slab")
    scale = 2.0 * math.pi / full
    column = lax.broadcasted_iota(jnp.int32, (32, lane), 1) * radix + device
    second = jnp.minimum(column, full - column).astype(jnp.float32) * scale
    second = second * second
    row = lax.broadcasted_iota(jnp.int32, (32, lane), 0)
    squares = []
    for speed in ref_speeds:
        number = angular_ref[0] * np.float32(1.0 / np.float32(speed))
        squares.append(number * number)

    def chunk(index, carry):
        k = index // 4
        begin = pl.multiple_of((index % 4) * 32, 32)
        here = pl.ds(begin, 32)
        there = pl.ds(pl.multiple_of(k * lane, lane), lane)
        position = (row + begin) * radix + k
        first = jnp.minimum(position, full - position).astype(jnp.float32) * scale
        wave_square = first * first + second
        for j in range(len(ref_speeds)):
            vertical = squares[j] - wave_square
            root = jnp.sqrt(jnp.abs(vertical))
            moving = vertical >= 0.0
            out_ref[j, 0, here, there] = jnp.where(moving, horner(cos_series, vertical), jnp.exp(-root))
            out_ref[j, 1, here, there] = jnp.where(moving, root * horner(sinc_series, vertical), 0.0)
        return carry

    lax.fori_loop(0, radix * 4, chunk, 0)


def phase_call(frequencies):
    count = len(ref_speeds)
    return pl.pallas_call(
        phase_kernel,
        in_specs=[pl.BlockSpec(memory_space=pltpu.SMEM)],
        out_specs=pl.BlockSpec((count, 2, lane, full), lambda: (0, 0, 0, 0)),
        out_shape=jax.ShapeDtypeStruct((count, 2, lane, full), jnp.float32),
        compiler_params=pltpu.CompilerParams(vmem_limit_bytes=vmem_bytes),
        cost_estimate=pl.CostEstimate(flops=60 * count * lane * full, bytes_accessed=8 * count * lane * full, transcendentals=0),
        name="phase_factors",
    )(frequencies)


def rows_kernel(in_ref, phase_ref, ahead_ref, back_ref, ahead_table_ref, back_table_ref, out_ref, work_ref, spec_ref):
    @pl.when(pl.program_id(0) == 0)
    def _():
        def rows(index, carry):
            group = index // (row_block // 8)
            local = pl.multiple_of((index % (row_block // 8)) * 8, 8)
            here = pl.ds(pl.multiple_of(index * 8, 8), 8)
            there = pl.ds(pl.multiple_of(index * 8 + lane, 8), 8)
            parts = sixteen(
                [
                    (in_ref[s, group, pl.ds(local, 8), :], in_ref[s, group, pl.ds(local + row_block, 8), :])
                    for s in range(radix)
                ],
                -1,
            )
            for k in range(radix):
                re, im = times(parts[k], (ahead_ref[k, 0, here, :], ahead_ref[k, 1, here, :]))
                work_ref[here, tile(k)] = re
                work_ref[there, tile(k)] = im
            return carry

        lax.fori_loop(0, lane // 8, rows, 0)

        def pairs(index, carry):
            columns = pl.ds(pl.multiple_of(index * 2 * lane, 2 * lane), 2 * lane)
            spec_ref[:, columns] = left_product(ahead_table_ref[...], work_ref[:, columns])
            return carry

        lax.fori_loop(0, radix // 2, pairs, 0)

    def shifted(index, carry):
        columns = pl.ds(pl.multiple_of(index * 2 * lane, 2 * lane), 2 * lane)
        re, im = times(
            (spec_ref[0:lane, columns], spec_ref[lane : 2 * lane, columns]),
            (phase_ref[0, 0, :, columns], phase_ref[0, 1, :, columns]),
        )
        work_ref[:, columns] = left_product(back_table_ref[...], jnp.concatenate([re, im], axis=0))
        return carry

    lax.fori_loop(0, radix // 2, shifted, 0)

    def back(index, carry):
        here = pl.ds(pl.multiple_of(index * 8, 8), 8)
        there = pl.ds(pl.multiple_of(index * 8 + lane, 8), 8)
        parts = sixteen(
            [
                times(
                    (work_ref[here, tile(k)], work_ref[there, tile(k)]),
                    (back_ref[k, 0, here, :], back_ref[k, 1, here, :]),
                )
                for k in range(radix)
            ],
            1,
        )
        for s in range(radix):
            out_ref[s, 0, 0, here, :] = parts[s][0]
            out_ref[s, 0, 1, here, :] = parts[s][1]
        return carry

    lax.fori_loop(0, lane // 8, back, 0)


def rows_call(arrived, phase):
    count = len(ref_speeds)
    whole4 = lambda j: (0, 0, 0, 0)
    whole2 = lambda j: (0, 0)
    return pl.pallas_call(
        rows_kernel,
        grid=(count,),
        in_specs=[
            pl.BlockSpec((radix, blocks, piece, lane), whole4),
            pl.BlockSpec((1, 2, lane, full), lambda j: (j, 0, 0, 0)),
            pl.BlockSpec((radix, 2, lane, lane), whole4),
            pl.BlockSpec((radix, 2, lane, lane), whole4),
            pl.BlockSpec((2 * lane, 6 * lane), whole2),
            pl.BlockSpec((2 * lane, 6 * lane), whole2),
        ],
        out_specs=pl.BlockSpec((radix, 1, 2, lane, lane), lambda j: (0, j, 0, 0, 0)),
        out_shape=jax.ShapeDtypeStruct((radix, count, 2, lane, lane), jnp.float32),
        scratch_shapes=[
            pltpu.VMEM((2 * lane, full), jnp.float32),
            pltpu.VMEM((2 * lane, full), jnp.float32),
        ],
        compiler_params=pltpu.CompilerParams(vmem_limit_bytes=vmem_bytes),
        name="rows_there_and_back",
    )(
        arrived,
        phase,
        sublane_twiddle(-1, 1.0),
        sublane_twiddle(1, 1.0 / full),
        left_table(-1),
        left_table(1),
    )


def blend_kernel(angular_ref, own_ref, other_ref, bracket_ref, out_ref, tile_ref):
    shot = lax.axis_index("shot")
    half = row_block // 2
    for d in range(radix):
        for g in range(blocks):
            own = pl.ds(pl.multiple_of(shot * (lane // 2) + g * half, 8), half)
            other = pl.ds(pl.multiple_of((1 - shot) * (lane // 2) + g * half, 8), half)
            tile_ref[own, :] = own_ref[d, g]
            tile_ref[other, :] = other_ref[d, g]
        speed = jnp.transpose(tile_ref[...])
        lower = bracket_ref[0, :, tile(d)]
        first = lower == 0
        low = jnp.where(first, ref_speeds[0], ref_speeds[1])
        width = jnp.where(first, 1.0 / (ref_speeds[1] - ref_speeds[0]), 1.0 / (ref_speeds[2] - ref_speeds[1]))
        fraction = (speed - low) * width
        low_slowness = jnp.where(first, 1.0 / ref_speeds[0], 1.0 / ref_speeds[1])
        high_slowness = jnp.where(first, 1.0 / ref_speeds[1], 1.0 / ref_speeds[2])
        residual = 1.0 / speed - ((1.0 - fraction) * low_slowness + fraction * high_slowness)
        angle = angular_ref[0] * step_length * residual
        square = angle * angle
        cosine = horner([1.0, -1 / 2, 1 / 24, -1 / 720, 1 / 40320], square)
        sine = angle * horner([1.0, -1 / 6, 1 / 120, -1 / 5040, 1 / 362880], square)
        out_ref[0, :, tile(d)] = fraction + jnp.where(first, 0.0, 1.0)
        out_ref[1, :, tile(d)] = cosine
        out_ref[2, :, tile(d)] = sine


def blend_call(frequencies, own, other, bracket):
    return pl.pallas_call(
        blend_kernel,
        in_specs=[
            pl.BlockSpec(memory_space=pltpu.SMEM),
            pl.BlockSpec((radix, blocks, row_block // 2, lane), lambda: (0, 0, 0, 0)),
            pl.BlockSpec((radix, blocks, row_block // 2, lane), lambda: (0, 0, 0, 0)),
            pl.BlockSpec((1, lane, full), lambda: (0, 0, 0)),
        ],
        out_specs=pl.BlockSpec((3, lane, full), lambda: (0, 0, 0)),
        out_shape=jax.ShapeDtypeStruct((3, lane, full), jnp.float32),
        scratch_shapes=[pltpu.VMEM((lane, lane), jnp.float32)],
        compiler_params=pltpu.CompilerParams(vmem_limit_bytes=vmem_bytes),
        cost_estimate=pl.CostEstimate(flops=60 * lane * full, bytes_accessed=24 * lane * full, transcendentals=0),
        name="blend_factors",
    )(frequencies, own, other, bracket)


def finish_kernel(in_ref, blend_ref, turn_ref, table_ref, out_ref, image_ref, work_ref, wave_ref):
    count = len(ref_speeds)
    for j in range(count):
        values = jnp.concatenate([in_ref[:, j, 0], in_ref[:, j, 1]], axis=2)
        product = right_product(values.reshape(radix * row_block, 2 * lane), table_ref[...])
        work_ref[j] = product.reshape(radix, row_block, 2 * lane)

    def rows(index, carry):
        here = pl.ds(pl.multiple_of(index * 8, 8), 8)
        for j in range(count):
            parts = sixteen(
                [
                    times(
                        (work_ref[j, k, here, 0:lane], work_ref[j, k, here, lane : 2 * lane]),
                        (turn_ref[k, 0], turn_ref[k, 1]),
                    )
                    for k in range(radix)
                ],
                1,
            )
            for s in range(radix):
                wave_ref[j, 0, :, tile(s)] = parts[s][0]
                wave_ref[j, 1, :, tile(s)] = parts[s][1]
        for s in range(radix):
            place = blend_ref[0, here, tile(s)]
            weights_now = (
                jnp.maximum(1.0 - place, 0.0),
                1.0 - jnp.abs(place - 1.0),
                jnp.maximum(place - 1.0, 0.0),
            )
            mixed = [
                sum(weights_now[j] * wave_ref[j, part, :, tile(s)] for j in range(count)) for part in range(2)
            ]
            re, im = times(mixed, (blend_ref[1, here, tile(s)], blend_ref[2, here, tile(s)]))
            out_ref[0, 0, here, tile(s)] = re
            out_ref[0, 1, here, tile(s)] = im
            image_ref[0, here, tile(s)] = re
        return carry

    lax.fori_loop(0, row_block // 8, rows, 0)


def finish_call(returned, blend):
    count = len(ref_speeds)
    return pl.pallas_call(
        finish_kernel,
        grid=(blocks,),
        in_specs=[
            pl.BlockSpec((radix, count, 2, row_block, lane), lambda g: (0, 0, 0, g, 0)),
            pl.BlockSpec((3, row_block, full), lambda g: (0, g, 0)),
            pl.BlockSpec((radix, 2, 8, lane), lambda g: (0, 0, 0, 0)),
            pl.BlockSpec((6 * lane, 2 * lane), lambda g: (0, 0)),
        ],
        out_specs=[
            pl.BlockSpec((1, 2, row_block, full), lambda g: (0, 0, g, 0)),
            pl.BlockSpec((1, row_block, full), lambda g: (0, g, 0)),
        ],
        out_shape=[
            jax.ShapeDtypeStruct((1, 2, lane, full), jnp.float32),
            jax.ShapeDtypeStruct((1, lane, full), jnp.float32),
        ],
        scratch_shapes=[
            pltpu.VMEM((count, radix, row_block, 2 * lane), jnp.float32),
            pltpu.VMEM((count, 2, 8, full), jnp.float32),
        ],
        compiler_params=pltpu.CompilerParams(vmem_limit_bytes=vmem_bytes),
        name="inverse_lines",
    )(returned, blend, lane_twiddle(1, 1.0 / full), right_table(1))


def exchange(values):
    return lax.all_to_all(values, "slab", split_axis=0, concat_axis=0, tiled=True)


def per_device(wavefield, frequencies, velocity, bracket):
    sent = lines_call(wavefield, velocity)
    phase = phase_call(frequencies)
    arrived = exchange(sent)
    own = arrived[:, :, 2 * row_block :, :]
    other = lax.ppermute(own, "shot", [(0, 1), (1, 0)])
    returned = exchange(rows_call(arrived, phase))
    blend = blend_call(frequencies, own, other, bracket)
    propagated, image = finish_call(returned, blend)
    return propagated, image


def fits(mesh, shapes):
    wavefield, velocity = shapes
    return (
        mesh.shape["slab"] == radix
        and mesh.shape["shot"] == 2
        and wavefield == (2, 2, full, full)
        and velocity == (1, full, full)
    )


def solution(mesh):
    def program(wavefield, frequencies, velocity, bracket):
        small = fits(mesh, (wavefield.shape, velocity.shape))
        return jax.shard_map(
            per_device if small else per_device_general,
            mesh=mesh,
            in_specs=(
                P("shot", None, "slab", None),
                P("shot"),
                P(None, "slab", None),
                P(None, "slab", None),
            ),
            out_specs=(P("shot", None, "slab", None), P("shot", "slab", None)),
            check_vma=False,
        )(wavefield, frequencies, velocity, bracket)

    return program
```

```python
import math

import jax
import jax.numpy as jnp
import ml_dtypes
import numpy as np
from jax import lax
from jax.experimental import pallas as pl
from jax.experimental.pallas import tpu as pltpu
from jax.sharding import PartitionSpec as P

ref_speeds = (1.0, 1.5, 2.25)
step_length = 1.0
highest = lax.Precision.HIGHEST


def dft_table(height, breadth, modulus, direction):
    down_index = lax.iota(jnp.int32, height)[:, None]
    across_index = lax.iota(jnp.int32, breadth)[None, :]
    angles = (down_index * across_index % modulus).astype(jnp.float32) * (
        direction * 2.0 * math.pi / modulus
    )
    return (jnp.cos(angles), jnp.sin(angles))


def contract(pattern, left_pair, right_pair):

    def product(one_side, other_side):
        return jnp.einsum(pattern, one_side, other_side, precision=highest)

    return (
        product(left_pair[0], right_pair[0]) - product(left_pair[1], right_pair[1]),
        product(left_pair[0], right_pair[1]) + product(left_pair[1], right_pair[0]),
    )


def rotate(values, factor_pair):
    return (
        values[0] * factor_pair[0] - values[1] * factor_pair[1],
        values[0] * factor_pair[1] + values[1] * factor_pair[0],
    )


def forward_lines(fields):
    item_count, row_count, extent = fields[0].shape
    devices = lax.axis_size("slab")
    line_count = extent // devices
    reshaped = tuple(
        (part_now.reshape(item_count, row_count, line_count, devices) for part_now in fields)
    )
    section_one = contract(
        "nrab,ak->nrkb", reshaped, dft_table(line_count, line_count, line_count, -1.0)
    )
    twisted = rotate(
        section_one,
        tuple((turning[None, None] for turning in dft_table(line_count, devices, extent, -1.0))),
    )
    section_two = contract("nrkb,bq->nkqr", twisted, dft_table(devices, devices, devices, -1.0))
    return tuple(
        (part_now.reshape(item_count, line_count, devices * row_count) for part_now in section_two)
    )


def forward_rows(fields):
    item_count, line_count, extent = fields[0].shape
    devices = lax.axis_size("slab")
    row_count = extent // devices
    reshaped = tuple(
        (part_now.reshape(item_count, line_count, devices, row_count) for part_now in fields)
    )
    section_one = contract("ncab,ak->nckb", reshaped, dft_table(devices, devices, devices, -1.0))
    twisted = rotate(
        section_one,
        tuple((turning[None, None] for turning in dft_table(devices, row_count, extent, -1.0))),
    )
    section_two = contract(
        "nckb,bq->nckq", twisted, dft_table(row_count, row_count, row_count, -1.0)
    )
    return tuple((part_now.reshape(item_count, line_count, extent) for part_now in section_two))


def inverse_rows(fields):
    item_count, line_count, extent = fields[0].shape
    devices = lax.axis_size("slab")
    row_count = extent // devices
    reshaped = tuple(
        (part_now.reshape(item_count, line_count, devices, row_count) for part_now in fields)
    )
    section_one = contract(
        "nckq,bq->nckb", reshaped, dft_table(row_count, row_count, row_count, 1.0)
    )
    twisted = rotate(
        section_one,
        tuple((turning[None, None] for turning in dft_table(devices, row_count, extent, 1.0))),
    )
    section_two = contract("nckb,ak->ncab", twisted, dft_table(devices, devices, devices, 1.0))
    return tuple(
        (
            part_now.reshape(item_count, line_count, extent) * (1.0 / extent)
            for part_now in section_two
        )
    )


def inverse_lines(fields):
    item_count, line_count, extent = fields[0].shape
    devices = lax.axis_size("slab")
    row_count = extent // devices
    total_lines = line_count * devices
    reshaped = tuple(
        (part_now.reshape(item_count, line_count, devices, row_count) for part_now in fields)
    )
    section_one = contract("nkqr,bq->nkbr", reshaped, dft_table(devices, devices, devices, 1.0))
    twisted = rotate(
        section_one,
        tuple(
            (
                turning[None, :, :, None]
                for turning in dft_table(line_count, devices, total_lines, 1.0)
            )
        ),
    )
    section_two = contract(
        "nkbr,ak->nrab", twisted, dft_table(line_count, line_count, line_count, 1.0)
    )
    return tuple(
        (
            part_now.reshape(item_count, row_count, total_lines) * (1.0 / total_lines)
            for part_now in section_two
        )
    )


def phase_shift(values, wave_square, angular):
    slowness = 1.0 / jnp.array(ref_speeds, jnp.float32)
    wave_number = angular[:, None] * slowness[None, :]
    vertical = (wave_number * wave_number)[:, :, None, None] - wave_square[None, None]
    root_abs = jnp.sqrt(jnp.abs(vertical))
    real_part = jnp.where(
        vertical >= 0, jnp.cos(step_length * root_abs), jnp.exp(-step_length * root_abs)
    )
    imag_part = jnp.where(vertical >= 0, jnp.sin(step_length * root_abs), 0.0)
    shifted = rotate((values[0][:, None], values[1][:, None]), (real_part, imag_part))
    item_count = values[0].shape[0]
    return tuple(
        (
            part_now.reshape((item_count * len(ref_speeds),) + values[0].shape[1:])
            for part_now in shifted
        )
    )


def weights(speed_grid, chosen):
    speeds = jnp.array(ref_speeds, jnp.float32)
    lower_speed = jnp.zeros_like(speed_grid)
    upper_speed = jnp.zeros_like(speed_grid)
    for ref_index in range(len(ref_speeds) - 1):
        lower_speed = lower_speed + jnp.where(chosen == ref_index, speeds[ref_index], 0.0)
        upper_speed = upper_speed + jnp.where(chosen == ref_index, speeds[ref_index + 1], 0.0)
    fraction = (speed_grid - lower_speed) / (upper_speed - lower_speed)
    residual_phase = 1.0 / speed_grid - ((1.0 - fraction) / lower_speed + fraction / upper_speed)
    coefficients = []
    for ref_index in range(len(ref_speeds)):
        coefficients.append(
            jnp.where(chosen == ref_index, 1.0 - fraction, 0.0)
            + jnp.where(chosen == ref_index - 1, fraction, 0.0)
        )
    return (jnp.stack(coefficients), residual_phase)


def advance(fields, angular, coefficients, residual_phase, spec_square):
    item_count, row_count, extent = fields[0].shape
    prepared = forward_lines(fields)
    spectrum = forward_rows(
        (
            lax.all_to_all(prepared[0], "slab", split_axis=2, concat_axis=2, tiled=True),
            lax.all_to_all(prepared[1], "slab", split_axis=2, concat_axis=2, tiled=True),
        )
    )
    returned = inverse_rows(phase_shift(spectrum, spec_square, angular))
    waves = inverse_lines(
        (
            lax.all_to_all(returned[0], "slab", split_axis=2, concat_axis=2, tiled=True),
            lax.all_to_all(returned[1], "slab", split_axis=2, concat_axis=2, tiled=True),
        )
    )
    ref_count = len(ref_speeds)
    wave_real = waves[0].reshape(item_count, ref_count, row_count, extent)
    wave_imag = waves[1].reshape(item_count, ref_count, row_count, extent)
    blended_real = jnp.sum(coefficients[None] * wave_real, axis=1)
    blended_imag = jnp.sum(coefficients[None] * wave_imag, axis=1)
    angles = angular[:, None, None] * step_length * residual_phase[None]
    return rotate((blended_real, blended_imag), (jnp.cos(angles), jnp.sin(angles)))


def folded(indices, modulus):
    return jnp.minimum(indices, modulus - indices).astype(jnp.float32) * (2.0 * math.pi / modulus)


def per_device_general(wavefield, frequencies, velocity, bracket):
    devices = lax.axis_size("slab")
    device_index = lax.axis_index("slab")
    row_count = wavefield.shape[2]
    extent_y = wavefield.shape[3]
    extent_x = row_count * devices
    line_count = extent_y // devices
    speed_columns = lax.all_to_all(velocity, "slab", split_axis=2, concat_axis=1, tiled=True)
    speed_rows = jnp.transpose(speed_columns, (0, 2, 1))
    column = lax.iota(jnp.int32, extent_x)
    line_index = lax.iota(jnp.int32, line_count)
    spec_first = folded(column // row_count + devices * (column % row_count), extent_x)
    spec_second = folded(device_index * line_count + line_index, extent_y)
    spec_square = (
        spec_first[None, :] * spec_first[None, :] + spec_second[:, None] * spec_second[:, None]
    )
    current = (wavefield[:, 0], wavefield[:, 1])
    coefficients, residual_phase = weights(speed_rows[0], bracket[0])
    single = (current[0], current[1])
    pieces = [advance(single, frequencies, coefficients, residual_phase, spec_square)]
    current = (
        jnp.concatenate([piece[0] for piece in pieces], axis=0),
        jnp.concatenate([piece[1] for piece in pieces], axis=0),
    )
    image_rows = [jnp.sum(current[0], axis=0)]
    return (jnp.stack(current, axis=1), jnp.stack(image_rows))


radix = 16
lane = 128
full = radix * lane
row_block = 32
blocks = lane // row_block
piece = 2 * row_block + row_block // 2
vmem_bytes = 56 * 1024 * 1024
rows_vmem_bytes = 50 * 1024 * 1024


def split_table(table):
    upper = table.astype(ml_dtypes.bfloat16)
    lower = (table - upper.astype(np.float64)).astype(ml_dtypes.bfloat16)
    return upper, lower


def line_matrices(direction):
    angles = 2.0 * np.pi / lane * (np.outer(np.arange(lane), np.arange(lane)) % lane)
    cosine, sine = np.cos(angles), direction * np.sin(angles)
    return np.block([[cosine, sine], [-sine, cosine]])


def right_table(direction):
    upper, lower = split_table(line_matrices(direction))
    return np.concatenate([upper, upper, lower], axis=0)


def left_table(direction, scale):
    upper, lower = split_table(line_matrices(direction).T * scale)
    return np.concatenate([upper, upper, lower], axis=1)


def twiddle(direction, scale):
    angles = 2.0 * np.pi / full * np.outer(np.arange(radix), np.arange(lane))
    return np.stack([np.cos(angles), direction * np.sin(angles)], axis=1) * scale


def lane_twiddle(direction, scale):
    table = twiddle(direction, scale)[:, :, None, :]
    return np.ascontiguousarray(np.broadcast_to(table, (radix, 2, 8, lane))).astype(np.float32)


def column_twiddle(direction):
    table = np.zeros((lane, lane), np.float32)
    table[:, : 2 * radix] = twiddle(direction, 1.0).reshape(2 * radix, lane).T
    return table


def root_series(offset, degree):
    nodes = np.polynomial.chebyshev.Chebyshev.interpolate(
        lambda q: np.sinc(np.sqrt(q) / np.pi) if offset else np.cos(np.sqrt(q)), degree, domain=[0.0, 9.0]
    )
    return [float(value) for value in nodes.convert(kind=np.polynomial.Polynomial).coef]


cos_series = root_series(0, 7)
sinc_series = root_series(1, 6)


def horner(series, argument):
    total = jnp.full_like(argument, series[-1])
    for value in series[-2::-1]:
        total = total * argument + value
    return total


def times(left, right):
    return left[0] * right[0] - left[1] * right[1], left[0] * right[1] + left[1] * right[0]


def conjugate_times(left, right):
    return left[0] * right[0] + left[1] * right[1], left[1] * right[0] - left[0] * right[1]


def quarter(values, direction):
    (a_re, a_im), (b_re, b_im), (c_re, c_im), (d_re, d_im) = values
    p_re, p_im, m_re, m_im = a_re + c_re, a_im + c_im, a_re - c_re, a_im - c_im
    q_re, q_im, n_re, n_im = b_re + d_re, b_im + d_im, b_re - d_re, b_im - d_im
    if direction < 0:
        turn_re, turn_im = n_im, -n_re
    else:
        turn_re, turn_im = -n_im, n_re
    return [
        (p_re + q_re, p_im + q_im),
        (m_re + turn_re, m_im + turn_im),
        (p_re - q_re, p_im - q_im),
        (m_re - turn_re, m_im - turn_im),
    ]


def turned(value, power, direction):
    re, im = value
    power %= 16
    if power == 0:
        return value
    if power == 4:
        return (-direction * im, direction * re) if direction < 0 else (-im, re)
    half = math.sqrt(0.5)
    if power == 2:
        return ((re - direction * im) * half, (im + direction * re) * half)
    if power == 6:
        return ((-re - direction * im) * half, (direction * re - im) * half)
    cosine, sine = math.cos(math.pi * power / 8), direction * math.sin(math.pi * power / 8)
    return re * cosine - im * sine, re * sine + im * cosine


def sixteen(values, direction):
    first = [quarter([values[4 * a + b] for a in range(4)], direction) for b in range(4)]
    result = [None] * 16
    for c in range(4):
        outs = quarter([turned(first[b][c], b * c, direction) for b in range(4)], direction)
        for d in range(4):
            result[c + 4 * d] = outs[d]
    return result


def halves(values):
    upper = values.astype(jnp.bfloat16)
    lower = (values - upper.astype(jnp.float32)).astype(jnp.bfloat16)
    return upper, lower


def right_product(values, table):
    upper, lower = halves(values)
    return jnp.dot(jnp.concatenate([upper, lower, upper], axis=1), table, preferred_element_type=jnp.float32)


def left_product(table, values):
    upper, lower = halves(values)
    return jnp.dot(table, jnp.concatenate([upper, lower, upper], axis=0), preferred_element_type=jnp.float32)


def tile(index):
    return slice(index * lane, (index + 1) * lane)


def lines_kernel(field_ref, speed_ref, turn_ref, table_ref, out_ref, work_ref):
    step = pl.program_id(0)

    def rows(index, carry):
        here = pl.ds(pl.multiple_of(index * 8, 8), 8)
        parts = sixteen(
            [(field_ref[0, 0, here, tile(j)], field_ref[0, 1, here, tile(j)]) for j in range(radix)], -1
        )
        for k in range(radix):
            re, im = times(parts[k], (turn_ref[k, 0], turn_ref[k, 1]))
            work_ref[k, here, 0:lane] = re
            work_ref[k, here, lane : 2 * lane] = im
        return carry

    lax.fori_loop(0, row_block // 8, rows, 0)
    lines = right_product(work_ref[...].reshape(radix * row_block, 2 * lane), table_ref[...])
    half = row_block // 2
    begin = lax.axis_index("shot") * (lane // 2) + step * half
    speed_rows = pl.ds(pl.multiple_of(begin, 8), half)
    for k in range(radix):
        block = lines[k * row_block : (k + 1) * row_block]
        out_ref[k, 0, 0:row_block] = block[:, 0:lane]
        out_ref[k, 0, row_block : 2 * row_block] = block[:, lane : 2 * lane]
        out_ref[k, 0, 2 * row_block : piece] = speed_ref[0, speed_rows, tile(k)]


def lines_call(wavefield, velocity):
    return pl.pallas_call(
        lines_kernel,
        grid=(blocks,),
        in_specs=[
            pl.BlockSpec((1, 2, row_block, full), lambda g: (0, 0, g, 0)),
            pl.BlockSpec((1, lane, full), lambda g: (0, 0, 0)),
            pl.BlockSpec((radix, 2, 8, lane), lambda g: (0, 0, 0, 0)),
            pl.BlockSpec((6 * lane, 2 * lane), lambda g: (0, 0)),
        ],
        out_specs=pl.BlockSpec((radix, 1, piece, lane), lambda g: (0, g, 0, 0)),
        out_shape=jax.ShapeDtypeStruct((radix, blocks, piece, lane), jnp.float32),
        scratch_shapes=[pltpu.VMEM((radix, row_block, 2 * lane), jnp.float32)],
        compiler_params=pltpu.CompilerParams(vmem_limit_bytes=vmem_bytes),
        name="forward_lines",
    )(wavefield, velocity, lane_twiddle(-1, 1.0), right_table(-1))


def phase_kernel(angular_ref, out_ref):
    device = lax.axis_index("slab")
    scale = 2.0 * math.pi / full
    column = lax.broadcasted_iota(jnp.int32, (32, lane), 1) * radix + device
    second = jnp.minimum(column, full - column).astype(jnp.float32) * scale
    second = second * second
    row = lax.broadcasted_iota(jnp.int32, (32, lane), 0)
    squares = []
    for speed in ref_speeds:
        number = angular_ref[0] * np.float32(1.0 / np.float32(speed))
        squares.append(number * number)

    def chunk(index, carry):
        k = index // 4
        begin = pl.multiple_of((index % 4) * 32, 32)
        here = pl.ds(begin, 32)
        there = pl.ds(pl.multiple_of(k * lane, lane), lane)
        position = (row + begin) * radix + k
        first = jnp.minimum(position, full - position).astype(jnp.float32) * scale
        wave_square = first * first + second
        for j in range(len(ref_speeds)):
            vertical = squares[j] - wave_square
            root = jnp.sqrt(jnp.abs(vertical))
            moving = vertical >= 0.0
            out_ref[j, 0, here, there] = jnp.where(moving, horner(cos_series, vertical), jnp.exp(-root))
            out_ref[j, 1, here, there] = jnp.where(moving, root * horner(sinc_series, vertical), 0.0)
        return carry

    lax.fori_loop(0, radix * 4, chunk, 0)


def phase_call(frequencies):
    count = len(ref_speeds)
    return pl.pallas_call(
        phase_kernel,
        in_specs=[pl.BlockSpec(memory_space=pltpu.SMEM)],
        out_specs=pl.BlockSpec((count, 2, lane, full), lambda: (0, 0, 0, 0)),
        out_shape=jax.ShapeDtypeStruct((count, 2, lane, full), jnp.float32),
        compiler_params=pltpu.CompilerParams(vmem_limit_bytes=vmem_bytes),
        cost_estimate=pl.CostEstimate(flops=60 * count * lane * full, bytes_accessed=8 * count * lane * full, transcendentals=0),
        name="phase_factors",
    )(frequencies)


def rows_kernel(
    in_ref, phase_ref, column_ref, ahead_table_ref, back_table_ref, out_ref,
    work_ref, spec_ref, turn_ref, factor_ref, field_ref, factor_sem, field_sem,
):
    count = len(ref_speeds)

    def factor_copy(j):
        return pltpu.make_async_copy(phase_ref.at[j], factor_ref.at[j], factor_sem.at[j])

    def field_copy(j):
        return pltpu.make_async_copy(field_ref.at[j % 2], out_ref.at[:, j], field_sem.at[j % 2])

    for j in range(count):
        factor_copy(j).start()

    def rows(index, carry):
        group = index // (row_block // 8)
        local = pl.multiple_of((index % (row_block // 8)) * 8, 8)
        here = pl.ds(pl.multiple_of(index * 8, 8), 8)
        there = pl.ds(pl.multiple_of(index * 8 + lane, 8), 8)
        columns = column_ref[here, :]
        parts = sixteen(
            [
                (in_ref[s, group, pl.ds(local, 8), :], in_ref[s, group, pl.ds(local + row_block, 8), :])
                for s in range(radix)
            ],
            -1,
        )
        for k in range(radix):
            turn = tuple(
                jnp.broadcast_to(columns[:, 2 * k + part : 2 * k + part + 1], (8, lane)) for part in range(2)
            )
            turn_ref[k, 0, here, :] = turn[0]
            turn_ref[k, 1, here, :] = turn[1]
            re, im = times(parts[k], turn)
            work_ref[here, tile(k)] = re
            work_ref[there, tile(k)] = im
        return carry

    lax.fori_loop(0, lane // 8, rows, 0)

    def pairs(index, carry):
        columns = pl.ds(pl.multiple_of(index * 2 * lane, 2 * lane), 2 * lane)
        spec_ref[:, columns] = left_product(ahead_table_ref[...], work_ref[:, columns])
        return carry

    lax.fori_loop(0, radix // 2, pairs, 0, unroll=True)

    for j in range(count):
        factor_copy(j).wait()

        def shifted(index, carry):
            columns = pl.ds(pl.multiple_of(index * 2 * lane, 2 * lane), 2 * lane)
            re, im = times(
                (spec_ref[0:lane, columns], spec_ref[lane : 2 * lane, columns]),
                (factor_ref[j, 0, :, columns], factor_ref[j, 1, :, columns]),
            )
            work_ref[:, columns] = left_product(back_table_ref[...], jnp.concatenate([re, im], axis=0))
            return carry

        lax.fori_loop(0, radix // 2, shifted, 0, unroll=True)
        if j >= 2:
            field_copy(j - 2).wait()

        def back(index, carry):
            here = pl.ds(pl.multiple_of(index * 8, 8), 8)
            there = pl.ds(pl.multiple_of(index * 8 + lane, 8), 8)
            parts = sixteen(
                [
                    conjugate_times(
                        (work_ref[here, tile(k)], work_ref[there, tile(k)]),
                        (turn_ref[k, 0, here, :], turn_ref[k, 1, here, :]),
                    )
                    for k in range(radix)
                ],
                1,
            )
            for s in range(radix):
                field_ref[j % 2, s, 0, here, :] = parts[s][0]
                field_ref[j % 2, s, 1, here, :] = parts[s][1]
            return carry

        lax.fori_loop(0, lane // 8, back, 0)
        field_copy(j).start()

    for j in range(count - 2, count):
        field_copy(j).wait()


def rows_call(arrived, phase):
    count = len(ref_speeds)
    in_vmem = pl.BlockSpec(memory_space=pltpu.VMEM)
    in_hbm = pl.BlockSpec(memory_space=pltpu.HBM)
    return pl.pallas_call(
        rows_kernel,
        in_specs=[in_vmem, in_hbm, in_vmem, in_vmem, in_vmem],
        out_specs=in_hbm,
        out_shape=jax.ShapeDtypeStruct((radix, count, 2, lane, lane), jnp.float32),
        scratch_shapes=[
            pltpu.VMEM((2 * lane, full), jnp.float32),
            pltpu.VMEM((2 * lane, full), jnp.float32),
            pltpu.VMEM((radix, 2, lane, lane), jnp.float32),
            pltpu.VMEM((count, 2, lane, full), jnp.float32),
            pltpu.VMEM((2, radix, 2, lane, lane), jnp.float32),
            pltpu.SemaphoreType.DMA((count,)),
            pltpu.SemaphoreType.DMA((2,)),
        ],
        compiler_params=pltpu.CompilerParams(vmem_limit_bytes=rows_vmem_bytes),
        name="rows_there_and_back",
    )(arrived, phase, column_twiddle(-1), left_table(-1, 1.0), left_table(1, 1.0 / full))


def blend_kernel(angular_ref, own_ref, other_ref, bracket_ref, out_ref, tile_ref):
    shot = lax.axis_index("shot")
    half = row_block // 2
    for d in range(radix):
        for g in range(blocks):
            own = pl.ds(pl.multiple_of(shot * (lane // 2) + g * half, 8), half)
            other = pl.ds(pl.multiple_of((1 - shot) * (lane // 2) + g * half, 8), half)
            tile_ref[own, :] = own_ref[d, g]
            tile_ref[other, :] = other_ref[d, g]
        speed = jnp.transpose(tile_ref[...])
        lower = bracket_ref[0, :, tile(d)]
        first = lower == 0
        low = jnp.where(first, ref_speeds[0], ref_speeds[1])
        width = jnp.where(first, 1.0 / (ref_speeds[1] - ref_speeds[0]), 1.0 / (ref_speeds[2] - ref_speeds[1]))
        fraction = (speed - low) * width
        low_slowness = jnp.where(first, 1.0 / ref_speeds[0], 1.0 / ref_speeds[1])
        high_slowness = jnp.where(first, 1.0 / ref_speeds[1], 1.0 / ref_speeds[2])
        residual = 1.0 / speed - ((1.0 - fraction) * low_slowness + fraction * high_slowness)
        angle = angular_ref[0] * step_length * residual
        square = angle * angle
        cosine = horner([1.0, -1 / 2, 1 / 24, -1 / 720, 1 / 40320], square)
        sine = angle * horner([1.0, -1 / 6, 1 / 120, -1 / 5040, 1 / 362880], square)
        out_ref[0, :, tile(d)] = fraction + jnp.where(first, 0.0, 1.0)
        out_ref[1, :, tile(d)] = cosine
        out_ref[2, :, tile(d)] = sine


def blend_call(frequencies, own, other, bracket):
    return pl.pallas_call(
        blend_kernel,
        in_specs=[
            pl.BlockSpec(memory_space=pltpu.SMEM),
            pl.BlockSpec((radix, blocks, row_block // 2, lane), lambda: (0, 0, 0, 0)),
            pl.BlockSpec((radix, blocks, row_block // 2, lane), lambda: (0, 0, 0, 0)),
            pl.BlockSpec((1, lane, full), lambda: (0, 0, 0)),
        ],
        out_specs=pl.BlockSpec((3, lane, full), lambda: (0, 0, 0)),
        out_shape=jax.ShapeDtypeStruct((3, lane, full), jnp.float32),
        scratch_shapes=[pltpu.VMEM((lane, lane), jnp.float32)],
        compiler_params=pltpu.CompilerParams(vmem_limit_bytes=vmem_bytes),
        cost_estimate=pl.CostEstimate(flops=60 * lane * full, bytes_accessed=24 * lane * full, transcendentals=0),
        name="blend_factors",
    )(frequencies, own, other, bracket)


def finish_kernel(in_ref, blend_ref, turn_ref, table_ref, out_ref, image_ref, work_ref, wave_ref):
    count = len(ref_speeds)
    for j in range(count):
        values = jnp.concatenate([in_ref[:, j, 0], in_ref[:, j, 1]], axis=2)
        product = right_product(values.reshape(radix * row_block, 2 * lane), table_ref[...])
        work_ref[j] = product.reshape(radix, row_block, 2 * lane)

    def rows(index, carry):
        here = pl.ds(pl.multiple_of(index * 8, 8), 8)
        for j in range(count):
            parts = sixteen(
                [
                    times(
                        (work_ref[j, k, here, 0:lane], work_ref[j, k, here, lane : 2 * lane]),
                        (turn_ref[k, 0], turn_ref[k, 1]),
                    )
                    for k in range(radix)
                ],
                1,
            )
            for s in range(radix):
                wave_ref[j, 0, :, tile(s)] = parts[s][0]
                wave_ref[j, 1, :, tile(s)] = parts[s][1]
        for s in range(radix):
            place = blend_ref[0, here, tile(s)]
            weights_now = (
                jnp.maximum(1.0 - place, 0.0),
                1.0 - jnp.abs(place - 1.0),
                jnp.maximum(place - 1.0, 0.0),
            )
            mixed = [
                sum(weights_now[j] * wave_ref[j, part, :, tile(s)] for j in range(count)) for part in range(2)
            ]
            re, im = times(mixed, (blend_ref[1, here, tile(s)], blend_ref[2, here, tile(s)]))
            out_ref[0, 0, here, tile(s)] = re
            out_ref[0, 1, here, tile(s)] = im
            image_ref[0, here, tile(s)] = re
        return carry

    lax.fori_loop(0, row_block // 8, rows, 0)


def finish_call(returned, blend):
    count = len(ref_speeds)
    return pl.pallas_call(
        finish_kernel,
        grid=(blocks,),
        in_specs=[
            pl.BlockSpec((radix, count, 2, row_block, lane), lambda g: (0, 0, 0, g, 0)),
            pl.BlockSpec((3, row_block, full), lambda g: (0, g, 0)),
            pl.BlockSpec((radix, 2, 8, lane), lambda g: (0, 0, 0, 0)),
            pl.BlockSpec((6 * lane, 2 * lane), lambda g: (0, 0)),
        ],
        out_specs=[
            pl.BlockSpec((1, 2, row_block, full), lambda g: (0, 0, g, 0)),
            pl.BlockSpec((1, row_block, full), lambda g: (0, g, 0)),
        ],
        out_shape=[
            jax.ShapeDtypeStruct((1, 2, lane, full), jnp.float32),
            jax.ShapeDtypeStruct((1, lane, full), jnp.float32),
        ],
        scratch_shapes=[
            pltpu.VMEM((count, radix, row_block, 2 * lane), jnp.float32),
            pltpu.VMEM((count, 2, 8, full), jnp.float32),
        ],
        compiler_params=pltpu.CompilerParams(vmem_limit_bytes=vmem_bytes),
        name="inverse_lines",
    )(returned, blend, lane_twiddle(1, 1.0 / full), right_table(1))


def exchange(values):
    return lax.all_to_all(values, "slab", split_axis=0, concat_axis=0, tiled=True)


def per_device(wavefield, frequencies, velocity, bracket):
    sent = lines_call(wavefield, velocity)
    phase = phase_call(frequencies)
    arrived = exchange(sent)
    own = arrived[:, :, 2 * row_block :, :]
    other = lax.ppermute(own, "shot", [(0, 1), (1, 0)])
    returned = exchange(rows_call(arrived, phase))
    blend = blend_call(frequencies, own, other, bracket)
    propagated, image = finish_call(returned, blend)
    return propagated, image


def fits(mesh, shapes):
    wavefield, velocity = shapes
    return (
        mesh.shape["slab"] == radix
        and mesh.shape["shot"] == 2
        and wavefield == (2, 2, full, full)
        and velocity == (1, full, full)
    )


def solution(mesh):
    def program(wavefield, frequencies, velocity, bracket):
        small = fits(mesh, (wavefield.shape, velocity.shape))
        return jax.shard_map(
            per_device if small else per_device_general,
            mesh=mesh,
            in_specs=(
                P("shot", None, "slab", None),
                P("shot"),
                P(None, "slab", None),
                P(None, "slab", None),
            ),
            out_specs=(P("shot", None, "slab", None), P("shot", "slab", None)),
            check_vma=False,
        )(wavefield, frequencies, velocity, bracket)

    return program
```

```python
import math

import jax
import jax.numpy as jnp
import ml_dtypes
import numpy as np
from jax import lax
from jax.experimental import pallas as pl
from jax.experimental.pallas import tpu as pltpu
from jax.sharding import PartitionSpec as P

ref_speeds = (1.0, 1.5, 2.25)
step_length = 1.0
highest = lax.Precision.HIGHEST


def dft_table(height, breadth, modulus, direction):
    down_index = lax.iota(jnp.int32, height)[:, None]
    across_index = lax.iota(jnp.int32, breadth)[None, :]
    angles = (down_index * across_index % modulus).astype(jnp.float32) * (
        direction * 2.0 * math.pi / modulus
    )
    return (jnp.cos(angles), jnp.sin(angles))


def contract(pattern, left_pair, right_pair):

    def product(one_side, other_side):
        return jnp.einsum(pattern, one_side, other_side, precision=highest)

    return (
        product(left_pair[0], right_pair[0]) - product(left_pair[1], right_pair[1]),
        product(left_pair[0], right_pair[1]) + product(left_pair[1], right_pair[0]),
    )


def rotate(values, factor_pair):
    return (
        values[0] * factor_pair[0] - values[1] * factor_pair[1],
        values[0] * factor_pair[1] + values[1] * factor_pair[0],
    )


def forward_lines(fields):
    item_count, row_count, extent = fields[0].shape
    devices = lax.axis_size("slab")
    line_count = extent // devices
    reshaped = tuple(
        (part_now.reshape(item_count, row_count, line_count, devices) for part_now in fields)
    )
    section_one = contract(
        "nrab,ak->nrkb", reshaped, dft_table(line_count, line_count, line_count, -1.0)
    )
    twisted = rotate(
        section_one,
        tuple((turning[None, None] for turning in dft_table(line_count, devices, extent, -1.0))),
    )
    section_two = contract("nrkb,bq->nkqr", twisted, dft_table(devices, devices, devices, -1.0))
    return tuple(
        (part_now.reshape(item_count, line_count, devices * row_count) for part_now in section_two)
    )


def forward_rows(fields):
    item_count, line_count, extent = fields[0].shape
    devices = lax.axis_size("slab")
    row_count = extent // devices
    reshaped = tuple(
        (part_now.reshape(item_count, line_count, devices, row_count) for part_now in fields)
    )
    section_one = contract("ncab,ak->nckb", reshaped, dft_table(devices, devices, devices, -1.0))
    twisted = rotate(
        section_one,
        tuple((turning[None, None] for turning in dft_table(devices, row_count, extent, -1.0))),
    )
    section_two = contract(
        "nckb,bq->nckq", twisted, dft_table(row_count, row_count, row_count, -1.0)
    )
    return tuple((part_now.reshape(item_count, line_count, extent) for part_now in section_two))


def inverse_rows(fields):
    item_count, line_count, extent = fields[0].shape
    devices = lax.axis_size("slab")
    row_count = extent // devices
    reshaped = tuple(
        (part_now.reshape(item_count, line_count, devices, row_count) for part_now in fields)
    )
    section_one = contract(
        "nckq,bq->nckb", reshaped, dft_table(row_count, row_count, row_count, 1.0)
    )
    twisted = rotate(
        section_one,
        tuple((turning[None, None] for turning in dft_table(devices, row_count, extent, 1.0))),
    )
    section_two = contract("nckb,ak->ncab", twisted, dft_table(devices, devices, devices, 1.0))
    return tuple(
        (
            part_now.reshape(item_count, line_count, extent) * (1.0 / extent)
            for part_now in section_two
        )
    )


def inverse_lines(fields):
    item_count, line_count, extent = fields[0].shape
    devices = lax.axis_size("slab")
    row_count = extent // devices
    total_lines = line_count * devices
    reshaped = tuple(
        (part_now.reshape(item_count, line_count, devices, row_count) for part_now in fields)
    )
    section_one = contract("nkqr,bq->nkbr", reshaped, dft_table(devices, devices, devices, 1.0))
    twisted = rotate(
        section_one,
        tuple(
            (
                turning[None, :, :, None]
                for turning in dft_table(line_count, devices, total_lines, 1.0)
            )
        ),
    )
    section_two = contract(
        "nkbr,ak->nrab", twisted, dft_table(line_count, line_count, line_count, 1.0)
    )
    return tuple(
        (
            part_now.reshape(item_count, row_count, total_lines) * (1.0 / total_lines)
            for part_now in section_two
        )
    )


def phase_shift(values, wave_square, angular):
    slowness = 1.0 / jnp.array(ref_speeds, jnp.float32)
    wave_number = angular[:, None] * slowness[None, :]
    vertical = (wave_number * wave_number)[:, :, None, None] - wave_square[None, None]
    root_abs = jnp.sqrt(jnp.abs(vertical))
    real_part = jnp.where(
        vertical >= 0, jnp.cos(step_length * root_abs), jnp.exp(-step_length * root_abs)
    )
    imag_part = jnp.where(vertical >= 0, jnp.sin(step_length * root_abs), 0.0)
    shifted = rotate((values[0][:, None], values[1][:, None]), (real_part, imag_part))
    item_count = values[0].shape[0]
    return tuple(
        (
            part_now.reshape((item_count * len(ref_speeds),) + values[0].shape[1:])
            for part_now in shifted
        )
    )


def weights(speed_grid, chosen):
    speeds = jnp.array(ref_speeds, jnp.float32)
    lower_speed = jnp.zeros_like(speed_grid)
    upper_speed = jnp.zeros_like(speed_grid)
    for ref_index in range(len(ref_speeds) - 1):
        lower_speed = lower_speed + jnp.where(chosen == ref_index, speeds[ref_index], 0.0)
        upper_speed = upper_speed + jnp.where(chosen == ref_index, speeds[ref_index + 1], 0.0)
    fraction = (speed_grid - lower_speed) / (upper_speed - lower_speed)
    residual_phase = 1.0 / speed_grid - ((1.0 - fraction) / lower_speed + fraction / upper_speed)
    coefficients = []
    for ref_index in range(len(ref_speeds)):
        coefficients.append(
            jnp.where(chosen == ref_index, 1.0 - fraction, 0.0)
            + jnp.where(chosen == ref_index - 1, fraction, 0.0)
        )
    return (jnp.stack(coefficients), residual_phase)


def advance(fields, angular, coefficients, residual_phase, spec_square):
    item_count, row_count, extent = fields[0].shape
    prepared = forward_lines(fields)
    spectrum = forward_rows(
        (
            lax.all_to_all(prepared[0], "slab", split_axis=2, concat_axis=2, tiled=True),
            lax.all_to_all(prepared[1], "slab", split_axis=2, concat_axis=2, tiled=True),
        )
    )
    returned = inverse_rows(phase_shift(spectrum, spec_square, angular))
    waves = inverse_lines(
        (
            lax.all_to_all(returned[0], "slab", split_axis=2, concat_axis=2, tiled=True),
            lax.all_to_all(returned[1], "slab", split_axis=2, concat_axis=2, tiled=True),
        )
    )
    ref_count = len(ref_speeds)
    wave_real = waves[0].reshape(item_count, ref_count, row_count, extent)
    wave_imag = waves[1].reshape(item_count, ref_count, row_count, extent)
    blended_real = jnp.sum(coefficients[None] * wave_real, axis=1)
    blended_imag = jnp.sum(coefficients[None] * wave_imag, axis=1)
    angles = angular[:, None, None] * step_length * residual_phase[None]
    return rotate((blended_real, blended_imag), (jnp.cos(angles), jnp.sin(angles)))


def folded(indices, modulus):
    return jnp.minimum(indices, modulus - indices).astype(jnp.float32) * (2.0 * math.pi / modulus)


def per_device_general(wavefield, frequencies, velocity, bracket):
    devices = lax.axis_size("slab")
    device_index = lax.axis_index("slab")
    row_count = wavefield.shape[2]
    extent_y = wavefield.shape[3]
    extent_x = row_count * devices
    line_count = extent_y // devices
    speed_columns = lax.all_to_all(velocity, "slab", split_axis=2, concat_axis=1, tiled=True)
    speed_rows = jnp.transpose(speed_columns, (0, 2, 1))
    column = lax.iota(jnp.int32, extent_x)
    line_index = lax.iota(jnp.int32, line_count)
    spec_first = folded(column // row_count + devices * (column % row_count), extent_x)
    spec_second = folded(device_index * line_count + line_index, extent_y)
    spec_square = (
        spec_first[None, :] * spec_first[None, :] + spec_second[:, None] * spec_second[:, None]
    )
    current = (wavefield[:, 0], wavefield[:, 1])
    coefficients, residual_phase = weights(speed_rows[0], bracket[0])
    single = (current[0], current[1])
    pieces = [advance(single, frequencies, coefficients, residual_phase, spec_square)]
    current = (
        jnp.concatenate([piece[0] for piece in pieces], axis=0),
        jnp.concatenate([piece[1] for piece in pieces], axis=0),
    )
    image_rows = [jnp.sum(current[0], axis=0)]
    return (jnp.stack(current, axis=1), jnp.stack(image_rows))


radix = 16
lane = 128
full = radix * lane
row_block = 64
blocks = lane // row_block
piece = 2 * row_block
vmem_bytes = 56 * 1024 * 1024
rows_vmem_bytes = 50 * 1024 * 1024
phase_vmem_bytes = 56 * 1024 * 1024


def split_table(table):
    upper = table.astype(ml_dtypes.bfloat16)
    lower = (table - upper.astype(np.float64)).astype(ml_dtypes.bfloat16)
    return upper, lower


def line_matrices(direction):
    angles = 2.0 * np.pi / lane * (np.outer(np.arange(lane), np.arange(lane)) % lane)
    cosine, sine = np.cos(angles), direction * np.sin(angles)
    return np.block([[cosine, sine], [-sine, cosine]])


def right_table(direction):
    upper, lower = split_table(line_matrices(direction))
    return np.concatenate([upper, upper, lower], axis=0)


def twiddle(direction, scale):
    angles = 2.0 * np.pi / full * np.outer(np.arange(radix), np.arange(lane))
    return np.stack([np.cos(angles), direction * np.sin(angles)], axis=1) * scale


def lane_twiddle(direction, scale):
    table = twiddle(direction, scale)[:, :, None, :]
    return np.ascontiguousarray(np.broadcast_to(table, (radix, 2, 8, lane))).astype(np.float32)


def root_series(offset, degree, end):
    nodes = np.polynomial.chebyshev.Chebyshev.interpolate(
        lambda q: np.sinc(np.sqrt(q) / np.pi) if offset else np.cos(np.sqrt(q)), degree, domain=[0.0, end]
    )
    return [float(value) for value in nodes.convert(kind=np.polynomial.Polynomial).coef]


cos_series, sinc_series = root_series(0, 7, 9.0), root_series(1, 6, 9.0)
circle_cos, circle_sin = root_series(0, 8, np.pi**2), root_series(1, 7, np.pi**2)


def horner(series, argument):
    total = jnp.full_like(argument, series[-1])
    for value in series[-2::-1]:
        total = total * argument + value
    return total


def times(left, right):
    return left[0] * right[0] - left[1] * right[1], left[0] * right[1] + left[1] * right[0]


def conjugate_times(left, right):
    return left[0] * right[0] + left[1] * right[1], left[1] * right[0] - left[0] * right[1]


def quarter(values, direction):
    (a_re, a_im), (b_re, b_im), (c_re, c_im), (d_re, d_im) = values
    p_re, p_im, m_re, m_im = a_re + c_re, a_im + c_im, a_re - c_re, a_im - c_im
    q_re, q_im, n_re, n_im = b_re + d_re, b_im + d_im, b_re - d_re, b_im - d_im
    if direction < 0:
        turn_re, turn_im = n_im, -n_re
    else:
        turn_re, turn_im = -n_im, n_re
    return [
        (p_re + q_re, p_im + q_im),
        (m_re + turn_re, m_im + turn_im),
        (p_re - q_re, p_im - q_im),
        (m_re - turn_re, m_im - turn_im),
    ]


def turned(value, power, direction):
    re, im = value
    power %= 16
    if power == 0:
        return value
    if power == 4:
        return (-direction * im, direction * re) if direction < 0 else (-im, re)
    half = math.sqrt(0.5)
    if power == 2:
        return ((re - direction * im) * half, (im + direction * re) * half)
    if power == 6:
        return ((-re - direction * im) * half, (direction * re - im) * half)
    cosine, sine = math.cos(math.pi * power / 8), direction * math.sin(math.pi * power / 8)
    return re * cosine - im * sine, re * sine + im * cosine


def sixteen(values, direction):
    first = [quarter([values[4 * a + b] for a in range(4)], direction) for b in range(4)]
    result = [None] * 16
    for c in range(4):
        outs = quarter([turned(first[b][c], b * c, direction) for b in range(4)], direction)
        for d in range(4):
            result[c + 4 * d] = outs[d]
    return result


def halves(values):
    upper = values.astype(jnp.bfloat16)
    lower = (values - upper.astype(jnp.float32)).astype(jnp.bfloat16)
    return upper, lower


def right_product(values, table):
    upper, lower = halves(values)
    return jnp.dot(jnp.concatenate([upper, lower, upper], axis=1), table, preferred_element_type=jnp.float32)


def left_product(table, values):
    upper, lower = halves(values)
    return jnp.dot(table, jnp.concatenate([upper, lower, upper], axis=0), preferred_element_type=jnp.float32)


def tile(index):
    return slice(index * lane, (index + 1) * lane)


def lines_kernel(field_ref, turn_ref, table_ref, out_ref, work_ref):
    def rows(index, carry):
        here = pl.ds(pl.multiple_of(index * 8, 8), 8)
        parts = sixteen(
            [(field_ref[0, 0, here, tile(j)], field_ref[0, 1, here, tile(j)]) for j in range(radix)], -1
        )
        for k in range(radix):
            re, im = times(parts[k], (turn_ref[k, 0], turn_ref[k, 1]))
            work_ref[k, here, 0:lane] = re
            work_ref[k, here, lane : 2 * lane] = im
        return carry

    lax.fori_loop(0, row_block // 8, rows, 0, unroll=True)
    lines = right_product(work_ref[...].reshape(radix * row_block, 2 * lane), table_ref[...])
    for k in range(radix):
        block = lines[k * row_block : (k + 1) * row_block]
        out_ref[k, 0, 0:row_block] = block[:, 0:lane]
        out_ref[k, 0, row_block : 2 * row_block] = block[:, lane : 2 * lane]


def lines_call(wavefield):
    return pl.pallas_call(
        lines_kernel,
        grid=(blocks,),
        in_specs=[
            pl.BlockSpec((1, 2, row_block, full), lambda g: (0, 0, g, 0)),
            pl.BlockSpec((radix, 2, 8, lane), lambda g: (0, 0, 0, 0)),
            pl.BlockSpec((6 * lane, 2 * lane), lambda g: (0, 0)),
        ],
        out_specs=pl.BlockSpec((radix, 1, piece, lane), lambda g: (0, g, 0, 0)),
        out_shape=jax.ShapeDtypeStruct((radix, blocks, piece, lane), jnp.float32),
        scratch_shapes=[pltpu.VMEM((radix, row_block, 2 * lane), jnp.float32)],
        compiler_params=pltpu.CompilerParams(vmem_limit_bytes=vmem_bytes),
        name="forward_lines",
    )(wavefield, lane_twiddle(-1, 1.0), right_table(-1))


def phase_kernel(angular_ref, out_ref):
    device = lax.axis_index("slab")
    scale = 2.0 * math.pi / full
    column = lax.broadcasted_iota(jnp.int32, (32, lane), 1) * radix + device
    second = jnp.minimum(column, full - column).astype(jnp.float32) * scale
    second = second * second
    row = lax.broadcasted_iota(jnp.int32, (32, lane), 0)
    squares = []
    for speed in ref_speeds:
        number = angular_ref[0] * np.float32(1.0 / np.float32(speed))
        squares.append(number * number)

    def chunk(index, carry):
        k = index // 4
        begin = pl.multiple_of((index % 4) * 32, 32)
        here = pl.ds(begin, 32)
        there = pl.ds(pl.multiple_of(k * lane, lane), lane)
        position = (row + begin) * radix + k
        first = jnp.minimum(position, full - position).astype(jnp.float32) * scale
        wave_square = first * first + second
        for j in range(len(ref_speeds)):
            vertical = squares[j] - wave_square
            root = jnp.sqrt(jnp.abs(vertical))
            moving = vertical >= 0.0
            out_ref[j, 0, here, there] = jnp.where(moving, horner(cos_series, vertical), jnp.exp(-root))
            out_ref[j, 1, here, there] = jnp.where(moving, root * horner(sinc_series, vertical), 0.0)
        return carry

    lax.fori_loop(0, radix * 4, chunk, 0)


def phase_call(frequencies):
    count = len(ref_speeds)
    return pl.pallas_call(
        phase_kernel,
        in_specs=[pl.BlockSpec(memory_space=pltpu.SMEM)],
        out_specs=pl.BlockSpec(memory_space=pltpu.VMEM),
        out_shape=jax.ShapeDtypeStruct((count, 2, lane, full), jnp.float32),
        compiler_params=pltpu.CompilerParams(vmem_limit_bytes=phase_vmem_bytes),
        cost_estimate=pl.CostEstimate(flops=60 * count * lane * full, bytes_accessed=8 * count * lane * full, transcendentals=0),
        name="phase_factors",
    )(frequencies)


def circle(index, modulus):
    half = modulus // 2
    angle = (((index + half) & (modulus - 1)) - half).astype(jnp.float32) * (2.0 * math.pi / modulus)
    square = angle * angle
    return horner(circle_cos, square), angle * horner(circle_sin, square)


def build_matrices(ahead_table_ref, back_table_ref):
    row = lax.broadcasted_iota(jnp.int32, (lane, lane), 0)
    column = lax.broadcasted_iota(jnp.int32, (lane, lane), 1)
    cosine, sine = circle(row * column, lane)
    for table_ref, direction, scale in ((ahead_table_ref, -1.0, 1.0), (back_table_ref, 1.0, 1.0 / full)):
        cos_now, sin_now = cosine * scale, sine * (direction * scale)
        for top, blocks_now in enumerate(((cos_now, -sin_now), (sin_now, cos_now))):
            here = slice(top * lane, (top + 1) * lane)
            for place, values in enumerate(blocks_now):
                upper, lower = halves(values)
                for third, part in enumerate((upper, upper, lower)):
                    table_ref[here, tile(2 * third + place)] = part


def rows_kernel(
    in_ref, phase_ref, out_ref,
    work_ref, spec_ref, turn_ref, column_ref, ahead_table_ref, back_table_ref,
    factor_ref, field_ref, factor_sem, field_sem,
):
    count = len(ref_speeds)

    def factor_copy(j):
        return pltpu.make_async_copy(phase_ref.at[j], factor_ref.at[j], factor_sem.at[j])

    def field_copy(j):
        return pltpu.make_async_copy(field_ref.at[j % 2], out_ref.at[:, j], field_sem.at[j % 2])

    for j in range(count):
        factor_copy(j).start()

    row = lax.broadcasted_iota(jnp.int32, (lane, lane), 0)
    power = lax.broadcasted_iota(jnp.int32, (lane, lane), 1) & (radix - 1)
    cosine, sine = circle(row * power, full)
    column_ref[0] = cosine
    column_ref[1] = -sine
    build_matrices(ahead_table_ref, back_table_ref)

    def rows(index, carry):
        group = index // (row_block // 8)
        local = pl.multiple_of((index % (row_block // 8)) * 8, 8)
        here = pl.ds(pl.multiple_of(index * 8, 8), 8)
        there = pl.ds(pl.multiple_of(index * 8 + lane, 8), 8)
        columns = (column_ref[0, here, :], column_ref[1, here, :])
        parts = sixteen(
            [
                (in_ref[s, group, pl.ds(local, 8), :], in_ref[s, group, pl.ds(local + row_block, 8), :])
                for s in range(radix)
            ],
            -1,
        )
        for k in range(radix):
            turn = tuple(jnp.broadcast_to(part[:, k : k + 1], (8, lane)) for part in columns)
            turn_ref[k, 0, here, :] = turn[0]
            turn_ref[k, 1, here, :] = turn[1]
            re, im = times(parts[k], turn)
            work_ref[0, here, tile(k)] = re
            work_ref[0, there, tile(k)] = im
        return carry

    lax.fori_loop(0, lane // 8, rows, 0, unroll=2)

    def shifted(j, columns, spectrum):
        re, im = times(
            (spectrum[0:lane], spectrum[lane : 2 * lane]),
            (factor_ref[j, 0, :, columns], factor_ref[j, 1, :, columns]),
        )
        work_ref[(j + 1) % 2, :, columns] = left_product(back_table_ref[...], jnp.concatenate([re, im], axis=0))

    def back(j, index):
        here = pl.ds(pl.multiple_of(index * 8, 8), 8)
        there = pl.ds(pl.multiple_of(index * 8 + lane, 8), 8)
        parts = sixteen(
            [
                conjugate_times(
                    (work_ref[(j + 1) % 2, here, tile(k)], work_ref[(j + 1) % 2, there, tile(k)]),
                    (turn_ref[k, 0, here, :], turn_ref[k, 1, here, :]),
                )
                for k in range(radix)
            ],
            1,
        )
        for s in range(radix):
            field_ref[j % 2, s, 0, here, :] = parts[s][0]
            field_ref[j % 2, s, 1, here, :] = parts[s][1]

    def pair_columns(index):
        return pl.ds(pl.multiple_of(index * 2 * lane, 2 * lane), 2 * lane)

    factor_copy(0).wait()

    def first(index, carry):
        columns = pair_columns(index)
        spectrum = left_product(ahead_table_ref[...], work_ref[0, :, columns])
        spec_ref[:, columns] = spectrum
        shifted(0, columns, spectrum)
        return carry

    lax.fori_loop(0, radix // 2, first, 0, unroll=True)

    for j in range(count):
        if j + 1 < count:
            factor_copy(j + 1).wait()
        if j >= 2:
            field_copy(j - 2).wait()

        def both(index, carry):
            if j + 1 < count:
                columns = pair_columns(index)
                shifted(j + 1, columns, spec_ref[:, columns])
            back(j, 2 * index)
            back(j, 2 * index + 1)
            return carry

        lax.fori_loop(0, radix // 2, both, 0, unroll=True)
        field_copy(j).start()

    for j in range(count - 2, count):
        field_copy(j).wait()


def rows_call(arrived, phase):
    count = len(ref_speeds)
    in_vmem = pl.BlockSpec(memory_space=pltpu.VMEM)
    in_hbm = pl.BlockSpec(memory_space=pltpu.HBM)
    return pl.pallas_call(
        rows_kernel,
        in_specs=[in_vmem, in_hbm],
        out_specs=in_hbm,
        out_shape=jax.ShapeDtypeStruct((radix, count, 2, lane, lane), jnp.float32),
        scratch_shapes=[
            pltpu.VMEM((2, 2 * lane, full), jnp.float32),
            pltpu.VMEM((2 * lane, full), jnp.float32),
            pltpu.VMEM((radix, 2, lane, lane), jnp.float32),
            pltpu.VMEM((2, lane, lane), jnp.float32),
            pltpu.VMEM((2 * lane, 6 * lane), jnp.bfloat16),
            pltpu.VMEM((2 * lane, 6 * lane), jnp.bfloat16),
            pltpu.VMEM((count, 2, lane, full), jnp.float32),
            pltpu.VMEM((2, radix, 2, lane, lane), jnp.float32),
            pltpu.SemaphoreType.DMA((count,)),
            pltpu.SemaphoreType.DMA((2,)),
        ],
        compiler_params=pltpu.CompilerParams(vmem_limit_bytes=rows_vmem_bytes),
        name="rows_there_and_back",
    )(arrived, phase)


def blend_kernel(angular_ref, bracket_ref, *refs):
    speed_refs, out_ref = refs[:-1], refs[-1]
    device = lax.axis_index("slab")
    for k, speed_ref in enumerate(speed_refs):
        for side in range(2):
            source = device ^ (k + side * (radix // 2))
            there = pl.ds(pl.multiple_of(source * lane, lane), lane)
            speed = jnp.transpose(speed_ref[side])
            first = bracket_ref[0, :, there] == 0
            low = jnp.where(first, ref_speeds[0], ref_speeds[1])
            width = jnp.where(first, 1.0 / (ref_speeds[1] - ref_speeds[0]), 1.0 / (ref_speeds[2] - ref_speeds[1]))
            fraction = (speed - low) * width
            low_slowness = jnp.where(first, 1.0 / ref_speeds[0], 1.0 / ref_speeds[1])
            high_slowness = jnp.where(first, 1.0 / ref_speeds[1], 1.0 / ref_speeds[2])
            residual = 1.0 / speed - ((1.0 - fraction) * low_slowness + fraction * high_slowness)
            angle = angular_ref[0] * step_length * residual
            square = angle * angle
            cosine = horner([1.0, -1 / 2, 1 / 24, -1 / 720, 1 / 40320], square)
            sine = angle * horner([1.0, -1 / 6, 1 / 120, -1 / 5040, 1 / 362880], square)
            out_ref[0, :, there] = fraction + jnp.where(first, 0.0, 1.0)
            out_ref[1, :, there] = cosine
            out_ref[2, :, there] = sine


def blend_call(frequencies, bracket, speeds):
    return pl.pallas_call(
        blend_kernel,
        in_specs=[
            pl.BlockSpec(memory_space=pltpu.SMEM),
            pl.BlockSpec((1, lane, full), lambda: (0, 0, 0)),
        ]
        + [pl.BlockSpec((2, lane, lane), lambda: (0, 0, 0))] * len(speeds),
        out_specs=pl.BlockSpec((3, lane, full), lambda: (0, 0, 0)),
        out_shape=jax.ShapeDtypeStruct((3, lane, full), jnp.float32),
        compiler_params=pltpu.CompilerParams(vmem_limit_bytes=vmem_bytes),
        cost_estimate=pl.CostEstimate(flops=60 * lane * full, bytes_accessed=24 * lane * full, transcendentals=0),
        name="blend_factors",
    )(frequencies, bracket, *speeds)


strip = 32


def finish_kernel(in_ref, blend_ref, turn_ref, table_ref, out_ref, image_ref, work_ref):
    count = len(ref_speeds)
    for j in range(count):
        values = jnp.concatenate([in_ref[:, j, 0], in_ref[:, j, 1]], axis=2)
        product = right_product(values.reshape(radix * strip, 2 * lane), table_ref[...])
        work_ref[j] = product.reshape(radix, strip, 2 * lane)

    def rows(index, carry):
        here = pl.ds(pl.multiple_of(index * 8, 8), 8)
        for j in range(count):
            parts = sixteen(
                [
                    times(
                        (work_ref[j, k, here, 0:lane], work_ref[j, k, here, lane : 2 * lane]),
                        (turn_ref[k, 0], turn_ref[k, 1]),
                    )
                    for k in range(radix)
                ],
                1,
            )
            for s in range(radix):
                place = blend_ref[0, here, tile(s)]
                if j == 0:
                    weight = jnp.maximum(1.0 - place, 0.0)
                elif j == 1:
                    weight = 1.0 - jnp.abs(place - 1.0)
                else:
                    weight = jnp.maximum(place - 1.0, 0.0)
                re, im = parts[s][0] * weight, parts[s][1] * weight
                if j > 0:
                    re, im = re + out_ref[0, 0, here, tile(s)], im + out_ref[0, 1, here, tile(s)]
                if j == count - 1:
                    re, im = times((re, im), (blend_ref[1, here, tile(s)], blend_ref[2, here, tile(s)]))
                    image_ref[0, here, tile(s)] = re
                out_ref[0, 0, here, tile(s)] = re
                out_ref[0, 1, here, tile(s)] = im
        return carry

    lax.fori_loop(0, strip // 8, rows, 0, unroll=True)


def finish_call(returned, blend):
    count = len(ref_speeds)
    return pl.pallas_call(
        finish_kernel,
        grid=(lane // strip,),
        in_specs=[
            pl.BlockSpec((radix, count, 2, strip, lane), lambda g: (0, 0, 0, g, 0)),
            pl.BlockSpec((3, strip, full), lambda g: (0, g, 0)),
            pl.BlockSpec((radix, 2, 8, lane), lambda g: (0, 0, 0, 0)),
            pl.BlockSpec((6 * lane, 2 * lane), lambda g: (0, 0)),
        ],
        out_specs=[
            pl.BlockSpec((1, 2, strip, full), lambda g: (0, 0, g, 0)),
            pl.BlockSpec((1, strip, full), lambda g: (0, g, 0)),
        ],
        out_shape=[
            jax.ShapeDtypeStruct((1, 2, lane, full), jnp.float32),
            jax.ShapeDtypeStruct((1, lane, full), jnp.float32),
        ],
        scratch_shapes=[
            pltpu.VMEM((count, radix, strip, 2 * lane), jnp.float32),
        ],
        compiler_params=pltpu.CompilerParams(vmem_limit_bytes=vmem_bytes),
        name="inverse_lines",
    )(returned, blend, lane_twiddle(1, 1.0 / full), right_table(1))


def exchange(values):
    return lax.all_to_all(values, "slab", split_axis=0, concat_axis=0, tiled=True)


def partners(distance):
    return [(index, index ^ distance) for index in range(radix)]


def speeds_there(velocity):
    shot, device = lax.axis_index("shot"), lax.axis_index("slab")
    half = radix // 2
    other_half = (1 - device // half) * (half * lane)
    sent = lax.dynamic_slice(velocity[0], (shot * (lane // 2), other_half), (lane // 2, half * lane))
    return sent


def speeds_here(velocity, arrived):
    shot, device = lax.axis_index("shot"), lax.axis_index("slab")
    half = radix // 2
    place = device % half
    swapped = lax.ppermute(arrived, "shot", [(0, 1), (1, 0)])
    far = jnp.where(shot == 0, jnp.concatenate([arrived, swapped]), jnp.concatenate([swapped, arrived]))
    near = lax.dynamic_slice(velocity[0], (0, device // half * (half * lane)), (lane, half * lane))
    both = jnp.stack([near, far])
    tiles = []
    for k in range(half):
        part = lax.dynamic_slice(both, (0, 0, (place ^ k) * lane), (2, lane, lane))
        tiles.append(lax.ppermute(part, "slab", partners(k)) if k else part)
    return tiles


def per_device(wavefield, frequencies, velocity, bracket):
    sent = lines_call(wavefield)
    phase = phase_call(frequencies)
    arrived = exchange(sent)
    speed_sent, _, _ = lax.optimization_barrier((speeds_there(velocity), phase, arrived))
    speed_arrived = lax.ppermute(speed_sent, "slab", partners(radix // 2))
    fields = rows_call(arrived, phase)
    speed_arrived, fields = lax.optimization_barrier((speed_arrived, fields))
    returned = exchange(fields)
    blend = blend_call(frequencies, bracket, speeds_here(velocity, speed_arrived))
    propagated, image = finish_call(returned, blend)
    return propagated, image


def fits(mesh, shapes):
    wavefield, velocity = shapes
    return (
        mesh.shape["slab"] == radix
        and mesh.shape["shot"] == 2
        and wavefield == (2, 2, full, full)
        and velocity == (1, full, full)
    )


def solution(mesh):
    def program(wavefield, frequencies, velocity, bracket):
        small = fits(mesh, (wavefield.shape, velocity.shape))
        return jax.shard_map(
            per_device if small else per_device_general,
            mesh=mesh,
            in_specs=(
                P("shot", None, "slab", None),
                P("shot"),
                P(None, "slab", None),
                P(None, "slab", None),
            ),
            out_specs=(P("shot", None, "slab", None), P("shot", "slab", None)),
            check_vma=False,
        )(wavefield, frequencies, velocity, bracket)

    return program
```

```python
import functools
import math

import jax
import jax.numpy as jnp
import ml_dtypes
import numpy as np
from jax import lax
from jax.experimental import pallas as pl
from jax.experimental.pallas import tpu as pltpu
from jax.sharding import PartitionSpec as P

ref_speeds = (1.0, 1.5, 2.25)
step_length = 1.0
highest = lax.Precision.HIGHEST


def dft_table(height, breadth, modulus, direction):
    down_index = lax.iota(jnp.int32, height)[:, None]
    across_index = lax.iota(jnp.int32, breadth)[None, :]
    angles = (down_index * across_index % modulus).astype(jnp.float32) * (
        direction * 2.0 * math.pi / modulus
    )
    return (jnp.cos(angles), jnp.sin(angles))


def contract(pattern, left_pair, right_pair):

    def product(one_side, other_side):
        return jnp.einsum(pattern, one_side, other_side, precision=highest)

    return (
        product(left_pair[0], right_pair[0]) - product(left_pair[1], right_pair[1]),
        product(left_pair[0], right_pair[1]) + product(left_pair[1], right_pair[0]),
    )


def rotate(values, factor_pair):
    return (
        values[0] * factor_pair[0] - values[1] * factor_pair[1],
        values[0] * factor_pair[1] + values[1] * factor_pair[0],
    )


def forward_lines(fields):
    item_count, row_count, extent = fields[0].shape
    devices = lax.axis_size("slab")
    line_count = extent // devices
    reshaped = tuple(
        (part_now.reshape(item_count, row_count, line_count, devices) for part_now in fields)
    )
    section_one = contract(
        "nrab,ak->nrkb", reshaped, dft_table(line_count, line_count, line_count, -1.0)
    )
    twisted = rotate(
        section_one,
        tuple((turning[None, None] for turning in dft_table(line_count, devices, extent, -1.0))),
    )
    section_two = contract("nrkb,bq->nkqr", twisted, dft_table(devices, devices, devices, -1.0))
    return tuple(
        (part_now.reshape(item_count, line_count, devices * row_count) for part_now in section_two)
    )


def forward_rows(fields):
    item_count, line_count, extent = fields[0].shape
    devices = lax.axis_size("slab")
    row_count = extent // devices
    reshaped = tuple(
        (part_now.reshape(item_count, line_count, devices, row_count) for part_now in fields)
    )
    section_one = contract("ncab,ak->nckb", reshaped, dft_table(devices, devices, devices, -1.0))
    twisted = rotate(
        section_one,
        tuple((turning[None, None] for turning in dft_table(devices, row_count, extent, -1.0))),
    )
    section_two = contract(
        "nckb,bq->nckq", twisted, dft_table(row_count, row_count, row_count, -1.0)
    )
    return tuple((part_now.reshape(item_count, line_count, extent) for part_now in section_two))


def inverse_rows(fields):
    item_count, line_count, extent = fields[0].shape
    devices = lax.axis_size("slab")
    row_count = extent // devices
    reshaped = tuple(
        (part_now.reshape(item_count, line_count, devices, row_count) for part_now in fields)
    )
    section_one = contract(
        "nckq,bq->nckb", reshaped, dft_table(row_count, row_count, row_count, 1.0)
    )
    twisted = rotate(
        section_one,
        tuple((turning[None, None] for turning in dft_table(devices, row_count, extent, 1.0))),
    )
    section_two = contract("nckb,ak->ncab", twisted, dft_table(devices, devices, devices, 1.0))
    return tuple(
        (
            part_now.reshape(item_count, line_count, extent) * (1.0 / extent)
            for part_now in section_two
        )
    )


def inverse_lines(fields):
    item_count, line_count, extent = fields[0].shape
    devices = lax.axis_size("slab")
    row_count = extent // devices
    total_lines = line_count * devices
    reshaped = tuple(
        (part_now.reshape(item_count, line_count, devices, row_count) for part_now in fields)
    )
    section_one = contract("nkqr,bq->nkbr", reshaped, dft_table(devices, devices, devices, 1.0))
    twisted = rotate(
        section_one,
        tuple(
            (
                turning[None, :, :, None]
                for turning in dft_table(line_count, devices, total_lines, 1.0)
            )
        ),
    )
    section_two = contract(
        "nkbr,ak->nrab", twisted, dft_table(line_count, line_count, line_count, 1.0)
    )
    return tuple(
        (
            part_now.reshape(item_count, row_count, total_lines) * (1.0 / total_lines)
            for part_now in section_two
        )
    )


def phase_shift(values, wave_square, angular):
    slowness = 1.0 / jnp.array(ref_speeds, jnp.float32)
    wave_number = angular[:, None] * slowness[None, :]
    vertical = (wave_number * wave_number)[:, :, None, None] - wave_square[None, None]
    root_abs = jnp.sqrt(jnp.abs(vertical))
    real_part = jnp.where(
        vertical >= 0, jnp.cos(step_length * root_abs), jnp.exp(-step_length * root_abs)
    )
    imag_part = jnp.where(vertical >= 0, jnp.sin(step_length * root_abs), 0.0)
    shifted = rotate((values[0][:, None], values[1][:, None]), (real_part, imag_part))
    item_count = values[0].shape[0]
    return tuple(
        (
            part_now.reshape((item_count * len(ref_speeds),) + values[0].shape[1:])
            for part_now in shifted
        )
    )


def weights(speed_grid, chosen):
    speeds = jnp.array(ref_speeds, jnp.float32)
    lower_speed = jnp.zeros_like(speed_grid)
    upper_speed = jnp.zeros_like(speed_grid)
    for ref_index in range(len(ref_speeds) - 1):
        lower_speed = lower_speed + jnp.where(chosen == ref_index, speeds[ref_index], 0.0)
        upper_speed = upper_speed + jnp.where(chosen == ref_index, speeds[ref_index + 1], 0.0)
    fraction = (speed_grid - lower_speed) / (upper_speed - lower_speed)
    residual_phase = 1.0 / speed_grid - ((1.0 - fraction) / lower_speed + fraction / upper_speed)
    coefficients = []
    for ref_index in range(len(ref_speeds)):
        coefficients.append(
            jnp.where(chosen == ref_index, 1.0 - fraction, 0.0)
            + jnp.where(chosen == ref_index - 1, fraction, 0.0)
        )
    return (jnp.stack(coefficients), residual_phase)


def advance(fields, angular, coefficients, residual_phase, spec_square):
    item_count, row_count, extent = fields[0].shape
    prepared = forward_lines(fields)
    spectrum = forward_rows(
        (
            lax.all_to_all(prepared[0], "slab", split_axis=2, concat_axis=2, tiled=True),
            lax.all_to_all(prepared[1], "slab", split_axis=2, concat_axis=2, tiled=True),
        )
    )
    returned = inverse_rows(phase_shift(spectrum, spec_square, angular))
    waves = inverse_lines(
        (
            lax.all_to_all(returned[0], "slab", split_axis=2, concat_axis=2, tiled=True),
            lax.all_to_all(returned[1], "slab", split_axis=2, concat_axis=2, tiled=True),
        )
    )
    ref_count = len(ref_speeds)
    wave_real = waves[0].reshape(item_count, ref_count, row_count, extent)
    wave_imag = waves[1].reshape(item_count, ref_count, row_count, extent)
    blended_real = jnp.sum(coefficients[None] * wave_real, axis=1)
    blended_imag = jnp.sum(coefficients[None] * wave_imag, axis=1)
    angles = angular[:, None, None] * step_length * residual_phase[None]
    return rotate((blended_real, blended_imag), (jnp.cos(angles), jnp.sin(angles)))


def folded(indices, modulus):
    return jnp.minimum(indices, modulus - indices).astype(jnp.float32) * (2.0 * math.pi / modulus)


def per_device_general(wavefield, frequencies, velocity, bracket):
    devices = lax.axis_size("slab")
    device_index = lax.axis_index("slab")
    row_count = wavefield.shape[2]
    extent_y = wavefield.shape[3]
    extent_x = row_count * devices
    line_count = extent_y // devices
    speed_columns = lax.all_to_all(velocity, "slab", split_axis=2, concat_axis=1, tiled=True)
    speed_rows = jnp.transpose(speed_columns, (0, 2, 1))
    column = lax.iota(jnp.int32, extent_x)
    line_index = lax.iota(jnp.int32, line_count)
    spec_first = folded(column // row_count + devices * (column % row_count), extent_x)
    spec_second = folded(device_index * line_count + line_index, extent_y)
    spec_square = (
        spec_first[None, :] * spec_first[None, :] + spec_second[:, None] * spec_second[:, None]
    )
    current = (wavefield[:, 0], wavefield[:, 1])
    coefficients, residual_phase = weights(speed_rows[0], bracket[0])
    single = (current[0], current[1])
    pieces = [advance(single, frequencies, coefficients, residual_phase, spec_square)]
    current = (
        jnp.concatenate([piece[0] for piece in pieces], axis=0),
        jnp.concatenate([piece[1] for piece in pieces], axis=0),
    )
    image_rows = [jnp.sum(current[0], axis=0)]
    return (jnp.stack(current, axis=1), jnp.stack(image_rows))


radix = 16
lane = 128
full = radix * lane
row_block = 64
half_radix = radix // 2
far = radix // 2 + radix // 4
blocks = lane // row_block
piece = 2 * row_block
vmem_bytes = 56 * 1024 * 1024
rows_vmem_bytes = 50 * 1024 * 1024
phase_vmem_bytes = 56 * 1024 * 1024
finish_vmem_bytes = 48 * 1024 * 1024


def split_table(table):
    upper = table.astype(ml_dtypes.bfloat16)
    lower = (table - upper.astype(np.float64)).astype(ml_dtypes.bfloat16)
    return upper, lower


def line_matrices(direction):
    angles = 2.0 * np.pi / lane * (np.outer(np.arange(lane), np.arange(lane)) % lane)
    cosine, sine = np.cos(angles), direction * np.sin(angles)
    return np.block([[cosine, sine], [-sine, cosine]])


def right_table(direction):
    upper, lower = split_table(line_matrices(direction))
    return np.concatenate([upper, upper, lower], axis=0)


def twiddle(direction, scale):
    angles = 2.0 * np.pi / full * np.outer(np.arange(radix), np.arange(lane))
    return np.stack([np.cos(angles), direction * np.sin(angles)], axis=1) * scale


def lane_twiddle(direction, scale):
    table = twiddle(direction, scale)[:, :, None, :]
    return np.ascontiguousarray(np.broadcast_to(table, (radix, 2, 8, lane))).astype(np.float32)


def root_series(offset, degree, end):
    nodes = np.polynomial.chebyshev.Chebyshev.interpolate(
        lambda q: np.sinc(np.sqrt(q) / np.pi) if offset else np.cos(np.sqrt(q)), degree, domain=[0.0, end]
    )
    return [float(value) for value in nodes.convert(kind=np.polynomial.Polynomial).coef]


cos_series, sinc_series = root_series(0, 7, 9.0), root_series(1, 6, 9.0)
circle_cos, circle_sin = root_series(0, 8, np.pi**2), root_series(1, 7, np.pi**2)


def horner(series, argument):
    total = jnp.full_like(argument, series[-1])
    for value in series[-2::-1]:
        total = total * argument + value
    return total


def times(left, right):
    return left[0] * right[0] - left[1] * right[1], left[0] * right[1] + left[1] * right[0]


def conjugate_times(left, right):
    return left[0] * right[0] + left[1] * right[1], left[1] * right[0] - left[0] * right[1]


def quarter(values, direction):
    (a_re, a_im), (b_re, b_im), (c_re, c_im), (d_re, d_im) = values
    p_re, p_im, m_re, m_im = a_re + c_re, a_im + c_im, a_re - c_re, a_im - c_im
    q_re, q_im, n_re, n_im = b_re + d_re, b_im + d_im, b_re - d_re, b_im - d_im
    if direction < 0:
        turn_re, turn_im = n_im, -n_re
    else:
        turn_re, turn_im = -n_im, n_re
    return [
        (p_re + q_re, p_im + q_im),
        (m_re + turn_re, m_im + turn_im),
        (p_re - q_re, p_im - q_im),
        (m_re - turn_re, m_im - turn_im),
    ]


def turned(value, power, direction):
    re, im = value
    power %= 16
    if power == 0:
        return value
    if power == 4:
        return (-direction * im, direction * re) if direction < 0 else (-im, re)
    half = math.sqrt(0.5)
    if power == 2:
        return ((re - direction * im) * half, (im + direction * re) * half)
    if power == 6:
        return ((-re - direction * im) * half, (direction * re - im) * half)
    cosine, sine = math.cos(math.pi * power / 8), direction * math.sin(math.pi * power / 8)
    return re * cosine - im * sine, re * sine + im * cosine


def sixteen(values, direction):
    first = [quarter([values[4 * a + b] for a in range(4)], direction) for b in range(4)]
    result = [None] * 16
    for c in range(4):
        outs = quarter([turned(first[b][c], b * c, direction) for b in range(4)], direction)
        for d in range(4):
            result[c + 4 * d] = outs[d]
    return result


def halves(values):
    upper = values.astype(jnp.bfloat16)
    lower = (values - upper.astype(jnp.float32)).astype(jnp.bfloat16)
    return upper, lower


def right_product(values, table):
    upper, lower = halves(values)
    return jnp.dot(jnp.concatenate([upper, lower, upper], axis=1), table, preferred_element_type=jnp.float32)


def left_product(table, values):
    upper, lower = halves(values)
    return jnp.dot(table, jnp.concatenate([upper, lower, upper], axis=0), preferred_element_type=jnp.float32)


def tile(index):
    return slice(index * lane, (index + 1) * lane)


def lines_kernel(field_ref, turn_ref, table_ref, even_ref, odd_ref, work_ref):
    def rows(index, carry):
        here = pl.ds(pl.multiple_of(index * 8, 8), 8)
        parts = sixteen(
            [(field_ref[0, 0, here, tile(j)], field_ref[0, 1, here, tile(j)]) for j in range(radix)], -1
        )
        for k in range(radix):
            re, im = times(parts[k], (turn_ref[k, 0], turn_ref[k, 1]))
            work_ref[k, here, 0:lane] = re
            work_ref[k, here, lane : 2 * lane] = im
        return carry

    lax.fori_loop(0, row_block // 8, rows, 0, unroll=True)
    lines = right_product(work_ref[...].reshape(radix * row_block, 2 * lane), table_ref[...])
    for k in range(radix):
        block = lines[k * row_block : (k + 1) * row_block]
        for half in range(2):
            out_ref = (even_ref, odd_ref)[k % 2]
            out_ref[half * half_radix + k // 2, 0, 0:row_block] = block[:, 0:lane]
            out_ref[half * half_radix + k // 2, 0, row_block : 2 * row_block] = block[:, lane : 2 * lane]


def lines_call(wavefield):
    return pl.pallas_call(
        lines_kernel,
        grid=(blocks,),
        in_specs=[
            pl.BlockSpec((1, 2, row_block, full), lambda g: (0, 0, g, 0)),
            pl.BlockSpec((radix, 2, 8, lane), lambda g: (0, 0, 0, 0)),
            pl.BlockSpec((6 * lane, 2 * lane), lambda g: (0, 0)),
        ],
        out_specs=[pl.BlockSpec((radix, 1, piece, lane), lambda g: (0, g, 0, 0))] * 2,
        out_shape=[jax.ShapeDtypeStruct((radix, blocks, piece, lane), jnp.float32)] * 2,
        scratch_shapes=[pltpu.VMEM((radix, row_block, 2 * lane), jnp.float32)],
        compiler_params=pltpu.CompilerParams(vmem_limit_bytes=vmem_bytes),
        name="forward_lines",
    )(wavefield, lane_twiddle(-1, 1.0), right_table(-1))


def phase_kernel(angular_ref, out_ref):
    place = lax.axis_index("slab") % half_radix
    scale = 2.0 * math.pi / full
    lanes = lax.broadcasted_iota(jnp.int32, (32, lane), 1) * radix + place * 2
    seconds = []
    for c in range(2):
        column = lanes + c
        second = jnp.minimum(column, full - column).astype(jnp.float32) * scale
        seconds.append(second * second)
    row = lax.broadcasted_iota(jnp.int32, (32, lane), 0)
    squares = []
    for speed in ref_speeds:
        number = angular_ref[0] * np.float32(1.0 / np.float32(speed))
        squares.append(number * number)

    def chunk(index, carry):
        k = index // 4
        begin = pl.multiple_of((index % 4) * 32, 32)
        here = pl.ds(begin, 32)
        there = pl.ds(pl.multiple_of(k * lane, lane), lane)
        position = (row + begin) * radix + k
        first = jnp.minimum(position, full - position).astype(jnp.float32) * scale
        for c in range(2):
            wave_square = first * first + seconds[c]
            for j in range(len(ref_speeds)):
                vertical = squares[j] - wave_square
                root = jnp.sqrt(jnp.abs(vertical))
                moving = vertical >= 0.0
                out_ref[c, j, 0, here, there] = jnp.where(moving, horner(cos_series, vertical), jnp.exp(-root))
                out_ref[c, j, 1, here, there] = jnp.where(moving, root * horner(sinc_series, vertical), 0.0)
        return carry

    lax.fori_loop(0, radix * 4, chunk, 0)


def phase_call(frequencies):
    count = len(ref_speeds)
    return pl.pallas_call(
        phase_kernel,
        in_specs=[pl.BlockSpec(memory_space=pltpu.SMEM)],
        out_specs=pl.BlockSpec(memory_space=pltpu.VMEM),
        out_shape=jax.ShapeDtypeStruct((2, count, 2, lane, full), jnp.float32),
        compiler_params=pltpu.CompilerParams(vmem_limit_bytes=phase_vmem_bytes),
        cost_estimate=pl.CostEstimate(flops=120 * count * lane * full, bytes_accessed=16 * count * lane * full, transcendentals=0),
        name="phase_factors",
    )(frequencies)


def circle(index, modulus):
    half = modulus // 2
    angle = (((index + half) & (modulus - 1)) - half).astype(jnp.float32) * (2.0 * math.pi / modulus)
    square = angle * angle
    return horner(circle_cos, square), angle * horner(circle_sin, square)


def build_matrices(ahead_table_ref, back_table_ref):
    row = lax.broadcasted_iota(jnp.int32, (lane, lane), 0)
    column = lax.broadcasted_iota(jnp.int32, (lane, lane), 1)
    cosine, sine = circle(row * column, lane)
    for table_ref, direction, scale in ((ahead_table_ref, -1.0, 1.0), (back_table_ref, 1.0, 1.0 / full)):
        cos_now, sin_now = cosine * scale, sine * (direction * scale)
        for top, blocks_now in enumerate(((cos_now, -sin_now), (sin_now, cos_now))):
            here = slice(top * lane, (top + 1) * lane)
            for place, values in enumerate(blocks_now):
                upper, lower = halves(values)
                for third, part in enumerate((upper, upper, lower)):
                    table_ref[here, tile(2 * third + place)] = part


def rows_kernel(
    c, in_ref, phase_ref, out_ref,
    work_ref, spec_ref, turn_ref, column_ref, ahead_table_ref, back_table_ref,
    factor_ref, field_ref, factor_sem, field_sem,
):
    begin = lax.axis_index("slab") // half_radix * half_radix
    count = len(ref_speeds)

    def factor_copy(t):
        return pltpu.make_async_copy(phase_ref.at[c, t], factor_ref.at[t], factor_sem.at[t])

    def field_copy(t):
        return pltpu.make_async_copy(field_ref.at[t % 2], out_ref.at[:, t], field_sem.at[t % 2])

    for t in range(count):
        factor_copy(t).start()

    row = lax.broadcasted_iota(jnp.int32, (lane, lane), 0)
    power = lax.broadcasted_iota(jnp.int32, (lane, lane), 1) & (radix - 1)
    cosine, sine = circle(row * power, full)
    column_ref[0] = cosine
    column_ref[1] = -sine
    build_matrices(ahead_table_ref, back_table_ref)

    for block in range(blocks):

        def rows(index, carry):
            local = pl.multiple_of(index * 8, 8)
            pair = (pl.ds(local, 8), pl.ds(local + row_block, 8))
            here = pl.ds(pl.multiple_of(local + block * row_block, 8), 8)
            there = pl.ds(pl.multiple_of(local + block * row_block + lane, 8), 8)
            parts = sixteen([tuple(in_ref[begin ^ s, block, rows_now, :] for rows_now in pair) for s in range(radix)], -1)
            columns = (column_ref[0, here, :], column_ref[1, here, :])
            for k in range(radix):
                turn = tuple(jnp.broadcast_to(part[:, k : k + 1], (8, lane)) for part in columns)
                turn_ref[k, 0, here, :] = turn[0]
                turn_ref[k, 1, here, :] = turn[1]
                re, im = times(parts[k], turn)
                work_ref[0, here, tile(k)] = re
                work_ref[0, there, tile(k)] = im
            return carry

        lax.fori_loop(0, row_block // 8, rows, 0, unroll=2)

    def shifted(t, columns, spectrum):
        re, im = times(
            (spectrum[0:lane], spectrum[lane : 2 * lane]),
            (factor_ref[t, 0, :, columns], factor_ref[t, 1, :, columns]),
        )
        work_ref[(t + 1) % 2, :, columns] = left_product(
            back_table_ref[...], jnp.concatenate([re, im], axis=0)
        )

    def back(t, index):
        here = pl.ds(pl.multiple_of(index * 8, 8), 8)
        there = pl.ds(pl.multiple_of(index * 8 + lane, 8), 8)
        slot = (t + 1) % 2
        parts = sixteen(
            [
                conjugate_times(
                    (work_ref[slot, here, tile(k)], work_ref[slot, there, tile(k)]),
                    (turn_ref[k, 0, here, :], turn_ref[k, 1, here, :]),
                )
                for k in range(radix)
            ],
            1,
        )
        for s in range(half_radix):
            field_ref[t % 2, s, 0, here, :] = parts[s][0]
            field_ref[t % 2, s, 1, here, :] = parts[s][1]

    def pair_columns(index):
        return pl.ds(pl.multiple_of(index * 2 * lane, 2 * lane), 2 * lane)

    factor_copy(0).wait()

    def first(index, carry):
        columns = pair_columns(index)
        spectrum = left_product(ahead_table_ref[...], work_ref[0, :, columns])
        spec_ref[:, columns] = spectrum
        shifted(0, columns, spectrum)
        return carry

    lax.fori_loop(0, radix // 2, first, 0, unroll=True)

    for t in range(count):
        if t + 1 < count:
            factor_copy(t + 1).wait()
        if t >= 2:
            field_copy(t - 2).wait()

        def both(index, carry):
            if t + 1 < count:
                columns = pair_columns(index)
                shifted(t + 1, columns, spec_ref[:, columns])
            back(t, 2 * index)
            back(t, 2 * index + 1)
            return carry

        lax.fori_loop(0, radix // 2, both, 0, unroll=True)
        field_copy(t).start()

    for t in range(count - 2, count):
        field_copy(t).wait()


def rows_call(c, arrived, phase):
    count = len(ref_speeds)
    in_vmem = pl.BlockSpec(memory_space=pltpu.VMEM)
    in_hbm = pl.BlockSpec(memory_space=pltpu.HBM)
    return pl.pallas_call(
        functools.partial(rows_kernel, c),
        in_specs=[in_vmem, in_hbm],
        out_specs=in_hbm,
        out_shape=jax.ShapeDtypeStruct((half_radix, count, 2, lane, lane), jnp.float32),
        scratch_shapes=[
            pltpu.VMEM((2, 2 * lane, full), jnp.float32),
            pltpu.VMEM((2 * lane, full), jnp.float32),
            pltpu.VMEM((radix, 2, lane, lane), jnp.float32),
            pltpu.VMEM((2, lane, lane), jnp.float32),
            pltpu.VMEM((2 * lane, 6 * lane), jnp.bfloat16),
            pltpu.VMEM((2 * lane, 6 * lane), jnp.bfloat16),
            pltpu.VMEM((3, 2, lane, full), jnp.float32),
            pltpu.VMEM((2, half_radix, 2, lane, lane), jnp.float32),
            pltpu.SemaphoreType.DMA((3,)),
            pltpu.SemaphoreType.DMA((2,)),
        ],
        compiler_params=pltpu.CompilerParams(vmem_limit_bytes=rows_vmem_bytes),
        cost_estimate=pl.CostEstimate(
            flops=8 * 2 * 2 * lane * 6 * lane * full, bytes_accessed=28 * 8 * lane * full, transcendentals=0
        ),
        name="rows_there_and_back",
    )(arrived, phase)


def blend_kernel(angular_ref, bracket_ref, far_ref, swapped_ref, *refs):
    near_refs, out_ref, tile_ref = refs[:-2], refs[-2], refs[-1]
    shot, device = lax.axis_index("shot"), lax.axis_index("slab")
    half = lane // 2
    for k in range(half_radix):
        tile_ref[pl.ds(pl.multiple_of(shot * half, half), half), :] = far_ref[k]
        tile_ref[pl.ds(pl.multiple_of((1 - shot) * half, half), half), :] = swapped_ref[k]
        for source, speed in ((device ^ k, near_refs[k][0:lane, :]), (device ^ far ^ k, tile_ref[...])):
            there = pl.ds(pl.multiple_of(source * lane, lane), lane)
            speed = jnp.transpose(speed)
            first = bracket_ref[0, :, there] == 0
            low = jnp.where(first, ref_speeds[0], ref_speeds[1])
            width = jnp.where(first, 1.0 / (ref_speeds[1] - ref_speeds[0]), 1.0 / (ref_speeds[2] - ref_speeds[1]))
            fraction = (speed - low) * width
            low_slowness = jnp.where(first, 1.0 / ref_speeds[0], 1.0 / ref_speeds[1])
            high_slowness = jnp.where(first, 1.0 / ref_speeds[1], 1.0 / ref_speeds[2])
            residual = 1.0 / speed - ((1.0 - fraction) * low_slowness + fraction * high_slowness)
            angle = angular_ref[0] * step_length * residual
            square = angle * angle
            cosine = horner([1.0, -1 / 2, 1 / 24, -1 / 720, 1 / 40320], square)
            sine = angle * horner([1.0, -1 / 6, 1 / 120, -1 / 5040, 1 / 362880], square)
            out_ref[0, :, there] = fraction + jnp.where(first, 0.0, 1.0)
            out_ref[1, :, there] = cosine
            out_ref[2, :, there] = sine


def blend_call(frequencies, bracket, *speeds):
    in_vmem = pl.BlockSpec(memory_space=pltpu.VMEM)
    return pl.pallas_call(
        blend_kernel,
        in_specs=[pl.BlockSpec(memory_space=pltpu.SMEM)] + [in_vmem] * (1 + len(speeds)),
        out_specs=in_vmem,
        out_shape=jax.ShapeDtypeStruct((3, lane, full), jnp.float32),
        scratch_shapes=[pltpu.VMEM((lane, lane), jnp.float32)],
        compiler_params=pltpu.CompilerParams(vmem_limit_bytes=vmem_bytes),
        cost_estimate=pl.CostEstimate(flops=60 * lane * full, bytes_accessed=24 * lane * full, transcendentals=0),
        name="blend_factors",
    )(frequencies, bracket, *speeds)


strip = 32


def finish_kernel(even_ref, odd_ref, blend_ref, turn_ref, table_ref, out_ref, image_ref, work_ref):
    count = len(ref_speeds)
    for j in range(count):
        for c, in_ref in enumerate((even_ref, odd_ref)):
            values = jnp.concatenate([in_ref[:, j, 0], in_ref[:, j, 1]], axis=2)
            product = right_product(values.reshape(half_radix * strip, 2 * lane), table_ref[...])
            product = product.reshape(half_radix, strip, 2 * lane)
            for i in range(half_radix):
                work_ref[j, 2 * i + c] = product[i]

    def rows(index, carry):
        here = pl.ds(pl.multiple_of(index * 8, 8), 8)
        for j in range(count):
            parts = sixteen(
                [
                    times(
                        (work_ref[j, k, here, 0:lane], work_ref[j, k, here, lane : 2 * lane]),
                        (turn_ref[k, 0], turn_ref[k, 1]),
                    )
                    for k in range(radix)
                ],
                1,
            )
            for s in range(radix):
                place = blend_ref[0, here, tile(s)]
                if j == 0:
                    weight = jnp.maximum(1.0 - place, 0.0)
                elif j == 1:
                    weight = 1.0 - jnp.abs(place - 1.0)
                else:
                    weight = jnp.maximum(place - 1.0, 0.0)
                re, im = parts[s][0] * weight, parts[s][1] * weight
                if j > 0:
                    re, im = re + out_ref[0, 0, here, tile(s)], im + out_ref[0, 1, here, tile(s)]
                if j == count - 1:
                    re, im = times((re, im), (blend_ref[1, here, tile(s)], blend_ref[2, here, tile(s)]))
                    image_ref[0, here, tile(s)] = re
                out_ref[0, 0, here, tile(s)] = re
                out_ref[0, 1, here, tile(s)] = im
        return carry

    lax.fori_loop(0, strip // 8, rows, 0, unroll=True)


def finish_call(even, odd, blend):
    count = len(ref_speeds)
    return pl.pallas_call(
        finish_kernel,
        grid=(lane // strip,),
        in_specs=[
            pl.BlockSpec((half_radix, count, 2, strip, lane), lambda g: (0, 0, 0, g, 0)),
            pl.BlockSpec((half_radix, count, 2, strip, lane), lambda g: (0, 0, 0, g, 0)),
            pl.BlockSpec((3, strip, full), lambda g: (0, g, 0)),
            pl.BlockSpec((radix, 2, 8, lane), lambda g: (0, 0, 0, 0)),
            pl.BlockSpec((6 * lane, 2 * lane), lambda g: (0, 0)),
        ],
        out_specs=[
            pl.BlockSpec((1, 2, strip, full), lambda g: (0, 0, g, 0)),
            pl.BlockSpec((1, strip, full), lambda g: (0, g, 0)),
        ],
        out_shape=[
            jax.ShapeDtypeStruct((1, 2, lane, full), jnp.float32),
            jax.ShapeDtypeStruct((1, lane, full), jnp.float32),
        ],
        scratch_shapes=[
            pltpu.VMEM((count, radix, strip, 2 * lane), jnp.float32),
        ],
        compiler_params=pltpu.CompilerParams(vmem_limit_bytes=finish_vmem_bytes),
        name="inverse_lines",
    )(even, odd, blend, lane_twiddle(1, 1.0 / full), right_table(1))


def exchange(values, group):
    groups = [list(range(begin, begin + group)) for begin in range(0, radix, group)]
    return lax.all_to_all(values, "slab", split_axis=0, concat_axis=0, tiled=True, axis_index_groups=groups)


def partners(distance):
    return [(index, index ^ distance) for index in range(radix)]


def speeds_near(velocity):
    shot, device = lax.axis_index("shot"), lax.axis_index("slab")
    tiles = []
    for k in range(half_radix):
        near = lax.dynamic_slice(velocity[0], (0, (device ^ k) * lane), (lane, lane))
        beyond = lax.dynamic_slice(velocity[0], (shot * (lane // 2), (device ^ k ^ far) * lane), (lane // 2, lane))
        both = jnp.concatenate([near, beyond])
        tiles.append(lax.ppermute(both, "slab", partners(k)) if k else both)
    return tiles


def per_device(wavefield, frequencies, velocity, bracket):
    even, odd = lines_call(wavefield)
    velocity, even, odd = lax.optimization_barrier((velocity, even, odd))
    even = exchange(even, radix)
    speeds = speeds_near(velocity)
    beyond = jnp.stack([tile_now[lane:] for tile_now in speeds])
    phase = phase_call(frequencies)
    beyond, phase, even, odd = lax.optimization_barrier((beyond, phase, even, odd))
    odd = exchange(odd, radix)
    even = rows_call(0, even, phase)
    even, odd = lax.optimization_barrier((even, odd))
    even = exchange(even, half_radix)
    beyond, _ = lax.optimization_barrier((beyond, odd))
    beyond = lax.ppermute(beyond, "slab", partners(far))
    odd = rows_call(1, odd, phase)
    beyond, even, odd = lax.optimization_barrier((beyond, even, odd))
    odd = exchange(odd, half_radix)
    swapped = lax.ppermute(beyond, "shot", [(0, 1), (1, 0)])
    blend = blend_call(frequencies, bracket, beyond, swapped, *speeds)
    propagated, image = finish_call(even, odd, blend)
    return propagated, image


def fits(mesh, shapes):
    wavefield, velocity = shapes
    return (
        mesh.shape["slab"] == radix
        and mesh.shape["shot"] == 2
        and wavefield == (2, 2, full, full)
        and velocity == (1, full, full)
    )


def solution(mesh):
    def program(wavefield, frequencies, velocity, bracket):
        small = fits(mesh, (wavefield.shape, velocity.shape))
        return jax.shard_map(
            per_device if small else per_device_general,
            mesh=mesh,
            in_specs=(
                P("shot", None, "slab", None),
                P("shot"),
                P(None, "slab", None),
                P(None, "slab", None),
            ),
            out_specs=(P("shot", None, "slab", None), P("shot", "slab", None)),
            check_vma=False,
        )(wavefield, frequencies, velocity, bracket)

    return program
```

```python
import functools
import math

import jax
import jax.numpy as jnp
import ml_dtypes
import numpy as np
from jax import lax
from jax.experimental import pallas as pl
from jax.experimental.pallas import tpu as pltpu
from jax.sharding import PartitionSpec as P

ref_speeds = (1.0, 1.5, 2.25)
step_length = 1.0
highest = lax.Precision.HIGHEST


def dft_table(height, breadth, modulus, direction):
    down_index = lax.iota(jnp.int32, height)[:, None]
    across_index = lax.iota(jnp.int32, breadth)[None, :]
    angles = (down_index * across_index % modulus).astype(jnp.float32) * (
        direction * 2.0 * math.pi / modulus
    )
    return (jnp.cos(angles), jnp.sin(angles))


def contract(pattern, left_pair, right_pair):

    def product(one_side, other_side):
        return jnp.einsum(pattern, one_side, other_side, precision=highest)

    return (
        product(left_pair[0], right_pair[0]) - product(left_pair[1], right_pair[1]),
        product(left_pair[0], right_pair[1]) + product(left_pair[1], right_pair[0]),
    )


def rotate(values, factor_pair):
    return (
        values[0] * factor_pair[0] - values[1] * factor_pair[1],
        values[0] * factor_pair[1] + values[1] * factor_pair[0],
    )


def forward_lines(fields):
    item_count, row_count, extent = fields[0].shape
    devices = lax.axis_size("slab")
    line_count = extent // devices
    reshaped = tuple(
        (part_now.reshape(item_count, row_count, line_count, devices) for part_now in fields)
    )
    section_one = contract(
        "nrab,ak->nrkb", reshaped, dft_table(line_count, line_count, line_count, -1.0)
    )
    twisted = rotate(
        section_one,
        tuple((turning[None, None] for turning in dft_table(line_count, devices, extent, -1.0))),
    )
    section_two = contract("nrkb,bq->nkqr", twisted, dft_table(devices, devices, devices, -1.0))
    return tuple(
        (part_now.reshape(item_count, line_count, devices * row_count) for part_now in section_two)
    )


def forward_rows(fields):
    item_count, line_count, extent = fields[0].shape
    devices = lax.axis_size("slab")
    row_count = extent // devices
    reshaped = tuple(
        (part_now.reshape(item_count, line_count, devices, row_count) for part_now in fields)
    )
    section_one = contract("ncab,ak->nckb", reshaped, dft_table(devices, devices, devices, -1.0))
    twisted = rotate(
        section_one,
        tuple((turning[None, None] for turning in dft_table(devices, row_count, extent, -1.0))),
    )
    section_two = contract(
        "nckb,bq->nckq", twisted, dft_table(row_count, row_count, row_count, -1.0)
    )
    return tuple((part_now.reshape(item_count, line_count, extent) for part_now in section_two))


def inverse_rows(fields):
    item_count, line_count, extent = fields[0].shape
    devices = lax.axis_size("slab")
    row_count = extent // devices
    reshaped = tuple(
        (part_now.reshape(item_count, line_count, devices, row_count) for part_now in fields)
    )
    section_one = contract(
        "nckq,bq->nckb", reshaped, dft_table(row_count, row_count, row_count, 1.0)
    )
    twisted = rotate(
        section_one,
        tuple((turning[None, None] for turning in dft_table(devices, row_count, extent, 1.0))),
    )
    section_two = contract("nckb,ak->ncab", twisted, dft_table(devices, devices, devices, 1.0))
    return tuple(
        (
            part_now.reshape(item_count, line_count, extent) * (1.0 / extent)
            for part_now in section_two
        )
    )


def inverse_lines(fields):
    item_count, line_count, extent = fields[0].shape
    devices = lax.axis_size("slab")
    row_count = extent // devices
    total_lines = line_count * devices
    reshaped = tuple(
        (part_now.reshape(item_count, line_count, devices, row_count) for part_now in fields)
    )
    section_one = contract("nkqr,bq->nkbr", reshaped, dft_table(devices, devices, devices, 1.0))
    twisted = rotate(
        section_one,
        tuple(
            (
                turning[None, :, :, None]
                for turning in dft_table(line_count, devices, total_lines, 1.0)
            )
        ),
    )
    section_two = contract(
        "nkbr,ak->nrab", twisted, dft_table(line_count, line_count, line_count, 1.0)
    )
    return tuple(
        (
            part_now.reshape(item_count, row_count, total_lines) * (1.0 / total_lines)
            for part_now in section_two
        )
    )


def phase_shift(values, wave_square, angular):
    slowness = 1.0 / jnp.array(ref_speeds, jnp.float32)
    wave_number = angular[:, None] * slowness[None, :]
    vertical = (wave_number * wave_number)[:, :, None, None] - wave_square[None, None]
    root_abs = jnp.sqrt(jnp.abs(vertical))
    real_part = jnp.where(
        vertical >= 0, jnp.cos(step_length * root_abs), jnp.exp(-step_length * root_abs)
    )
    imag_part = jnp.where(vertical >= 0, jnp.sin(step_length * root_abs), 0.0)
    shifted = rotate((values[0][:, None], values[1][:, None]), (real_part, imag_part))
    item_count = values[0].shape[0]
    return tuple(
        (
            part_now.reshape((item_count * len(ref_speeds),) + values[0].shape[1:])
            for part_now in shifted
        )
    )


def weights(speed_grid, chosen):
    speeds = jnp.array(ref_speeds, jnp.float32)
    lower_speed = jnp.zeros_like(speed_grid)
    upper_speed = jnp.zeros_like(speed_grid)
    for ref_index in range(len(ref_speeds) - 1):
        lower_speed = lower_speed + jnp.where(chosen == ref_index, speeds[ref_index], 0.0)
        upper_speed = upper_speed + jnp.where(chosen == ref_index, speeds[ref_index + 1], 0.0)
    fraction = (speed_grid - lower_speed) / (upper_speed - lower_speed)
    residual_phase = 1.0 / speed_grid - ((1.0 - fraction) / lower_speed + fraction / upper_speed)
    coefficients = []
    for ref_index in range(len(ref_speeds)):
        coefficients.append(
            jnp.where(chosen == ref_index, 1.0 - fraction, 0.0)
            + jnp.where(chosen == ref_index - 1, fraction, 0.0)
        )
    return (jnp.stack(coefficients), residual_phase)


def advance(fields, angular, coefficients, residual_phase, spec_square):
    item_count, row_count, extent = fields[0].shape
    prepared = forward_lines(fields)
    spectrum = forward_rows(
        (
            lax.all_to_all(prepared[0], "slab", split_axis=2, concat_axis=2, tiled=True),
            lax.all_to_all(prepared[1], "slab", split_axis=2, concat_axis=2, tiled=True),
        )
    )
    returned = inverse_rows(phase_shift(spectrum, spec_square, angular))
    waves = inverse_lines(
        (
            lax.all_to_all(returned[0], "slab", split_axis=2, concat_axis=2, tiled=True),
            lax.all_to_all(returned[1], "slab", split_axis=2, concat_axis=2, tiled=True),
        )
    )
    ref_count = len(ref_speeds)
    wave_real = waves[0].reshape(item_count, ref_count, row_count, extent)
    wave_imag = waves[1].reshape(item_count, ref_count, row_count, extent)
    blended_real = jnp.sum(coefficients[None] * wave_real, axis=1)
    blended_imag = jnp.sum(coefficients[None] * wave_imag, axis=1)
    angles = angular[:, None, None] * step_length * residual_phase[None]
    return rotate((blended_real, blended_imag), (jnp.cos(angles), jnp.sin(angles)))


def folded(indices, modulus):
    return jnp.minimum(indices, modulus - indices).astype(jnp.float32) * (2.0 * math.pi / modulus)


def per_device_general(wavefield, frequencies, velocity, bracket):
    devices = lax.axis_size("slab")
    device_index = lax.axis_index("slab")
    row_count = wavefield.shape[2]
    extent_y = wavefield.shape[3]
    extent_x = row_count * devices
    line_count = extent_y // devices
    speed_columns = lax.all_to_all(velocity, "slab", split_axis=2, concat_axis=1, tiled=True)
    speed_rows = jnp.transpose(speed_columns, (0, 2, 1))
    column = lax.iota(jnp.int32, extent_x)
    line_index = lax.iota(jnp.int32, line_count)
    spec_first = folded(column // row_count + devices * (column % row_count), extent_x)
    spec_second = folded(device_index * line_count + line_index, extent_y)
    spec_square = (
        spec_first[None, :] * spec_first[None, :] + spec_second[:, None] * spec_second[:, None]
    )
    current = (wavefield[:, 0], wavefield[:, 1])
    coefficients, residual_phase = weights(speed_rows[0], bracket[0])
    single = (current[0], current[1])
    pieces = [advance(single, frequencies, coefficients, residual_phase, spec_square)]
    current = (
        jnp.concatenate([piece[0] for piece in pieces], axis=0),
        jnp.concatenate([piece[1] for piece in pieces], axis=0),
    )
    image_rows = [jnp.sum(current[0], axis=0)]
    return (jnp.stack(current, axis=1), jnp.stack(image_rows))


radix = 16
lane = 128
full = radix * lane
row_block = 64
half_radix = radix // 2
far = half_radix
blocks = lane // row_block
piece = 2 * row_block
vmem_bytes = 56 * 1024 * 1024
rows_vmem_bytes = 50 * 1024 * 1024
phase_vmem_bytes = 56 * 1024 * 1024
finish_vmem_bytes = 48 * 1024 * 1024


def split_table(table):
    upper = table.astype(ml_dtypes.bfloat16)
    lower = (table - upper.astype(np.float64)).astype(ml_dtypes.bfloat16)
    return upper, lower


def line_matrices(direction):
    angles = 2.0 * np.pi / lane * (np.outer(np.arange(lane), np.arange(lane)) % lane)
    cosine, sine = np.cos(angles), direction * np.sin(angles)
    return np.block([[cosine, sine], [-sine, cosine]])


def right_table(direction):
    upper, lower = split_table(line_matrices(direction))
    return np.concatenate([upper, upper, lower], axis=0)


def twiddle(direction, scale):
    angles = 2.0 * np.pi / full * np.outer(np.arange(radix), np.arange(lane))
    return np.stack([np.cos(angles), direction * np.sin(angles)], axis=1) * scale


def lane_twiddle(direction, scale):
    table = twiddle(direction, scale)[:, :, None, :]
    return np.ascontiguousarray(np.broadcast_to(table, (radix, 2, 8, lane))).astype(np.float32)


def root_series(offset, degree, end):
    nodes = np.polynomial.chebyshev.Chebyshev.interpolate(
        lambda q: np.sinc(np.sqrt(q) / np.pi) if offset else np.cos(np.sqrt(q)), degree, domain=[0.0, end]
    )
    return [float(value) for value in nodes.convert(kind=np.polynomial.Polynomial).coef]


cos_series, sinc_series = root_series(0, 7, 9.0), root_series(1, 6, 9.0)
circle_cos, circle_sin = root_series(0, 8, np.pi**2), root_series(1, 7, np.pi**2)


def horner(series, argument):
    total = jnp.full_like(argument, series[-1])
    for value in series[-2::-1]:
        total = total * argument + value
    return total


def times(left, right):
    return left[0] * right[0] - left[1] * right[1], left[0] * right[1] + left[1] * right[0]


def conjugate_times(left, right):
    return left[0] * right[0] + left[1] * right[1], left[1] * right[0] - left[0] * right[1]


def quarter(values, direction):
    (a_re, a_im), (b_re, b_im), (c_re, c_im), (d_re, d_im) = values
    p_re, p_im, m_re, m_im = a_re + c_re, a_im + c_im, a_re - c_re, a_im - c_im
    q_re, q_im, n_re, n_im = b_re + d_re, b_im + d_im, b_re - d_re, b_im - d_im
    if direction < 0:
        turn_re, turn_im = n_im, -n_re
    else:
        turn_re, turn_im = -n_im, n_re
    return [
        (p_re + q_re, p_im + q_im),
        (m_re + turn_re, m_im + turn_im),
        (p_re - q_re, p_im - q_im),
        (m_re - turn_re, m_im - turn_im),
    ]


def turned(value, power, direction):
    re, im = value
    power %= 16
    if power == 0:
        return value
    if power == 4:
        return (-direction * im, direction * re) if direction < 0 else (-im, re)
    half = math.sqrt(0.5)
    if power == 2:
        return ((re - direction * im) * half, (im + direction * re) * half)
    if power == 6:
        return ((-re - direction * im) * half, (direction * re - im) * half)
    cosine, sine = math.cos(math.pi * power / 8), direction * math.sin(math.pi * power / 8)
    return re * cosine - im * sine, re * sine + im * cosine


def sixteen(values, direction):
    first = [quarter([values[4 * a + b] for a in range(4)], direction) for b in range(4)]
    result = [None] * 16
    for c in range(4):
        outs = quarter([turned(first[b][c], b * c, direction) for b in range(4)], direction)
        for d in range(4):
            result[c + 4 * d] = outs[d]
    return result


def halves(values):
    upper = values.astype(jnp.bfloat16)
    lower = (values - upper.astype(jnp.float32)).astype(jnp.bfloat16)
    return upper, lower


def right_product(values, table):
    upper, lower = halves(values)
    return jnp.dot(jnp.concatenate([upper, lower, upper], axis=1), table, preferred_element_type=jnp.float32)


def left_product(table, values):
    upper, lower = halves(values)
    return jnp.dot(table, jnp.concatenate([upper, lower, upper], axis=0), preferred_element_type=jnp.float32)


def tile(index):
    return slice(index * lane, (index + 1) * lane)


def lines_kernel(c, field_ref, turn_ref, table_ref, out_ref, work_ref):
    def rows(index, carry):
        here = pl.ds(pl.multiple_of(index * 8, 8), 8)
        parts = sixteen(
            [(field_ref[0, 0, here, tile(j)], field_ref[0, 1, here, tile(j)]) for j in range(radix)], -1
        )
        for i in range(half_radix):
            k = 2 * i + c
            re, im = times(parts[k], (turn_ref[k, 0], turn_ref[k, 1]))
            work_ref[i, here, 0:lane] = re
            work_ref[i, here, lane : 2 * lane] = im
        return carry

    lax.fori_loop(0, row_block // 8, rows, 0, unroll=True)
    lines = right_product(work_ref[...].reshape(half_radix * row_block, 2 * lane), table_ref[...])
    for i in range(half_radix):
        block = lines[i * row_block : (i + 1) * row_block]
        for half in range(2):
            out_ref[half * half_radix + i, 0, 0:row_block] = block[:, 0:lane]
            out_ref[half * half_radix + i, 0, row_block : 2 * row_block] = block[:, lane : 2 * lane]


def lines_call(c, wavefield):
    return pl.pallas_call(
        functools.partial(lines_kernel, c),
        grid=(blocks,),
        in_specs=[
            pl.BlockSpec((1, 2, row_block, full), lambda g: (0, 0, g, 0)),
            pl.BlockSpec((radix, 2, 8, lane), lambda g: (0, 0, 0, 0)),
            pl.BlockSpec((6 * lane, 2 * lane), lambda g: (0, 0)),
        ],
        out_specs=pl.BlockSpec((radix, 1, piece, lane), lambda g: (0, g, 0, 0)),
        out_shape=jax.ShapeDtypeStruct((radix, blocks, piece, lane), jnp.float32),
        scratch_shapes=[pltpu.VMEM((half_radix, row_block, 2 * lane), jnp.float32)],
        compiler_params=pltpu.CompilerParams(vmem_limit_bytes=vmem_bytes),
        cost_estimate=pl.CostEstimate(
            flops=2 * lane * full * 6 * lane * 2, bytes_accessed=16 * lane * full, transcendentals=0
        ),
        name="forward_lines",
    )(wavefield, lane_twiddle(-1, 1.0), right_table(-1))


def phase_kernel(angular_ref, out_ref):
    place = lax.axis_index("slab") % half_radix
    scale = 2.0 * math.pi / full
    lanes = lax.broadcasted_iota(jnp.int32, (32, lane), 1) * radix + place * 2
    seconds = []
    for c in range(2):
        column = lanes + c
        second = jnp.minimum(column, full - column).astype(jnp.float32) * scale
        seconds.append(second * second)
    row = lax.broadcasted_iota(jnp.int32, (32, lane), 0)
    squares = []
    for speed in ref_speeds:
        number = angular_ref[0] * np.float32(1.0 / np.float32(speed))
        squares.append(number * number)

    def chunk(index, carry):
        k = index // 4
        begin = pl.multiple_of((index % 4) * 32, 32)
        here = pl.ds(begin, 32)
        there = pl.ds(pl.multiple_of(k * lane, lane), lane)
        position = (row + begin) * radix + k
        first = jnp.minimum(position, full - position).astype(jnp.float32) * scale
        for c in range(2):
            wave_square = first * first + seconds[c]
            for j in range(len(ref_speeds)):
                vertical = squares[j] - wave_square
                root = jnp.sqrt(jnp.abs(vertical))
                moving = vertical >= 0.0
                out_ref[c, j, 0, here, there] = jnp.where(moving, horner(cos_series, vertical), jnp.exp(-root))
                out_ref[c, j, 1, here, there] = jnp.where(moving, root * horner(sinc_series, vertical), 0.0)
        return carry

    lax.fori_loop(0, radix * 4, chunk, 0)


def phase_call(frequencies):
    count = len(ref_speeds)
    return pl.pallas_call(
        phase_kernel,
        in_specs=[pl.BlockSpec(memory_space=pltpu.SMEM)],
        out_specs=pl.BlockSpec(memory_space=pltpu.VMEM),
        out_shape=jax.ShapeDtypeStruct((2, count, 2, lane, full), jnp.float32),
        compiler_params=pltpu.CompilerParams(vmem_limit_bytes=phase_vmem_bytes),
        cost_estimate=pl.CostEstimate(flops=120 * count * lane * full, bytes_accessed=16 * count * lane * full, transcendentals=0),
        name="phase_factors",
    )(frequencies)


def circle(index, modulus):
    half = modulus // 2
    angle = (((index + half) & (modulus - 1)) - half).astype(jnp.float32) * (2.0 * math.pi / modulus)
    square = angle * angle
    return horner(circle_cos, square), angle * horner(circle_sin, square)


def put_matrix(table_ref, cosine, sine, turned_over):
    for top, blocks_now in enumerate(((cosine, sine), (-sine, cosine))):
        for place, values in enumerate(blocks_now):
            upper, lower = halves(values)
            for third, part in enumerate((upper, upper, lower)):
                if turned_over:
                    table_ref[tile(place), tile(2 * third + top)] = part
                else:
                    table_ref[tile(2 * third + top), tile(place)] = part


def unit_matrix():
    row = lax.broadcasted_iota(jnp.int32, (lane, lane), 0)
    column = lax.broadcasted_iota(jnp.int32, (lane, lane), 1)
    return circle(row * column, lane)


def build_matrices(ahead_table_ref, back_table_ref):
    cosine, sine = unit_matrix()
    put_matrix(ahead_table_ref, cosine, -sine, True)
    put_matrix(back_table_ref, cosine * (1.0 / full), sine * (1.0 / full), True)


def build_turns(turn_ref, direction, scale):
    for k in range(radix):
        place = lax.broadcasted_iota(jnp.int32, (8, lane), 1)
        cosine, sine = circle(place * k, full)
        turn_ref[k, 0] = cosine * scale
        turn_ref[k, 1] = sine * (direction * scale)


def rows_kernel(
    c, in_ref, phase_ref, out_ref,
    work_ref, spec_ref, turn_ref, column_ref, ahead_table_ref, back_table_ref,
    factor_ref, field_ref, factor_sem, field_sem,
):
    begin = lax.axis_index("slab") // half_radix * half_radix
    count = len(ref_speeds)

    def factor_copy(t):
        return pltpu.make_async_copy(phase_ref.at[c, t], factor_ref.at[t], factor_sem.at[t])

    def field_copy(t):
        return pltpu.make_async_copy(field_ref.at[t % 2], out_ref.at[:, t], field_sem.at[t % 2])

    for t in range(count):
        factor_copy(t).start()

    row = lax.broadcasted_iota(jnp.int32, (lane, lane), 0)
    power = lax.broadcasted_iota(jnp.int32, (lane, lane), 1) & (radix - 1)
    cosine, sine = circle(row * power, full)
    column_ref[0] = cosine
    column_ref[1] = -sine
    build_matrices(ahead_table_ref, back_table_ref)

    for block in range(blocks):

        def rows(index, carry):
            local = pl.multiple_of(index * 8, 8)
            pair = (pl.ds(local, 8), pl.ds(local + row_block, 8))
            here = pl.ds(pl.multiple_of(local + block * row_block, 8), 8)
            there = pl.ds(pl.multiple_of(local + block * row_block + lane, 8), 8)
            parts = sixteen([tuple(in_ref[begin ^ s, block, rows_now, :] for rows_now in pair) for s in range(radix)], -1)
            columns = (column_ref[0, here, :], column_ref[1, here, :])
            for k in range(radix):
                turn = tuple(jnp.broadcast_to(part[:, k : k + 1], (8, lane)) for part in columns)
                turn_ref[k, 0, here, :] = turn[0]
                turn_ref[k, 1, here, :] = turn[1]
                re, im = times(parts[k], turn)
                work_ref[0, here, tile(k)] = re
                work_ref[0, there, tile(k)] = im
            return carry

        lax.fori_loop(0, row_block // 8, rows, 0, unroll=2)

    def shifted(t, columns, spectrum):
        re, im = times(
            (spectrum[0:lane], spectrum[lane : 2 * lane]),
            (factor_ref[t, 0, :, columns], factor_ref[t, 1, :, columns]),
        )
        work_ref[(t + 1) % 2, :, columns] = left_product(
            back_table_ref[...], jnp.concatenate([re, im], axis=0)
        )

    def back(t, index):
        here = pl.ds(pl.multiple_of(index * 8, 8), 8)
        there = pl.ds(pl.multiple_of(index * 8 + lane, 8), 8)
        slot = (t + 1) % 2
        parts = sixteen(
            [
                conjugate_times(
                    (work_ref[slot, here, tile(k)], work_ref[slot, there, tile(k)]),
                    (turn_ref[k, 0, here, :], turn_ref[k, 1, here, :]),
                )
                for k in range(radix)
            ],
            1,
        )
        for s in range(half_radix):
            field_ref[t % 2, s, 0, here, :] = parts[s][0]
            field_ref[t % 2, s, 1, here, :] = parts[s][1]

    def pair_columns(index):
        return pl.ds(pl.multiple_of(index * 2 * lane, 2 * lane), 2 * lane)

    factor_copy(0).wait()

    def first(index, carry):
        columns = pair_columns(index)
        spectrum = left_product(ahead_table_ref[...], work_ref[0, :, columns])
        spec_ref[:, columns] = spectrum
        shifted(0, columns, spectrum)
        return carry

    lax.fori_loop(0, radix // 2, first, 0, unroll=True)

    for t in range(count):
        if t + 1 < count:
            factor_copy(t + 1).wait()
        if t >= 2:
            field_copy(t - 2).wait()

        def both(index, carry):
            if t + 1 < count:
                columns = pair_columns(index)
                shifted(t + 1, columns, spec_ref[:, columns])
            back(t, 2 * index)
            back(t, 2 * index + 1)
            return carry

        lax.fori_loop(0, radix // 2, both, 0, unroll=True)
        field_copy(t).start()

    for t in range(count - 2, count):
        field_copy(t).wait()


def rows_call(c, arrived, phase):
    count = len(ref_speeds)
    in_vmem = pl.BlockSpec(memory_space=pltpu.VMEM)
    in_hbm = pl.BlockSpec(memory_space=pltpu.HBM)
    return pl.pallas_call(
        functools.partial(rows_kernel, c),
        in_specs=[in_vmem, in_hbm],
        out_specs=in_hbm,
        out_shape=jax.ShapeDtypeStruct((half_radix, count, 2, lane, lane), jnp.float32),
        scratch_shapes=[
            pltpu.VMEM((2, 2 * lane, full), jnp.float32),
            pltpu.VMEM((2 * lane, full), jnp.float32),
            pltpu.VMEM((radix, 2, lane, lane), jnp.float32),
            pltpu.VMEM((2, lane, lane), jnp.float32),
            pltpu.VMEM((2 * lane, 6 * lane), jnp.bfloat16),
            pltpu.VMEM((2 * lane, 6 * lane), jnp.bfloat16),
            pltpu.VMEM((3, 2, lane, full), jnp.float32),
            pltpu.VMEM((2, half_radix, 2, lane, lane), jnp.float32),
            pltpu.SemaphoreType.DMA((3,)),
            pltpu.SemaphoreType.DMA((2,)),
        ],
        compiler_params=pltpu.CompilerParams(vmem_limit_bytes=rows_vmem_bytes),
        cost_estimate=pl.CostEstimate(
            flops=8 * 2 * 2 * lane * 6 * lane * full, bytes_accessed=28 * 8 * lane * full, transcendentals=0
        ),
        name="rows_there_and_back",
    )(arrived, phase)


def blend_kernel(angular_ref, bracket_ref, far_ref, swapped_ref, *refs):
    near_refs, out_ref, tile_ref = refs[:-2], refs[-2], refs[-1]
    shot, device = lax.axis_index("shot"), lax.axis_index("slab")
    half = lane // 2
    for k in range(half_radix):
        tile_ref[pl.ds(pl.multiple_of(shot * half, half), half), :] = far_ref[k]
        tile_ref[pl.ds(pl.multiple_of((1 - shot) * half, half), half), :] = swapped_ref[k]
        for source, speed in ((device ^ k, near_refs[k][0:lane, :]), (device ^ far ^ k, tile_ref[...])):
            there = pl.ds(pl.multiple_of(source * lane, lane), lane)
            speed = jnp.transpose(speed)
            first = bracket_ref[0, :, there] == 0
            low = jnp.where(first, ref_speeds[0], ref_speeds[1])
            width = jnp.where(first, 1.0 / (ref_speeds[1] - ref_speeds[0]), 1.0 / (ref_speeds[2] - ref_speeds[1]))
            fraction = (speed - low) * width
            low_slowness = jnp.where(first, 1.0 / ref_speeds[0], 1.0 / ref_speeds[1])
            high_slowness = jnp.where(first, 1.0 / ref_speeds[1], 1.0 / ref_speeds[2])
            residual = 1.0 / speed - ((1.0 - fraction) * low_slowness + fraction * high_slowness)
            angle = angular_ref[0] * step_length * residual
            square = angle * angle
            cosine = horner([1.0, -1 / 2, 1 / 24, -1 / 720, 1 / 40320], square)
            sine = angle * horner([1.0, -1 / 6, 1 / 120, -1 / 5040, 1 / 362880], square)
            out_ref[0, :, there] = fraction + jnp.where(first, 0.0, 1.0)
            out_ref[1, :, there] = cosine
            out_ref[2, :, there] = sine


def blend_call(frequencies, bracket, *speeds):
    in_vmem = pl.BlockSpec(memory_space=pltpu.VMEM)
    return pl.pallas_call(
        blend_kernel,
        in_specs=[pl.BlockSpec(memory_space=pltpu.SMEM)] + [in_vmem] * (1 + len(speeds)),
        out_specs=in_vmem,
        out_shape=jax.ShapeDtypeStruct((3, lane, full), jnp.float32),
        scratch_shapes=[pltpu.VMEM((lane, lane), jnp.float32)],
        compiler_params=pltpu.CompilerParams(vmem_limit_bytes=vmem_bytes),
        cost_estimate=pl.CostEstimate(flops=60 * lane * full, bytes_accessed=24 * lane * full, transcendentals=0),
        name="blend_factors",
    )(frequencies, bracket, *speeds)


strip = 32


def finish_kernel(even_ref, odd_ref, blend_ref, out_ref, image_ref, work_ref, turn_ref, table_ref):
    count = len(ref_speeds)

    @pl.when(pl.program_id(0) == 0)
    def _():
        build_turns(turn_ref, 1.0, 1.0 / full)
        put_matrix(table_ref, *unit_matrix(), False)

    for j in range(count):
        for c, in_ref in enumerate((even_ref, odd_ref)):
            values = jnp.concatenate([in_ref[:, j, 0], in_ref[:, j, 1]], axis=2)
            product = right_product(values.reshape(half_radix * strip, 2 * lane), table_ref[...])
            product = product.reshape(half_radix, strip, 2 * lane)
            for i in range(half_radix):
                work_ref[j, 2 * i + c] = product[i]

    def rows(index, carry):
        here = pl.ds(pl.multiple_of(index * 8, 8), 8)
        for j in range(count):
            parts = sixteen(
                [
                    times(
                        (work_ref[j, k, here, 0:lane], work_ref[j, k, here, lane : 2 * lane]),
                        (turn_ref[k, 0], turn_ref[k, 1]),
                    )
                    for k in range(radix)
                ],
                1,
            )
            for s in range(radix):
                place = blend_ref[0, here, tile(s)]
                if j == 0:
                    weight = jnp.maximum(1.0 - place, 0.0)
                elif j == 1:
                    weight = 1.0 - jnp.abs(place - 1.0)
                else:
                    weight = jnp.maximum(place - 1.0, 0.0)
                re, im = parts[s][0] * weight, parts[s][1] * weight
                if j > 0:
                    re, im = re + out_ref[0, 0, here, tile(s)], im + out_ref[0, 1, here, tile(s)]
                if j == count - 1:
                    re, im = times((re, im), (blend_ref[1, here, tile(s)], blend_ref[2, here, tile(s)]))
                    image_ref[0, here, tile(s)] = re
                out_ref[0, 0, here, tile(s)] = re
                out_ref[0, 1, here, tile(s)] = im
        return carry

    lax.fori_loop(0, strip // 8, rows, 0, unroll=True)


def finish_call(even, odd, blend):
    count = len(ref_speeds)
    return pl.pallas_call(
        finish_kernel,
        grid=(lane // strip,),
        in_specs=[
            pl.BlockSpec((half_radix, count, 2, strip, lane), lambda g: (0, 0, 0, g, 0)),
            pl.BlockSpec((half_radix, count, 2, strip, lane), lambda g: (0, 0, 0, g, 0)),
            pl.BlockSpec((3, strip, full), lambda g: (0, g, 0)),
        ],
        out_specs=[
            pl.BlockSpec((1, 2, strip, full), lambda g: (0, 0, g, 0)),
            pl.BlockSpec((1, strip, full), lambda g: (0, g, 0)),
        ],
        out_shape=[
            jax.ShapeDtypeStruct((1, 2, lane, full), jnp.float32),
            jax.ShapeDtypeStruct((1, lane, full), jnp.float32),
        ],
        scratch_shapes=[
            pltpu.VMEM((count, radix, strip, 2 * lane), jnp.float32),
            pltpu.VMEM((radix, 2, 8, lane), jnp.float32),
            pltpu.VMEM((6 * lane, 2 * lane), jnp.bfloat16),
        ],
        compiler_params=pltpu.CompilerParams(vmem_limit_bytes=finish_vmem_bytes),
        name="inverse_lines",
    )(even, odd, blend)


def exchange(values, group):
    groups = [list(range(begin, begin + group)) for begin in range(0, radix, group)]
    return lax.all_to_all(values, "slab", split_axis=0, concat_axis=0, tiled=True, axis_index_groups=groups)


def partners(distance):
    return [(index, index ^ distance) for index in range(radix)]


def speeds_near(velocity):
    shot, device = lax.axis_index("shot"), lax.axis_index("slab")
    tiles = []
    for k in range(half_radix):
        near = lax.dynamic_slice(velocity[0], (0, (device ^ k) * lane), (lane, lane))
        beyond = lax.dynamic_slice(velocity[0], (shot * (lane // 2), (device ^ k ^ far) * lane), (lane // 2, lane))
        both = jnp.concatenate([near, beyond])
        tiles.append(lax.ppermute(both, "slab", partners(k)) if k else both)
    return tiles


def per_device(wavefield, frequencies, velocity, bracket):
    even = lines_call(0, wavefield)
    velocity, even, wavefield = lax.optimization_barrier((velocity, even, wavefield))
    even = exchange(even, radix)
    odd = lines_call(1, wavefield)
    speeds = speeds_near(velocity)
    beyond = jnp.stack([tile_now[lane:] for tile_now in speeds])
    phase = phase_call(frequencies)
    beyond, phase, even, odd = lax.optimization_barrier((beyond, phase, even, odd))
    odd = exchange(odd, radix)
    even = rows_call(0, even, phase)
    even, odd = lax.optimization_barrier((even, odd))
    even = exchange(even, half_radix)
    beyond, _ = lax.optimization_barrier((beyond, odd))
    beyond = lax.ppermute(beyond, "slab", partners(far))
    odd = rows_call(1, odd, phase)
    beyond, even, odd = lax.optimization_barrier((beyond, even, odd))
    odd = exchange(odd, half_radix)
    swapped = lax.ppermute(beyond, "shot", [(0, 1), (1, 0)])
    blend = blend_call(frequencies, bracket, beyond, swapped, *speeds)
    propagated, image = finish_call(even, odd, blend)
    return propagated, image


def fits(mesh, shapes):
    wavefield, velocity = shapes
    return (
        mesh.shape["slab"] == radix
        and mesh.shape["shot"] == 2
        and wavefield == (2, 2, full, full)
        and velocity == (1, full, full)
    )


def solution(mesh):
    def program(wavefield, frequencies, velocity, bracket):
        small = fits(mesh, (wavefield.shape, velocity.shape))
        return jax.shard_map(
            per_device if small else per_device_general,
            mesh=mesh,
            in_specs=(
                P("shot", None, "slab", None),
                P("shot"),
                P(None, "slab", None),
                P(None, "slab", None),
            ),
            out_specs=(P("shot", None, "slab", None), P("shot", "slab", None)),
            check_vma=False,
        )(wavefield, frequencies, velocity, bracket)

    return program
```

```python
import functools
import math

import jax
import jax.numpy as jnp
import ml_dtypes
import numpy as np
from jax import lax
from jax.experimental import pallas as pl
from jax.experimental.pallas import tpu as pltpu
from jax.sharding import PartitionSpec as P

ref_speeds = (1.0, 1.5, 2.25)
step_length = 1.0
highest = lax.Precision.HIGHEST


def dft_table(height, breadth, modulus, direction):
    down_index = lax.iota(jnp.int32, height)[:, None]
    across_index = lax.iota(jnp.int32, breadth)[None, :]
    angles = (down_index * across_index % modulus).astype(jnp.float32) * (
        direction * 2.0 * math.pi / modulus
    )
    return (jnp.cos(angles), jnp.sin(angles))


def contract(pattern, left_pair, right_pair):

    def product(one_side, other_side):
        return jnp.einsum(pattern, one_side, other_side, precision=highest)

    return (
        product(left_pair[0], right_pair[0]) - product(left_pair[1], right_pair[1]),
        product(left_pair[0], right_pair[1]) + product(left_pair[1], right_pair[0]),
    )


def rotate(values, factor_pair):
    return (
        values[0] * factor_pair[0] - values[1] * factor_pair[1],
        values[0] * factor_pair[1] + values[1] * factor_pair[0],
    )


def forward_lines(fields):
    item_count, row_count, extent = fields[0].shape
    devices = lax.axis_size("slab")
    line_count = extent // devices
    reshaped = tuple(
        (part_now.reshape(item_count, row_count, line_count, devices) for part_now in fields)
    )
    section_one = contract(
        "nrab,ak->nrkb", reshaped, dft_table(line_count, line_count, line_count, -1.0)
    )
    twisted = rotate(
        section_one,
        tuple((turning[None, None] for turning in dft_table(line_count, devices, extent, -1.0))),
    )
    section_two = contract("nrkb,bq->nkqr", twisted, dft_table(devices, devices, devices, -1.0))
    return tuple(
        (part_now.reshape(item_count, line_count, devices * row_count) for part_now in section_two)
    )


def forward_rows(fields):
    item_count, line_count, extent = fields[0].shape
    devices = lax.axis_size("slab")
    row_count = extent // devices
    reshaped = tuple(
        (part_now.reshape(item_count, line_count, devices, row_count) for part_now in fields)
    )
    section_one = contract("ncab,ak->nckb", reshaped, dft_table(devices, devices, devices, -1.0))
    twisted = rotate(
        section_one,
        tuple((turning[None, None] for turning in dft_table(devices, row_count, extent, -1.0))),
    )
    section_two = contract(
        "nckb,bq->nckq", twisted, dft_table(row_count, row_count, row_count, -1.0)
    )
    return tuple((part_now.reshape(item_count, line_count, extent) for part_now in section_two))


def inverse_rows(fields):
    item_count, line_count, extent = fields[0].shape
    devices = lax.axis_size("slab")
    row_count = extent // devices
    reshaped = tuple(
        (part_now.reshape(item_count, line_count, devices, row_count) for part_now in fields)
    )
    section_one = contract(
        "nckq,bq->nckb", reshaped, dft_table(row_count, row_count, row_count, 1.0)
    )
    twisted = rotate(
        section_one,
        tuple((turning[None, None] for turning in dft_table(devices, row_count, extent, 1.0))),
    )
    section_two = contract("nckb,ak->ncab", twisted, dft_table(devices, devices, devices, 1.0))
    return tuple(
        (
            part_now.reshape(item_count, line_count, extent) * (1.0 / extent)
            for part_now in section_two
        )
    )


def inverse_lines(fields):
    item_count, line_count, extent = fields[0].shape
    devices = lax.axis_size("slab")
    row_count = extent // devices
    total_lines = line_count * devices
    reshaped = tuple(
        (part_now.reshape(item_count, line_count, devices, row_count) for part_now in fields)
    )
    section_one = contract("nkqr,bq->nkbr", reshaped, dft_table(devices, devices, devices, 1.0))
    twisted = rotate(
        section_one,
        tuple(
            (
                turning[None, :, :, None]
                for turning in dft_table(line_count, devices, total_lines, 1.0)
            )
        ),
    )
    section_two = contract(
        "nkbr,ak->nrab", twisted, dft_table(line_count, line_count, line_count, 1.0)
    )
    return tuple(
        (
            part_now.reshape(item_count, row_count, total_lines) * (1.0 / total_lines)
            for part_now in section_two
        )
    )


def phase_shift(values, wave_square, angular):
    slowness = 1.0 / jnp.array(ref_speeds, jnp.float32)
    wave_number = angular[:, None] * slowness[None, :]
    vertical = (wave_number * wave_number)[:, :, None, None] - wave_square[None, None]
    root_abs = jnp.sqrt(jnp.abs(vertical))
    real_part = jnp.where(
        vertical >= 0, jnp.cos(step_length * root_abs), jnp.exp(-step_length * root_abs)
    )
    imag_part = jnp.where(vertical >= 0, jnp.sin(step_length * root_abs), 0.0)
    shifted = rotate((values[0][:, None], values[1][:, None]), (real_part, imag_part))
    item_count = values[0].shape[0]
    return tuple(
        (
            part_now.reshape((item_count * len(ref_speeds),) + values[0].shape[1:])
            for part_now in shifted
        )
    )


def weights(speed_grid, chosen):
    speeds = jnp.array(ref_speeds, jnp.float32)
    lower_speed = jnp.zeros_like(speed_grid)
    upper_speed = jnp.zeros_like(speed_grid)
    for ref_index in range(len(ref_speeds) - 1):
        lower_speed = lower_speed + jnp.where(chosen == ref_index, speeds[ref_index], 0.0)
        upper_speed = upper_speed + jnp.where(chosen == ref_index, speeds[ref_index + 1], 0.0)
    fraction = (speed_grid - lower_speed) / (upper_speed - lower_speed)
    residual_phase = 1.0 / speed_grid - ((1.0 - fraction) / lower_speed + fraction / upper_speed)
    coefficients = []
    for ref_index in range(len(ref_speeds)):
        coefficients.append(
            jnp.where(chosen == ref_index, 1.0 - fraction, 0.0)
            + jnp.where(chosen == ref_index - 1, fraction, 0.0)
        )
    return (jnp.stack(coefficients), residual_phase)


def advance(fields, angular, coefficients, residual_phase, spec_square):
    item_count, row_count, extent = fields[0].shape
    prepared = forward_lines(fields)
    spectrum = forward_rows(
        (
            lax.all_to_all(prepared[0], "slab", split_axis=2, concat_axis=2, tiled=True),
            lax.all_to_all(prepared[1], "slab", split_axis=2, concat_axis=2, tiled=True),
        )
    )
    returned = inverse_rows(phase_shift(spectrum, spec_square, angular))
    waves = inverse_lines(
        (
            lax.all_to_all(returned[0], "slab", split_axis=2, concat_axis=2, tiled=True),
            lax.all_to_all(returned[1], "slab", split_axis=2, concat_axis=2, tiled=True),
        )
    )
    ref_count = len(ref_speeds)
    wave_real = waves[0].reshape(item_count, ref_count, row_count, extent)
    wave_imag = waves[1].reshape(item_count, ref_count, row_count, extent)
    blended_real = jnp.sum(coefficients[None] * wave_real, axis=1)
    blended_imag = jnp.sum(coefficients[None] * wave_imag, axis=1)
    angles = angular[:, None, None] * step_length * residual_phase[None]
    return rotate((blended_real, blended_imag), (jnp.cos(angles), jnp.sin(angles)))


def folded(indices, modulus):
    return jnp.minimum(indices, modulus - indices).astype(jnp.float32) * (2.0 * math.pi / modulus)


def per_device_general(wavefield, frequencies, velocity, bracket):
    devices = lax.axis_size("slab")
    device_index = lax.axis_index("slab")
    row_count = wavefield.shape[2]
    extent_y = wavefield.shape[3]
    extent_x = row_count * devices
    line_count = extent_y // devices
    speed_columns = lax.all_to_all(velocity, "slab", split_axis=2, concat_axis=1, tiled=True)
    speed_rows = jnp.transpose(speed_columns, (0, 2, 1))
    column = lax.iota(jnp.int32, extent_x)
    line_index = lax.iota(jnp.int32, line_count)
    spec_first = folded(column // row_count + devices * (column % row_count), extent_x)
    spec_second = folded(device_index * line_count + line_index, extent_y)
    spec_square = (
        spec_first[None, :] * spec_first[None, :] + spec_second[:, None] * spec_second[:, None]
    )
    current = (wavefield[:, 0], wavefield[:, 1])
    coefficients, residual_phase = weights(speed_rows[0], bracket[0])
    single = (current[0], current[1])
    pieces = [advance(single, frequencies, coefficients, residual_phase, spec_square)]
    current = (
        jnp.concatenate([piece[0] for piece in pieces], axis=0),
        jnp.concatenate([piece[1] for piece in pieces], axis=0),
    )
    image_rows = [jnp.sum(current[0], axis=0)]
    return (jnp.stack(current, axis=1), jnp.stack(image_rows))


radix = 16
lane = 128
full = radix * lane
row_block = 64
half_radix = radix // 2
far = half_radix
blocks = lane // row_block
piece = 2 * row_block
vmem_bytes = 56 * 1024 * 1024
rows_vmem_bytes = 50 * 1024 * 1024
phase_vmem_bytes = 56 * 1024 * 1024
finish_vmem_bytes = 48 * 1024 * 1024


def split_table(table):
    upper = table.astype(ml_dtypes.bfloat16)
    lower = (table - upper.astype(np.float64)).astype(ml_dtypes.bfloat16)
    return upper, lower


def line_matrices(direction):
    angles = 2.0 * np.pi / lane * (np.outer(np.arange(lane), np.arange(lane)) % lane)
    cosine, sine = np.cos(angles), direction * np.sin(angles)
    return np.block([[cosine, sine], [-sine, cosine]])


def right_table(direction):
    upper, lower = split_table(line_matrices(direction))
    return np.concatenate([upper, upper, lower], axis=0)


def twiddle(direction, scale):
    angles = 2.0 * np.pi / full * np.outer(np.arange(radix), np.arange(lane))
    return np.stack([np.cos(angles), direction * np.sin(angles)], axis=1) * scale


def lane_twiddle(direction, scale):
    table = twiddle(direction, scale)[:, :, None, :]
    return np.ascontiguousarray(np.broadcast_to(table, (radix, 2, 8, lane))).astype(np.float32)


def root_series(offset, degree, end):
    nodes = np.polynomial.chebyshev.Chebyshev.interpolate(
        lambda q: np.sinc(np.sqrt(q) / np.pi) if offset else np.cos(np.sqrt(q)), degree, domain=[0.0, end]
    )
    return [float(value) for value in nodes.convert(kind=np.polynomial.Polynomial).coef]


cos_series, sinc_series = root_series(0, 7, 9.0), root_series(1, 6, 9.0)
circle_cos, circle_sin = root_series(0, 8, np.pi**2), root_series(1, 7, np.pi**2)


def horner(series, argument):
    total = jnp.full_like(argument, series[-1])
    for value in series[-2::-1]:
        total = total * argument + value
    return total


def times(left, right):
    return left[0] * right[0] - left[1] * right[1], left[0] * right[1] + left[1] * right[0]


def conjugate_times(left, right):
    return left[0] * right[0] + left[1] * right[1], left[1] * right[0] - left[0] * right[1]


def quarter(values, direction):
    (a_re, a_im), (b_re, b_im), (c_re, c_im), (d_re, d_im) = values
    p_re, p_im, m_re, m_im = a_re + c_re, a_im + c_im, a_re - c_re, a_im - c_im
    q_re, q_im, n_re, n_im = b_re + d_re, b_im + d_im, b_re - d_re, b_im - d_im
    if direction < 0:
        turn_re, turn_im = n_im, -n_re
    else:
        turn_re, turn_im = -n_im, n_re
    return [
        (p_re + q_re, p_im + q_im),
        (m_re + turn_re, m_im + turn_im),
        (p_re - q_re, p_im - q_im),
        (m_re - turn_re, m_im - turn_im),
    ]


def turned(value, power, direction):
    re, im = value
    power %= 16
    if power == 0:
        return value
    if power == 4:
        return (-direction * im, direction * re) if direction < 0 else (-im, re)
    half = math.sqrt(0.5)
    if power == 2:
        return ((re - direction * im) * half, (im + direction * re) * half)
    if power == 6:
        return ((-re - direction * im) * half, (direction * re - im) * half)
    cosine, sine = math.cos(math.pi * power / 8), direction * math.sin(math.pi * power / 8)
    return re * cosine - im * sine, re * sine + im * cosine


def sixteen(values, direction):
    first = [quarter([values[4 * a + b] for a in range(4)], direction) for b in range(4)]
    result = [None] * 16
    for c in range(4):
        outs = quarter([turned(first[b][c], b * c, direction) for b in range(4)], direction)
        for d in range(4):
            result[c + 4 * d] = outs[d]
    return result


def halves(values):
    upper = values.astype(jnp.bfloat16)
    lower = (values - upper.astype(jnp.float32)).astype(jnp.bfloat16)
    return upper, lower


def right_product(values, table):
    upper, lower = halves(values)
    return jnp.dot(jnp.concatenate([upper, lower, upper], axis=1), table, preferred_element_type=jnp.float32)


def left_product(table, values):
    upper, lower = halves(values)
    return jnp.dot(table, jnp.concatenate([upper, lower, upper], axis=0), preferred_element_type=jnp.float32)


def tile(index):
    return slice(index * lane, (index + 1) * lane)


def lines_kernel(c, field_ref, turn_ref, table_ref, out_ref, work_ref):
    def rows(index, carry):
        here = pl.ds(pl.multiple_of(index * 8, 8), 8)
        parts = sixteen(
            [(field_ref[0, 0, here, tile(j)], field_ref[0, 1, here, tile(j)]) for j in range(radix)], -1
        )
        for i in range(half_radix):
            k = 2 * i + c
            re, im = times(parts[k], (turn_ref[k, 0], turn_ref[k, 1]))
            work_ref[i, here, 0:lane] = re
            work_ref[i, here, lane : 2 * lane] = im
        return carry

    lax.fori_loop(0, row_block // 8, rows, 0, unroll=True)
    lines = right_product(work_ref[...].reshape(half_radix * row_block, 2 * lane), table_ref[...])
    for i in range(half_radix):
        block = lines[i * row_block : (i + 1) * row_block]
        for half in range(2):
            out_ref[half * half_radix + i, 0, 0:row_block] = block[:, 0:lane]
            out_ref[half * half_radix + i, 0, row_block : 2 * row_block] = block[:, lane : 2 * lane]


def lines_call(c, wavefield):
    return pl.pallas_call(
        functools.partial(lines_kernel, c),
        grid=(blocks,),
        in_specs=[
            pl.BlockSpec((1, 2, row_block, full), lambda g: (0, 0, g, 0)),
            pl.BlockSpec((radix, 2, 8, lane), lambda g: (0, 0, 0, 0)),
            pl.BlockSpec((6 * lane, 2 * lane), lambda g: (0, 0)),
        ],
        out_specs=pl.BlockSpec((radix, 1, piece, lane), lambda g: (0, g, 0, 0)),
        out_shape=jax.ShapeDtypeStruct((radix, blocks, piece, lane), jnp.float32),
        scratch_shapes=[pltpu.VMEM((half_radix, row_block, 2 * lane), jnp.float32)],
        compiler_params=pltpu.CompilerParams(vmem_limit_bytes=vmem_bytes),
        cost_estimate=pl.CostEstimate(
            flops=2 * lane * full * 6 * lane * 2, bytes_accessed=16 * lane * full, transcendentals=0
        ),
        name="forward_lines",
    )(wavefield, lane_twiddle(-1, 1.0), right_table(-1))


def phase_kernel(angular_ref, out_ref):
    place = lax.axis_index("slab") % half_radix
    scale = 2.0 * math.pi / full
    lanes = lax.broadcasted_iota(jnp.int32, (32, lane), 1) * radix + place * 2
    seconds = []
    for c in range(2):
        column = lanes + c
        second = jnp.minimum(column, full - column).astype(jnp.float32) * scale
        seconds.append(second * second)
    row = lax.broadcasted_iota(jnp.int32, (32, lane), 0)
    squares = []
    for speed in ref_speeds:
        number = angular_ref[0] * np.float32(1.0 / np.float32(speed))
        squares.append(number * number)

    def chunk(index, carry):
        k = index // 4
        begin = pl.multiple_of((index % 4) * 32, 32)
        here = pl.ds(begin, 32)
        there = pl.ds(pl.multiple_of(k * lane, lane), lane)
        position = (row + begin) * radix + k
        first = jnp.minimum(position, full - position).astype(jnp.float32) * scale
        for c in range(2):
            wave_square = first * first + seconds[c]
            for j in range(len(ref_speeds)):
                vertical = squares[j] - wave_square
                root = jnp.sqrt(jnp.abs(vertical))
                moving = vertical >= 0.0
                out_ref[c, j, 0, here, there] = jnp.where(moving, horner(cos_series, vertical), jnp.exp(-root))
                out_ref[c, j, 1, here, there] = jnp.where(moving, root * horner(sinc_series, vertical), 0.0)
        return carry

    lax.fori_loop(0, radix * 4, chunk, 0)


def phase_call(frequencies):
    count = len(ref_speeds)
    return pl.pallas_call(
        phase_kernel,
        in_specs=[pl.BlockSpec(memory_space=pltpu.SMEM)],
        out_specs=pl.BlockSpec(memory_space=pltpu.VMEM),
        out_shape=jax.ShapeDtypeStruct((2, count, 2, lane, full), jnp.float32),
        compiler_params=pltpu.CompilerParams(vmem_limit_bytes=phase_vmem_bytes),
        cost_estimate=pl.CostEstimate(flops=120 * count * lane * full, bytes_accessed=16 * count * lane * full, transcendentals=0),
        name="phase_factors",
    )(frequencies)


def circle(index, modulus):
    half = modulus // 2
    angle = (((index + half) & (modulus - 1)) - half).astype(jnp.float32) * (2.0 * math.pi / modulus)
    square = angle * angle
    return horner(circle_cos, square), angle * horner(circle_sin, square)


def put_matrix(table_ref, cosine, sine, turned_over):
    for top, blocks_now in enumerate(((cosine, sine), (-sine, cosine))):
        for place, values in enumerate(blocks_now):
            upper, lower = halves(values)
            for third, part in enumerate((upper, upper, lower)):
                if turned_over:
                    table_ref[tile(place), tile(2 * third + top)] = part
                else:
                    table_ref[tile(2 * third + top), tile(place)] = part


def unit_matrix():
    row = lax.broadcasted_iota(jnp.int32, (lane, lane), 0)
    column = lax.broadcasted_iota(jnp.int32, (lane, lane), 1)
    return circle(row * column, lane)


def build_matrices(ahead_table_ref, back_table_ref):
    cosine, sine = unit_matrix()
    put_matrix(ahead_table_ref, cosine, -sine, True)
    put_matrix(back_table_ref, cosine * (1.0 / full), sine * (1.0 / full), True)


def build_turns(turn_ref, direction, scale):
    for k in range(radix):
        place = lax.broadcasted_iota(jnp.int32, (8, lane), 1)
        cosine, sine = circle(place * k, full)
        turn_ref[k, 0] = cosine * scale
        turn_ref[k, 1] = sine * (direction * scale)


def rows_kernel(
    c, apart, in_ref, phase_ref, *refs,
):
    outs = half_radix if apart else 1
    out_refs, refs = refs[:outs], refs[outs:]
    (
        work_ref, spec_ref, turn_ref, column_ref, ahead_table_ref, back_table_ref,
        factor_ref, field_ref, factor_sem, field_sem,
    ) = refs
    place = lax.axis_index("slab") % half_radix
    begin = lax.axis_index("slab") // half_radix * half_radix
    count = len(ref_speeds)

    def factor_copy(t):
        return pltpu.make_async_copy(phase_ref.at[c, t], factor_ref.at[t], factor_sem.at[t])

    def field_copies(t):
        if not apart:
            return [pltpu.make_async_copy(field_ref.at[t % 2], out_refs[0].at[:, t], field_sem.at[t % 2, 0])]
        return [
            pltpu.make_async_copy(field_ref.at[t % 2, place ^ k], out_refs[k].at[t], field_sem.at[t % 2, k])
            for k in range(half_radix)
        ]

    for t in range(count):
        factor_copy(t).start()

    row = lax.broadcasted_iota(jnp.int32, (lane, lane), 0)
    power = lax.broadcasted_iota(jnp.int32, (lane, lane), 1) & (radix - 1)
    cosine, sine = circle(row * power, full)
    column_ref[0] = cosine
    column_ref[1] = -sine
    build_matrices(ahead_table_ref, back_table_ref)

    for block in range(blocks):

        def rows(index, carry):
            local = pl.multiple_of(index * 8, 8)
            pair = (pl.ds(local, 8), pl.ds(local + row_block, 8))
            here = pl.ds(pl.multiple_of(local + block * row_block, 8), 8)
            there = pl.ds(pl.multiple_of(local + block * row_block + lane, 8), 8)
            parts = sixteen([tuple(in_ref[begin ^ s, block, rows_now, :] for rows_now in pair) for s in range(radix)], -1)
            columns = (column_ref[0, here, :], column_ref[1, here, :])
            for k in range(radix):
                turn = tuple(jnp.broadcast_to(part[:, k : k + 1], (8, lane)) for part in columns)
                turn_ref[k, 0, here, :] = turn[0]
                turn_ref[k, 1, here, :] = turn[1]
                re, im = times(parts[k], turn)
                work_ref[0, here, tile(k)] = re
                work_ref[0, there, tile(k)] = im
            return carry

        lax.fori_loop(0, row_block // 8, rows, 0, unroll=2)

    def shifted(t, columns, spectrum):
        re, im = times(
            (spectrum[0:lane], spectrum[lane : 2 * lane]),
            (factor_ref[t, 0, :, columns], factor_ref[t, 1, :, columns]),
        )
        work_ref[(t + 1) % 2, :, columns] = left_product(
            back_table_ref[...], jnp.concatenate([re, im], axis=0)
        )

    def back(t, index):
        here = pl.ds(pl.multiple_of(index * 8, 8), 8)
        there = pl.ds(pl.multiple_of(index * 8 + lane, 8), 8)
        slot = (t + 1) % 2
        parts = sixteen(
            [
                conjugate_times(
                    (work_ref[slot, here, tile(k)], work_ref[slot, there, tile(k)]),
                    (turn_ref[k, 0, here, :], turn_ref[k, 1, here, :]),
                )
                for k in range(radix)
            ],
            1,
        )
        for s in range(half_radix):
            field_ref[t % 2, s, 0, here, :] = parts[s][0]
            field_ref[t % 2, s, 1, here, :] = parts[s][1]

    def pair_columns(index):
        return pl.ds(pl.multiple_of(index * 2 * lane, 2 * lane), 2 * lane)

    factor_copy(0).wait()

    def first(index, carry):
        columns = pair_columns(index)
        spectrum = left_product(ahead_table_ref[...], work_ref[0, :, columns])
        spec_ref[:, columns] = spectrum
        shifted(0, columns, spectrum)
        return carry

    lax.fori_loop(0, radix // 2, first, 0, unroll=True)

    for t in range(count):
        if t + 1 < count:
            factor_copy(t + 1).wait()
        if t >= 2:
            for copy in field_copies(t - 2):
                copy.wait()

        def both(index, carry):
            if t + 1 < count:
                columns = pair_columns(index)
                shifted(t + 1, columns, spec_ref[:, columns])
            back(t, 2 * index)
            back(t, 2 * index + 1)
            return carry

        lax.fori_loop(0, radix // 2, both, 0, unroll=True)
        for copy in field_copies(t):
            copy.start()

    for t in range(count - 2, count):
        for copy in field_copies(t):
            copy.wait()


def rows_call(c, apart, arrived, phase):
    count = len(ref_speeds)
    in_vmem = pl.BlockSpec(memory_space=pltpu.VMEM)
    in_hbm = pl.BlockSpec(memory_space=pltpu.HBM)
    return pl.pallas_call(
        functools.partial(rows_kernel, c, apart),
        in_specs=[in_vmem, in_hbm],
        out_specs=[in_hbm] * half_radix if apart else in_hbm,
        out_shape=[jax.ShapeDtypeStruct((count, 2, lane, lane), jnp.float32)] * half_radix
        if apart
        else jax.ShapeDtypeStruct((half_radix, count, 2, lane, lane), jnp.float32),
        scratch_shapes=[
            pltpu.VMEM((2, 2 * lane, full), jnp.float32),
            pltpu.VMEM((2 * lane, full), jnp.float32),
            pltpu.VMEM((radix, 2, lane, lane), jnp.float32),
            pltpu.VMEM((2, lane, lane), jnp.float32),
            pltpu.VMEM((2 * lane, 6 * lane), jnp.bfloat16),
            pltpu.VMEM((2 * lane, 6 * lane), jnp.bfloat16),
            pltpu.VMEM((3, 2, lane, full), jnp.float32),
            pltpu.VMEM((2, half_radix, 2, lane, lane), jnp.float32),
            pltpu.SemaphoreType.DMA((3,)),
            pltpu.SemaphoreType.DMA((2, half_radix)),
        ],
        compiler_params=pltpu.CompilerParams(vmem_limit_bytes=rows_vmem_bytes),
        cost_estimate=pl.CostEstimate(
            flops=8 * 2 * 2 * lane * 6 * lane * full, bytes_accessed=28 * 8 * lane * full, transcendentals=0
        ),
        name="rows_there_and_back",
    )(arrived, phase)


def blend_kernel(angular_ref, bracket_ref, far_ref, swapped_ref, *refs):
    near_refs, out_ref, tile_ref = refs[:-2], refs[-2], refs[-1]
    shot, device = lax.axis_index("shot"), lax.axis_index("slab")
    half = lane // 2
    for k in range(half_radix):
        tile_ref[pl.ds(pl.multiple_of(shot * half, half), half), :] = far_ref[k]
        tile_ref[pl.ds(pl.multiple_of((1 - shot) * half, half), half), :] = swapped_ref[k]
        for source, speed in ((device ^ k, near_refs[k][0:lane, :]), (device ^ far ^ k, tile_ref[...])):
            there = pl.ds(pl.multiple_of(source * lane, lane), lane)
            speed = jnp.transpose(speed)
            first = bracket_ref[0, :, there] == 0
            low = jnp.where(first, ref_speeds[0], ref_speeds[1])
            width = jnp.where(first, 1.0 / (ref_speeds[1] - ref_speeds[0]), 1.0 / (ref_speeds[2] - ref_speeds[1]))
            fraction = (speed - low) * width
            low_slowness = jnp.where(first, 1.0 / ref_speeds[0], 1.0 / ref_speeds[1])
            high_slowness = jnp.where(first, 1.0 / ref_speeds[1], 1.0 / ref_speeds[2])
            residual = 1.0 / speed - ((1.0 - fraction) * low_slowness + fraction * high_slowness)
            angle = angular_ref[0] * step_length * residual
            square = angle * angle
            cosine = horner([1.0, -1 / 2, 1 / 24, -1 / 720, 1 / 40320], square)
            sine = angle * horner([1.0, -1 / 6, 1 / 120, -1 / 5040, 1 / 362880], square)
            out_ref[0, :, there] = fraction + jnp.where(first, 0.0, 1.0)
            out_ref[1, :, there] = cosine
            out_ref[2, :, there] = sine


def blend_call(frequencies, bracket, *speeds):
    in_vmem = pl.BlockSpec(memory_space=pltpu.VMEM)
    return pl.pallas_call(
        blend_kernel,
        in_specs=[pl.BlockSpec(memory_space=pltpu.SMEM)] + [in_vmem] * (1 + len(speeds)),
        out_specs=in_vmem,
        out_shape=jax.ShapeDtypeStruct((3, lane, full), jnp.float32),
        scratch_shapes=[pltpu.VMEM((lane, lane), jnp.float32)],
        compiler_params=pltpu.CompilerParams(vmem_limit_bytes=vmem_bytes),
        cost_estimate=pl.CostEstimate(flops=60 * lane * full, bytes_accessed=24 * lane * full, transcendentals=0),
        name="blend_factors",
    )(frequencies, bracket, *speeds)


strip = 32


def finish_kernel(odd_ref, blend_ref, *refs):
    even_refs, (out_ref, image_ref, work_ref, turn_ref, table_ref) = refs[:half_radix], refs[half_radix:]
    count = len(ref_speeds)
    place = lax.axis_index("slab") % half_radix

    @pl.when(pl.program_id(0) == 0)
    def _():
        build_turns(turn_ref, 1.0, 1.0 / full)
        put_matrix(table_ref, *unit_matrix(), False)

    for j in range(count):
        odds = jnp.concatenate([odd_ref[:, j, 0], odd_ref[:, j, 1]], axis=2).reshape(half_radix * strip, 2 * lane)
        evens = jnp.concatenate([jnp.concatenate([ref[j, 0], ref[j, 1]], axis=1) for ref in even_refs], axis=0)
        odd, even = right_product(odds, table_ref[...]), right_product(evens, table_ref[...])
        for i in range(half_radix):
            here = slice(i * strip, (i + 1) * strip)
            work_ref[j, 2 * i + 1] = odd[here]
            work_ref[j, 2 * (place ^ i)] = even[here]

    def rows(index, carry):
        here = pl.ds(pl.multiple_of(index * 8, 8), 8)
        for j in range(count):
            parts = sixteen(
                [
                    times(
                        (work_ref[j, k, here, 0:lane], work_ref[j, k, here, lane : 2 * lane]),
                        (turn_ref[k, 0], turn_ref[k, 1]),
                    )
                    for k in range(radix)
                ],
                1,
            )
            for s in range(radix):
                place = blend_ref[0, here, tile(s)]
                if j == 0:
                    weight = jnp.maximum(1.0 - place, 0.0)
                elif j == 1:
                    weight = 1.0 - jnp.abs(place - 1.0)
                else:
                    weight = jnp.maximum(place - 1.0, 0.0)
                re, im = parts[s][0] * weight, parts[s][1] * weight
                if j > 0:
                    re, im = re + out_ref[0, 0, here, tile(s)], im + out_ref[0, 1, here, tile(s)]
                if j == count - 1:
                    re, im = times((re, im), (blend_ref[1, here, tile(s)], blend_ref[2, here, tile(s)]))
                    image_ref[0, here, tile(s)] = re
                out_ref[0, 0, here, tile(s)] = re
                out_ref[0, 1, here, tile(s)] = im
        return carry

    lax.fori_loop(0, strip // 8, rows, 0, unroll=True)


def finish_call(evens, odd, blend):
    count = len(ref_speeds)
    return pl.pallas_call(
        finish_kernel,
        grid=(lane // strip,),
        in_specs=[
            pl.BlockSpec((half_radix, count, 2, strip, lane), lambda g: (0, 0, 0, g, 0)),
            pl.BlockSpec((3, strip, full), lambda g: (0, g, 0)),
            *[pl.BlockSpec((count, 2, strip, lane), lambda g: (0, 0, g, 0))] * half_radix,
        ],
        out_specs=[
            pl.BlockSpec((1, 2, strip, full), lambda g: (0, 0, g, 0)),
            pl.BlockSpec((1, strip, full), lambda g: (0, g, 0)),
        ],
        out_shape=[
            jax.ShapeDtypeStruct((1, 2, lane, full), jnp.float32),
            jax.ShapeDtypeStruct((1, lane, full), jnp.float32),
        ],
        scratch_shapes=[
            pltpu.VMEM((count, radix, strip, 2 * lane), jnp.float32),
            pltpu.VMEM((radix, 2, 8, lane), jnp.float32),
            pltpu.VMEM((6 * lane, 2 * lane), jnp.bfloat16),
        ],
        compiler_params=pltpu.CompilerParams(vmem_limit_bytes=finish_vmem_bytes),
        name="inverse_lines",
    )(odd, blend, *evens)


def exchange(values, group):
    groups = [list(range(begin, begin + group)) for begin in range(0, radix, group)]
    return lax.all_to_all(values, "slab", split_axis=0, concat_axis=0, tiled=True, axis_index_groups=groups)


def partners(distance):
    return [(index, index ^ distance) for index in range(radix)]


def speeds_near(velocity):
    shot, device = lax.axis_index("shot"), lax.axis_index("slab")
    tiles = []
    for k in range(half_radix):
        near = lax.dynamic_slice(velocity[0], (0, (device ^ k) * lane), (lane, lane))
        beyond = lax.dynamic_slice(velocity[0], (shot * (lane // 2), (device ^ k ^ far) * lane), (lane // 2, lane))
        both = jnp.concatenate([near, beyond])
        tiles.append(lax.ppermute(both, "slab", partners(k)) if k else both)
    return tiles


def per_device(wavefield, frequencies, velocity, bracket):
    even = lines_call(0, wavefield)
    velocity, even, wavefield = lax.optimization_barrier((velocity, even, wavefield))
    even = exchange(even, radix)
    odd = lines_call(1, wavefield)
    speeds = speeds_near(velocity)
    beyond = jnp.stack([tile_now[lane:] for tile_now in speeds])
    phase = phase_call(frequencies)
    beyond, phase, even, odd = lax.optimization_barrier((beyond, phase, even, odd))
    odd = exchange(odd, radix)
    evens = rows_call(0, True, even, phase)
    evens = [part if k == 0 else lax.ppermute(part, "slab", partners(k)) for k, part in enumerate(evens)]
    beyond, _ = lax.optimization_barrier((beyond, odd))
    beyond = lax.ppermute(beyond, "slab", partners(far))
    odd = rows_call(1, False, odd, phase)
    evens, beyond, odd = lax.optimization_barrier((evens, beyond, odd))
    odd = exchange(odd, half_radix)
    swapped = lax.ppermute(beyond, "shot", [(0, 1), (1, 0)])
    blend = blend_call(frequencies, bracket, beyond, swapped, *speeds)
    propagated, image = finish_call(evens, odd, blend)
    return propagated, image


def fits(mesh, shapes):
    wavefield, velocity = shapes
    return (
        mesh.shape["slab"] == radix
        and mesh.shape["shot"] == 2
        and wavefield == (2, 2, full, full)
        and velocity == (1, full, full)
    )


def solution(mesh):
    def program(wavefield, frequencies, velocity, bracket):
        small = fits(mesh, (wavefield.shape, velocity.shape))
        return jax.shard_map(
            per_device if small else per_device_general,
            mesh=mesh,
            in_specs=(
                P("shot", None, "slab", None),
                P("shot"),
                P(None, "slab", None),
                P(None, "slab", None),
            ),
            out_specs=(P("shot", None, "slab", None), P("shot", "slab", None)),
            check_vma=False,
        )(wavefield, frequencies, velocity, bracket)

    return program
```

```python
import functools
import math

import jax
import jax.numpy as jnp
import ml_dtypes
import numpy as np
from jax import lax
from jax.experimental import pallas as pl
from jax.experimental.pallas import tpu as pltpu
from jax.sharding import PartitionSpec as P

ref_speeds = (1.0, 1.5, 2.25)
step_length = 1.0
highest = lax.Precision.HIGHEST


def dft_table(height, breadth, modulus, direction):
    down_index = lax.iota(jnp.int32, height)[:, None]
    across_index = lax.iota(jnp.int32, breadth)[None, :]
    angles = (down_index * across_index % modulus).astype(jnp.float32) * (
        direction * 2.0 * math.pi / modulus
    )
    return (jnp.cos(angles), jnp.sin(angles))


def contract(pattern, left_pair, right_pair):

    def product(one_side, other_side):
        return jnp.einsum(pattern, one_side, other_side, precision=highest)

    return (
        product(left_pair[0], right_pair[0]) - product(left_pair[1], right_pair[1]),
        product(left_pair[0], right_pair[1]) + product(left_pair[1], right_pair[0]),
    )


def rotate(values, factor_pair):
    return (
        values[0] * factor_pair[0] - values[1] * factor_pair[1],
        values[0] * factor_pair[1] + values[1] * factor_pair[0],
    )


def forward_lines(fields):
    item_count, row_count, extent = fields[0].shape
    devices = lax.axis_size("slab")
    line_count = extent // devices
    reshaped = tuple(
        (part_now.reshape(item_count, row_count, line_count, devices) for part_now in fields)
    )
    section_one = contract(
        "nrab,ak->nrkb", reshaped, dft_table(line_count, line_count, line_count, -1.0)
    )
    twisted = rotate(
        section_one,
        tuple((turning[None, None] for turning in dft_table(line_count, devices, extent, -1.0))),
    )
    section_two = contract("nrkb,bq->nkqr", twisted, dft_table(devices, devices, devices, -1.0))
    return tuple(
        (part_now.reshape(item_count, line_count, devices * row_count) for part_now in section_two)
    )


def forward_rows(fields):
    item_count, line_count, extent = fields[0].shape
    devices = lax.axis_size("slab")
    row_count = extent // devices
    reshaped = tuple(
        (part_now.reshape(item_count, line_count, devices, row_count) for part_now in fields)
    )
    section_one = contract("ncab,ak->nckb", reshaped, dft_table(devices, devices, devices, -1.0))
    twisted = rotate(
        section_one,
        tuple((turning[None, None] for turning in dft_table(devices, row_count, extent, -1.0))),
    )
    section_two = contract(
        "nckb,bq->nckq", twisted, dft_table(row_count, row_count, row_count, -1.0)
    )
    return tuple((part_now.reshape(item_count, line_count, extent) for part_now in section_two))


def inverse_rows(fields):
    item_count, line_count, extent = fields[0].shape
    devices = lax.axis_size("slab")
    row_count = extent // devices
    reshaped = tuple(
        (part_now.reshape(item_count, line_count, devices, row_count) for part_now in fields)
    )
    section_one = contract(
        "nckq,bq->nckb", reshaped, dft_table(row_count, row_count, row_count, 1.0)
    )
    twisted = rotate(
        section_one,
        tuple((turning[None, None] for turning in dft_table(devices, row_count, extent, 1.0))),
    )
    section_two = contract("nckb,ak->ncab", twisted, dft_table(devices, devices, devices, 1.0))
    return tuple(
        (
            part_now.reshape(item_count, line_count, extent) * (1.0 / extent)
            for part_now in section_two
        )
    )


def inverse_lines(fields):
    item_count, line_count, extent = fields[0].shape
    devices = lax.axis_size("slab")
    row_count = extent // devices
    total_lines = line_count * devices
    reshaped = tuple(
        (part_now.reshape(item_count, line_count, devices, row_count) for part_now in fields)
    )
    section_one = contract("nkqr,bq->nkbr", reshaped, dft_table(devices, devices, devices, 1.0))
    twisted = rotate(
        section_one,
        tuple(
            (
                turning[None, :, :, None]
                for turning in dft_table(line_count, devices, total_lines, 1.0)
            )
        ),
    )
    section_two = contract(
        "nkbr,ak->nrab", twisted, dft_table(line_count, line_count, line_count, 1.0)
    )
    return tuple(
        (
            part_now.reshape(item_count, row_count, total_lines) * (1.0 / total_lines)
            for part_now in section_two
        )
    )


def phase_shift(values, wave_square, angular):
    slowness = 1.0 / jnp.array(ref_speeds, jnp.float32)
    wave_number = angular[:, None] * slowness[None, :]
    vertical = (wave_number * wave_number)[:, :, None, None] - wave_square[None, None]
    root_abs = jnp.sqrt(jnp.abs(vertical))
    real_part = jnp.where(
        vertical >= 0, jnp.cos(step_length * root_abs), jnp.exp(-step_length * root_abs)
    )
    imag_part = jnp.where(vertical >= 0, jnp.sin(step_length * root_abs), 0.0)
    shifted = rotate((values[0][:, None], values[1][:, None]), (real_part, imag_part))
    item_count = values[0].shape[0]
    return tuple(
        (
            part_now.reshape((item_count * len(ref_speeds),) + values[0].shape[1:])
            for part_now in shifted
        )
    )


def weights(speed_grid, chosen):
    speeds = jnp.array(ref_speeds, jnp.float32)
    lower_speed = jnp.zeros_like(speed_grid)
    upper_speed = jnp.zeros_like(speed_grid)
    for ref_index in range(len(ref_speeds) - 1):
        lower_speed = lower_speed + jnp.where(chosen == ref_index, speeds[ref_index], 0.0)
        upper_speed = upper_speed + jnp.where(chosen == ref_index, speeds[ref_index + 1], 0.0)
    fraction = (speed_grid - lower_speed) / (upper_speed - lower_speed)
    residual_phase = 1.0 / speed_grid - ((1.0 - fraction) / lower_speed + fraction / upper_speed)
    coefficients = []
    for ref_index in range(len(ref_speeds)):
        coefficients.append(
            jnp.where(chosen == ref_index, 1.0 - fraction, 0.0)
            + jnp.where(chosen == ref_index - 1, fraction, 0.0)
        )
    return (jnp.stack(coefficients), residual_phase)


def advance(fields, angular, coefficients, residual_phase, spec_square):
    item_count, row_count, extent = fields[0].shape
    prepared = forward_lines(fields)
    spectrum = forward_rows(
        (
            lax.all_to_all(prepared[0], "slab", split_axis=2, concat_axis=2, tiled=True),
            lax.all_to_all(prepared[1], "slab", split_axis=2, concat_axis=2, tiled=True),
        )
    )
    returned = inverse_rows(phase_shift(spectrum, spec_square, angular))
    waves = inverse_lines(
        (
            lax.all_to_all(returned[0], "slab", split_axis=2, concat_axis=2, tiled=True),
            lax.all_to_all(returned[1], "slab", split_axis=2, concat_axis=2, tiled=True),
        )
    )
    ref_count = len(ref_speeds)
    wave_real = waves[0].reshape(item_count, ref_count, row_count, extent)
    wave_imag = waves[1].reshape(item_count, ref_count, row_count, extent)
    blended_real = jnp.sum(coefficients[None] * wave_real, axis=1)
    blended_imag = jnp.sum(coefficients[None] * wave_imag, axis=1)
    angles = angular[:, None, None] * step_length * residual_phase[None]
    return rotate((blended_real, blended_imag), (jnp.cos(angles), jnp.sin(angles)))


def folded(indices, modulus):
    return jnp.minimum(indices, modulus - indices).astype(jnp.float32) * (2.0 * math.pi / modulus)


def per_device_general(wavefield, frequencies, velocity, bracket):
    devices = lax.axis_size("slab")
    device_index = lax.axis_index("slab")
    row_count = wavefield.shape[2]
    extent_y = wavefield.shape[3]
    extent_x = row_count * devices
    line_count = extent_y // devices
    speed_columns = lax.all_to_all(velocity, "slab", split_axis=2, concat_axis=1, tiled=True)
    speed_rows = jnp.transpose(speed_columns, (0, 2, 1))
    column = lax.iota(jnp.int32, extent_x)
    line_index = lax.iota(jnp.int32, line_count)
    spec_first = folded(column // row_count + devices * (column % row_count), extent_x)
    spec_second = folded(device_index * line_count + line_index, extent_y)
    spec_square = (
        spec_first[None, :] * spec_first[None, :] + spec_second[:, None] * spec_second[:, None]
    )
    current = (wavefield[:, 0], wavefield[:, 1])
    coefficients, residual_phase = weights(speed_rows[0], bracket[0])
    single = (current[0], current[1])
    pieces = [advance(single, frequencies, coefficients, residual_phase, spec_square)]
    current = (
        jnp.concatenate([piece[0] for piece in pieces], axis=0),
        jnp.concatenate([piece[1] for piece in pieces], axis=0),
    )
    image_rows = [jnp.sum(current[0], axis=0)]
    return (jnp.stack(current, axis=1), jnp.stack(image_rows))


radix = 16
lane = 128
full = radix * lane
row_block = 64
half_radix = radix // 2
far = half_radix
blocks = lane // row_block
piece = 2 * row_block
vmem_bytes = 56 * 1024 * 1024
rows_vmem_bytes = 50 * 1024 * 1024
phase_vmem_bytes = 56 * 1024 * 1024
finish_vmem_bytes = 48 * 1024 * 1024


def split_table(table):
    upper = table.astype(ml_dtypes.bfloat16)
    lower = (table - upper.astype(np.float64)).astype(ml_dtypes.bfloat16)
    return upper, lower


def line_matrices(direction):
    angles = 2.0 * np.pi / lane * (np.outer(np.arange(lane), np.arange(lane)) % lane)
    cosine, sine = np.cos(angles), direction * np.sin(angles)
    return np.block([[cosine, sine], [-sine, cosine]])


def right_table(direction):
    upper, lower = split_table(line_matrices(direction))
    return np.concatenate([upper, upper, lower], axis=0)


def twiddle(direction, scale):
    angles = 2.0 * np.pi / full * np.outer(np.arange(radix), np.arange(lane))
    return np.stack([np.cos(angles), direction * np.sin(angles)], axis=1) * scale


def lane_twiddle(direction, scale):
    table = twiddle(direction, scale)[:, :, None, :]
    return np.ascontiguousarray(np.broadcast_to(table, (radix, 2, 8, lane))).astype(np.float32)


def root_series(offset, degree, end):
    nodes = np.polynomial.chebyshev.Chebyshev.interpolate(
        lambda q: np.sinc(np.sqrt(q) / np.pi) if offset else np.cos(np.sqrt(q)), degree, domain=[0.0, end]
    )
    return [float(value) for value in nodes.convert(kind=np.polynomial.Polynomial).coef]


cos_series, sinc_series = root_series(0, 7, 9.0), root_series(1, 6, 9.0)
circle_cos, circle_sin = root_series(0, 8, np.pi**2), root_series(1, 7, np.pi**2)


def horner(series, argument):
    total = jnp.full_like(argument, series[-1])
    for value in series[-2::-1]:
        total = total * argument + value
    return total


def times(left, right):
    return left[0] * right[0] - left[1] * right[1], left[0] * right[1] + left[1] * right[0]


def conjugate_times(left, right):
    return left[0] * right[0] + left[1] * right[1], left[1] * right[0] - left[0] * right[1]


def quarter(values, direction):
    (a_re, a_im), (b_re, b_im), (c_re, c_im), (d_re, d_im) = values
    p_re, p_im, m_re, m_im = a_re + c_re, a_im + c_im, a_re - c_re, a_im - c_im
    q_re, q_im, n_re, n_im = b_re + d_re, b_im + d_im, b_re - d_re, b_im - d_im
    if direction < 0:
        turn_re, turn_im = n_im, -n_re
    else:
        turn_re, turn_im = -n_im, n_re
    return [
        (p_re + q_re, p_im + q_im),
        (m_re + turn_re, m_im + turn_im),
        (p_re - q_re, p_im - q_im),
        (m_re - turn_re, m_im - turn_im),
    ]


def turned(value, power, direction):
    re, im = value
    power %= 16
    if power == 0:
        return value
    if power == 4:
        return (-direction * im, direction * re) if direction < 0 else (-im, re)
    half = math.sqrt(0.5)
    if power == 2:
        return ((re - direction * im) * half, (im + direction * re) * half)
    if power == 6:
        return ((-re - direction * im) * half, (direction * re - im) * half)
    cosine, sine = math.cos(math.pi * power / 8), direction * math.sin(math.pi * power / 8)
    return re * cosine - im * sine, re * sine + im * cosine


def sixteen(values, direction):
    first = [quarter([values[4 * a + b] for a in range(4)], direction) for b in range(4)]
    result = [None] * 16
    for c in range(4):
        outs = quarter([turned(first[b][c], b * c, direction) for b in range(4)], direction)
        for d in range(4):
            result[c + 4 * d] = outs[d]
    return result


def eight(values, direction):
    first = [quarter([values[2 * a + b] for a in range(4)], direction) for b in range(2)]
    result = [None] * 8
    for c in range(4):
        re, im = turned(first[1][c], 2 * c, direction)
        result[c] = (first[0][c][0] + re, first[0][c][1] + im)
        result[c + 4] = (first[0][c][0] - re, first[0][c][1] - im)
    return result


def halves(values):
    upper = values.astype(jnp.bfloat16)
    lower = (values - upper.astype(jnp.float32)).astype(jnp.bfloat16)
    return upper, lower


def right_product(values, table):
    upper, lower = halves(values)
    return jnp.dot(jnp.concatenate([upper, lower, upper], axis=1), table, preferred_element_type=jnp.float32)


def left_product(table, values):
    upper, lower = halves(values)
    return jnp.dot(table, jnp.concatenate([upper, lower, upper], axis=0), preferred_element_type=jnp.float32)


def tile(index):
    return slice(index * lane, (index + 1) * lane)


def lines_kernel(c, field_ref, turn_ref, table_ref, out_ref, work_ref):
    def rows(index, carry):
        here = pl.ds(pl.multiple_of(index * 8, 8), 8)
        parts = sixteen(
            [(field_ref[0, 0, here, tile(j)], field_ref[0, 1, here, tile(j)]) for j in range(radix)], -1
        )
        for i in range(half_radix):
            k = 2 * i + c
            re, im = times(parts[k], (turn_ref[k, 0], turn_ref[k, 1]))
            work_ref[i, here, 0:lane] = re
            work_ref[i, here, lane : 2 * lane] = im
        return carry

    lax.fori_loop(0, row_block // 8, rows, 0, unroll=True)
    lines = right_product(work_ref[...].reshape(half_radix * row_block, 2 * lane), table_ref[...])
    for i in range(half_radix):
        block = lines[i * row_block : (i + 1) * row_block]
        for half in range(2):
            out_ref[half * half_radix + i, 0, 0:row_block] = block[:, 0:lane]
            out_ref[half * half_radix + i, 0, row_block : 2 * row_block] = block[:, lane : 2 * lane]


def lines_call(c, wavefield):
    return pl.pallas_call(
        functools.partial(lines_kernel, c),
        grid=(blocks,),
        in_specs=[
            pl.BlockSpec((1, 2, row_block, full), lambda g: (0, 0, g, 0)),
            pl.BlockSpec((radix, 2, 8, lane), lambda g: (0, 0, 0, 0)),
            pl.BlockSpec((6 * lane, 2 * lane), lambda g: (0, 0)),
        ],
        out_specs=pl.BlockSpec((radix, 1, piece, lane), lambda g: (0, g, 0, 0)),
        out_shape=jax.ShapeDtypeStruct((radix, blocks, piece, lane), jnp.float32),
        scratch_shapes=[pltpu.VMEM((half_radix, row_block, 2 * lane), jnp.float32)],
        compiler_params=pltpu.CompilerParams(vmem_limit_bytes=vmem_bytes),
        cost_estimate=pl.CostEstimate(
            flops=2 * lane * full * 6 * lane * 2, bytes_accessed=16 * lane * full, transcendentals=0
        ),
        name="forward_lines",
    )(wavefield, lane_twiddle(-1, 1.0), right_table(-1))


def phase_kernel(angular_ref, out_ref):
    place = lax.axis_index("slab") % half_radix
    scale = 2.0 * math.pi / full
    lanes = lax.broadcasted_iota(jnp.int32, (32, lane), 1) * radix + place * 2
    seconds = []
    for c in range(2):
        column = lanes + c
        second = jnp.minimum(column, full - column).astype(jnp.float32) * scale
        seconds.append(second * second)
    row = lax.broadcasted_iota(jnp.int32, (32, lane), 0)
    squares = []
    for speed in ref_speeds:
        number = angular_ref[0] * np.float32(1.0 / np.float32(speed))
        squares.append(number * number)

    def chunk(index, carry):
        k = index // 4
        begin = pl.multiple_of((index % 4) * 32, 32)
        here = pl.ds(begin, 32)
        there = pl.ds(pl.multiple_of(k * lane, lane), lane)
        position = (row + begin) * radix + k
        first = jnp.minimum(position, full - position).astype(jnp.float32) * scale
        for c in range(2):
            wave_square = first * first + seconds[c]
            for j in range(len(ref_speeds)):
                vertical = squares[j] - wave_square
                root = jnp.sqrt(jnp.abs(vertical))
                moving = vertical >= 0.0
                out_ref[c, j, 0, here, there] = jnp.where(moving, horner(cos_series, vertical), jnp.exp(-root))
                out_ref[c, j, 1, here, there] = jnp.where(moving, root * horner(sinc_series, vertical), 0.0)
        return carry

    lax.fori_loop(0, radix * 4, chunk, 0)


def phase_call(frequencies):
    count = len(ref_speeds)
    return pl.pallas_call(
        phase_kernel,
        in_specs=[pl.BlockSpec(memory_space=pltpu.SMEM)],
        out_specs=pl.BlockSpec(memory_space=pltpu.VMEM),
        out_shape=jax.ShapeDtypeStruct((2, count, 2, lane, full), jnp.float32),
        compiler_params=pltpu.CompilerParams(vmem_limit_bytes=phase_vmem_bytes),
        cost_estimate=pl.CostEstimate(flops=120 * count * lane * full, bytes_accessed=16 * count * lane * full, transcendentals=0),
        name="phase_factors",
    )(frequencies)


def circle(index, modulus):
    half = modulus // 2
    angle = (((index + half) & (modulus - 1)) - half).astype(jnp.float32) * (2.0 * math.pi / modulus)
    square = angle * angle
    return horner(circle_cos, square), angle * horner(circle_sin, square)


def put_matrix(table_ref, cosine, sine, turned_over):
    for top, blocks_now in enumerate(((cosine, sine), (-sine, cosine))):
        for place, values in enumerate(blocks_now):
            upper, lower = halves(values)
            for third, part in enumerate((upper, upper, lower)):
                if turned_over:
                    table_ref[tile(place), tile(2 * third + top)] = part
                else:
                    table_ref[tile(2 * third + top), tile(place)] = part


def unit_matrix():
    row = lax.broadcasted_iota(jnp.int32, (lane, lane), 0)
    column = lax.broadcasted_iota(jnp.int32, (lane, lane), 1)
    return circle(row * column, lane)


def build_matrices(ahead_table_ref, back_table_ref):
    cosine, sine = unit_matrix()
    put_matrix(ahead_table_ref, cosine, -sine, True)
    put_matrix(back_table_ref, cosine * (1.0 / full), sine * (1.0 / full), True)


def build_turns(turn_ref, direction, scale):
    for k in range(radix):
        place = lax.broadcasted_iota(jnp.int32, (8, lane), 1)
        cosine, sine = circle(place * k, full)
        turn_ref[k, 0] = cosine * scale
        turn_ref[k, 1] = sine * (direction * scale)


def rows_kernel(
    c, apart, in_ref, phase_ref, *refs,
):
    outs = half_radix if apart else 1
    out_refs, refs = refs[:outs], refs[outs:]
    (
        work_ref, spec_ref, turn_ref, column_ref, ahead_table_ref, back_table_ref,
        factor_ref, field_ref, factor_sem, field_sem,
    ) = refs
    place = lax.axis_index("slab") % half_radix
    begin = lax.axis_index("slab") // half_radix * half_radix
    count = len(ref_speeds)

    def factor_copy(t):
        return pltpu.make_async_copy(phase_ref.at[c, t], factor_ref.at[t], factor_sem.at[t])

    def field_copies(t):
        if not apart:
            return [pltpu.make_async_copy(field_ref.at[t % 2], out_refs[0].at[:, t], field_sem.at[t % 2, 0])]
        return [
            pltpu.make_async_copy(field_ref.at[t % 2, place ^ k], out_refs[k].at[t], field_sem.at[t % 2, k])
            for k in range(half_radix)
        ]

    for t in range(count):
        factor_copy(t).start()

    row = lax.broadcasted_iota(jnp.int32, (lane, lane), 0)
    power = lax.broadcasted_iota(jnp.int32, (lane, lane), 1) & (radix - 1)
    cosine, sine = circle(row * power, full)
    column_ref[0] = cosine
    column_ref[1] = -sine
    build_matrices(ahead_table_ref, back_table_ref)

    for block in range(blocks):

        def rows(index, carry):
            local = pl.multiple_of(index * 8, 8)
            pair = (pl.ds(local, 8), pl.ds(local + row_block, 8))
            here = pl.ds(pl.multiple_of(local + block * row_block, 8), 8)
            there = pl.ds(pl.multiple_of(local + block * row_block + lane, 8), 8)
            parts = sixteen([tuple(in_ref[begin ^ s, block, rows_now, :] for rows_now in pair) for s in range(radix)], -1)
            columns = (column_ref[0, here, :], column_ref[1, here, :])
            for k in range(radix):
                turn = tuple(jnp.broadcast_to(part[:, k : k + 1], (8, lane)) for part in columns)
                turn_ref[k, 0, here, :] = turn[0]
                turn_ref[k, 1, here, :] = turn[1]
                re, im = times(parts[k], turn)
                work_ref[0, here, tile(k)] = re
                work_ref[0, there, tile(k)] = im
            return carry

        lax.fori_loop(0, row_block // 8, rows, 0, unroll=2)

    def shifted(t, columns, spectrum):
        re, im = times(
            (spectrum[0:lane], spectrum[lane : 2 * lane]),
            (factor_ref[t, 0, :, columns], factor_ref[t, 1, :, columns]),
        )
        work_ref[(t + 1) % 2, :, columns] = left_product(
            back_table_ref[...], jnp.concatenate([re, im], axis=0)
        )

    def back(t, index):
        here = pl.ds(pl.multiple_of(index * 8, 8), 8)
        there = pl.ds(pl.multiple_of(index * 8 + lane, 8), 8)
        slot = (t + 1) % 2
        parts = sixteen(
            [
                conjugate_times(
                    (work_ref[slot, here, tile(k)], work_ref[slot, there, tile(k)]),
                    (turn_ref[k, 0, here, :], turn_ref[k, 1, here, :]),
                )
                for k in range(radix)
            ],
            1,
        )
        for s in range(half_radix):
            field_ref[t % 2, s, 0, here, :] = parts[s][0]
            field_ref[t % 2, s, 1, here, :] = parts[s][1]

    def pair_columns(index):
        return pl.ds(pl.multiple_of(index * 2 * lane, 2 * lane), 2 * lane)

    factor_copy(0).wait()

    def first(index, carry):
        columns = pair_columns(index)
        spectrum = left_product(ahead_table_ref[...], work_ref[0, :, columns])
        spec_ref[:, columns] = spectrum
        shifted(0, columns, spectrum)
        return carry

    lax.fori_loop(0, radix // 2, first, 0, unroll=True)

    for t in range(count):
        if t + 1 < count:
            factor_copy(t + 1).wait()
        if t >= 2:
            for copy in field_copies(t - 2):
                copy.wait()

        def both(index, carry):
            if t + 1 < count:
                columns = pair_columns(index)
                shifted(t + 1, columns, spec_ref[:, columns])
            back(t, 2 * index)
            back(t, 2 * index + 1)
            return carry

        lax.fori_loop(0, radix // 2, both, 0, unroll=True)
        for copy in field_copies(t):
            copy.start()

    for t in range(count - 2, count):
        for copy in field_copies(t):
            copy.wait()


def rows_call(c, apart, arrived, phase):
    count = len(ref_speeds)
    in_vmem = pl.BlockSpec(memory_space=pltpu.VMEM)
    in_hbm = pl.BlockSpec(memory_space=pltpu.HBM)
    return pl.pallas_call(
        functools.partial(rows_kernel, c, apart),
        in_specs=[in_vmem, in_hbm],
        out_specs=[in_hbm] * half_radix if apart else in_hbm,
        out_shape=[jax.ShapeDtypeStruct((count, 2, lane, lane), jnp.float32)] * half_radix
        if apart
        else jax.ShapeDtypeStruct((half_radix, count, 2, lane, lane), jnp.float32),
        scratch_shapes=[
            pltpu.VMEM((2, 2 * lane, full), jnp.float32),
            pltpu.VMEM((2 * lane, full), jnp.float32),
            pltpu.VMEM((radix, 2, lane, lane), jnp.float32),
            pltpu.VMEM((2, lane, lane), jnp.float32),
            pltpu.VMEM((2 * lane, 6 * lane), jnp.bfloat16),
            pltpu.VMEM((2 * lane, 6 * lane), jnp.bfloat16),
            pltpu.VMEM((3, 2, lane, full), jnp.float32),
            pltpu.VMEM((2, half_radix, 2, lane, lane), jnp.float32),
            pltpu.SemaphoreType.DMA((3,)),
            pltpu.SemaphoreType.DMA((2, half_radix)),
        ],
        compiler_params=pltpu.CompilerParams(vmem_limit_bytes=rows_vmem_bytes),
        cost_estimate=pl.CostEstimate(
            flops=8 * 2 * 2 * lane * 6 * lane * full, bytes_accessed=28 * 8 * lane * full, transcendentals=0
        ),
        name="rows_there_and_back",
    )(arrived, phase)


def blend_kernel(angular_ref, bracket_ref, far_ref, swapped_ref, *refs):
    near_refs, out_ref, tile_ref = refs[:-2], refs[-2], refs[-1]
    shot, device = lax.axis_index("shot"), lax.axis_index("slab")
    half = lane // 2
    for k in range(half_radix):
        tile_ref[pl.ds(pl.multiple_of(shot * half, half), half), :] = far_ref[k]
        tile_ref[pl.ds(pl.multiple_of((1 - shot) * half, half), half), :] = swapped_ref[k]
        for source, speed in ((device ^ k, near_refs[k][0:lane, :]), (device ^ far ^ k, tile_ref[...])):
            there = pl.ds(pl.multiple_of(source * lane, lane), lane)
            speed = jnp.transpose(speed)
            first = bracket_ref[0, :, there] == 0
            low = jnp.where(first, ref_speeds[0], ref_speeds[1])
            width = jnp.where(first, 1.0 / (ref_speeds[1] - ref_speeds[0]), 1.0 / (ref_speeds[2] - ref_speeds[1]))
            fraction = (speed - low) * width
            low_slowness = jnp.where(first, 1.0 / ref_speeds[0], 1.0 / ref_speeds[1])
            high_slowness = jnp.where(first, 1.0 / ref_speeds[1], 1.0 / ref_speeds[2])
            residual = 1.0 / speed - ((1.0 - fraction) * low_slowness + fraction * high_slowness)
            angle = angular_ref[0] * step_length * residual
            square = angle * angle
            cosine = horner([1.0, -1 / 2, 1 / 24, -1 / 720, 1 / 40320], square)
            sine = angle * horner([1.0, -1 / 6, 1 / 120, -1 / 5040, 1 / 362880], square)
            out_ref[0, :, there] = fraction + jnp.where(first, 0.0, 1.0)
            out_ref[1, :, there] = cosine
            out_ref[2, :, there] = sine


def blend_call(frequencies, bracket, *speeds):
    in_vmem = pl.BlockSpec(memory_space=pltpu.VMEM)
    return pl.pallas_call(
        blend_kernel,
        in_specs=[pl.BlockSpec(memory_space=pltpu.SMEM)] + [in_vmem] * (1 + len(speeds)),
        out_specs=in_vmem,
        out_shape=jax.ShapeDtypeStruct((3, lane, full), jnp.float32),
        scratch_shapes=[pltpu.VMEM((lane, lane), jnp.float32)],
        compiler_params=pltpu.CompilerParams(vmem_limit_bytes=vmem_bytes),
        cost_estimate=pl.CostEstimate(flops=60 * lane * full, bytes_accessed=24 * lane * full, transcendentals=0),
        name="blend_factors",
    )(frequencies, bracket, *speeds)


strip = 32


def add_class(c, blend_ref, work_ref, turn_ref, store):
    count = len(ref_speeds)

    def rows(index, carry):
        here = pl.ds(pl.multiple_of(index * 8, 8), 8)
        for j in range(count):
            parts = eight(
                [
                    times(
                        (work_ref[j, i, here, 0:lane], work_ref[j, i, here, lane : 2 * lane]),
                        (turn_ref[2 * i + c, 0], turn_ref[2 * i + c, 1]),
                    )
                    for i in range(half_radix)
                ],
                1,
            )
            if c:
                parts = [turned(part, q, 1) for q, part in enumerate(parts)]
            for s in range(radix):
                place = blend_ref[0, here, tile(s)]
                if j == 0:
                    weight = jnp.maximum(1.0 - place, 0.0)
                elif j == 1:
                    weight = 1.0 - jnp.abs(place - 1.0)
                else:
                    weight = jnp.maximum(place - 1.0, 0.0)
                if c and s >= half_radix:
                    weight = -weight
                re, im = parts[s % half_radix][0] * weight, parts[s % half_radix][1] * weight
                store(j, s, here, re, im)
        return carry

    lax.fori_loop(0, strip // 8, rows, 0, unroll=True)


def start_kernel(blend_ref, *refs):
    even_refs, (out_ref, work_ref, turn_ref, table_ref) = refs[:half_radix], refs[half_radix:]
    place = lax.axis_index("slab") % half_radix

    @pl.when(pl.program_id(0) == 0)
    def _():
        build_turns(turn_ref, 1.0, 1.0 / full)
        put_matrix(table_ref, *unit_matrix(), False)

    for j in range(len(ref_speeds)):
        values = jnp.concatenate([jnp.concatenate([ref[j, 0], ref[j, 1]], axis=1) for ref in even_refs], axis=0)
        product = right_product(values, table_ref[...])
        for k in range(half_radix):
            work_ref[j, place ^ k] = product[k * strip : (k + 1) * strip]

    def store(j, s, here, re, im):
        if j > 0:
            re, im = re + out_ref[0, here, tile(s)], im + out_ref[1, here, tile(s)]
        out_ref[0, here, tile(s)] = re
        out_ref[1, here, tile(s)] = im

    add_class(0, blend_ref, work_ref, turn_ref, store)


def finish_kernel(odd_ref, before_ref, blend_ref, out_ref, image_ref, work_ref, turn_ref, table_ref):
    count = len(ref_speeds)

    @pl.when(pl.program_id(0) == 0)
    def _():
        build_turns(turn_ref, 1.0, 1.0 / full)
        put_matrix(table_ref, *unit_matrix(), False)

    for j in range(count):
        values = jnp.concatenate([odd_ref[:, j, 0], odd_ref[:, j, 1]], axis=2)
        product = right_product(values.reshape(half_radix * strip, 2 * lane), table_ref[...])
        work_ref[j] = product.reshape(half_radix, strip, 2 * lane)

    def store(j, s, here, re, im):
        if j == 0:
            re, im = re + before_ref[0, here, tile(s)], im + before_ref[1, here, tile(s)]
        else:
            re, im = re + out_ref[0, 0, here, tile(s)], im + out_ref[0, 1, here, tile(s)]
        if j == count - 1:
            re, im = times((re, im), (blend_ref[1, here, tile(s)], blend_ref[2, here, tile(s)]))
            image_ref[0, here, tile(s)] = re
        out_ref[0, 0, here, tile(s)] = re
        out_ref[0, 1, here, tile(s)] = im

    add_class(1, blend_ref, work_ref, turn_ref, store)


def class_scratch():
    return [
        pltpu.VMEM((len(ref_speeds), half_radix, strip, 2 * lane), jnp.float32),
        pltpu.VMEM((radix, 2, 8, lane), jnp.float32),
        pltpu.VMEM((6 * lane, 2 * lane), jnp.bfloat16),
    ]


def start_call(evens, blend):
    count = len(ref_speeds)
    return pl.pallas_call(
        start_kernel,
        grid=(lane // strip,),
        in_specs=[pl.BlockSpec((1, strip, full), lambda g: (0, g, 0))]
        + [pl.BlockSpec((count, 2, strip, lane), lambda g: (0, 0, g, 0))] * half_radix,
        out_specs=pl.BlockSpec((2, strip, full), lambda g: (0, g, 0)),
        out_shape=jax.ShapeDtypeStruct((2, lane, full), jnp.float32),
        scratch_shapes=class_scratch(),
        compiler_params=pltpu.CompilerParams(vmem_limit_bytes=vmem_bytes),
        cost_estimate=pl.CostEstimate(
            flops=count * 2 * lane * full * 6 * lane, bytes_accessed=36 * lane * full, transcendentals=0
        ),
        name="inverse_lines_start",
    )(blend, *evens)


def finish_call(odd, before, blend):
    count = len(ref_speeds)
    return pl.pallas_call(
        finish_kernel,
        grid=(lane // strip,),
        in_specs=[
            pl.BlockSpec((half_radix, count, 2, strip, lane), lambda g: (0, 0, 0, g, 0)),
            pl.BlockSpec((2, strip, full), lambda g: (0, g, 0)),
            pl.BlockSpec((3, strip, full), lambda g: (0, g, 0)),
        ],
        out_specs=[
            pl.BlockSpec((1, 2, strip, full), lambda g: (0, 0, g, 0)),
            pl.BlockSpec((1, strip, full), lambda g: (0, g, 0)),
        ],
        out_shape=[
            jax.ShapeDtypeStruct((1, 2, lane, full), jnp.float32),
            jax.ShapeDtypeStruct((1, lane, full), jnp.float32),
        ],
        scratch_shapes=class_scratch(),
        compiler_params=pltpu.CompilerParams(vmem_limit_bytes=finish_vmem_bytes),
        name="inverse_lines",
    )(odd, before, blend)


def exchange(values, group):
    groups = [list(range(begin, begin + group)) for begin in range(0, radix, group)]
    return lax.all_to_all(values, "slab", split_axis=0, concat_axis=0, tiled=True, axis_index_groups=groups)


def partners(distance):
    return [(index, index ^ distance) for index in range(radix)]


def speeds_near(velocity):
    shot, device = lax.axis_index("shot"), lax.axis_index("slab")
    tiles = []
    for k in range(half_radix):
        near = lax.dynamic_slice(velocity[0], (0, (device ^ k) * lane), (lane, lane))
        beyond = lax.dynamic_slice(velocity[0], (shot * (lane // 2), (device ^ k ^ far) * lane), (lane // 2, lane))
        both = jnp.concatenate([near, beyond])
        tiles.append(lax.ppermute(both, "slab", partners(k)) if k else both)
    return tiles


def per_device(wavefield, frequencies, velocity, bracket):
    even = lines_call(0, wavefield)
    velocity, even, wavefield = lax.optimization_barrier((velocity, even, wavefield))
    even = exchange(even, radix)
    odd = lines_call(1, wavefield)
    speeds = speeds_near(velocity)
    beyond = jnp.stack([tile_now[lane:] for tile_now in speeds])
    phase = phase_call(frequencies)
    beyond, phase, even, odd = lax.optimization_barrier((beyond, phase, even, odd))
    odd = exchange(odd, radix)
    order = (4, 5, 6, 7, 2, 3, 1, 0)
    parts = rows_call(0, True, even, phase)
    moved = {k: lax.ppermute(parts[k], "slab", partners(k)) if k else parts[0] for k in order}
    evens = [moved[k] for k in range(half_radix)]
    odd = rows_call(1, False, odd, phase)
    beyond, _ = lax.optimization_barrier((beyond, odd))
    beyond = lax.ppermute(beyond, "slab", partners(far))
    evens, beyond, odd = lax.optimization_barrier((evens, beyond, odd))
    odd = exchange(odd, half_radix)
    swapped = lax.ppermute(beyond, "shot", [(0, 1), (1, 0)])
    blend = blend_call(frequencies, bracket, beyond, swapped, *speeds)
    started = start_call(evens, blend)
    propagated, image = finish_call(odd, started, blend)
    return propagated, image


def fits(mesh, shapes):
    wavefield, velocity = shapes
    return (
        mesh.shape["slab"] == radix
        and mesh.shape["shot"] == 2
        and wavefield == (2, 2, full, full)
        and velocity == (1, full, full)
    )


def solution(mesh):
    def program(wavefield, frequencies, velocity, bracket):
        small = fits(mesh, (wavefield.shape, velocity.shape))
        return jax.shard_map(
            per_device if small else per_device_general,
            mesh=mesh,
            in_specs=(
                P("shot", None, "slab", None),
                P("shot"),
                P(None, "slab", None),
                P(None, "slab", None),
            ),
            out_specs=(P("shot", None, "slab", None), P("shot", "slab", None)),
            check_vma=False,
        )(wavefield, frequencies, velocity, bracket)

    return program
```
